128 devices in a mesh: seq: 8 (over z, core), head: 16 (over x, y).
Axes of the slice: x: 4, y: 4, z: 4, core: 2. Of those that a mesh axis runs over, the one named last changes fastest.
Arguments:
- hidden_in: float32 [2048, 1536], P('seq'), may hold values from -6 to 6
- norm_gain: float32 [2, 1536], replicated, may hold values from 0.1 to 1.9
- gate_mixer_weight: bfloat16 [2, 1536, 2, 3072], P(None, None, None, 'head'), may hold values from -0.15625 to 0.15625
- w_bc: bfloat16 [2, 1536, 256], replicated, may hold values from -0.15625 to 0.15625
- w_dt: bfloat16 [2, 1536, 48], P(None, None, 'head'), may hold values from -0.15625 to 0.15625
- conv_x: float32 [2, 5, 3072], P(None, None, 'head'), may hold values from -3 to 3
- conv_bc: float32 [2, 5, 256], replicated, may hold values from -3 to 3
- head_params: float32 [2, 3, 48], P(None, None, 'head'), as said below
- gate_gain: float32 [2, 3072], P(None, 'head'), may hold values from 0.1 to 1.9
- w_out: bfloat16 [2, 3072, 1536], P(None, 'head'), may hold values from -0.109375 to 0.109375
- out_grad: float32 [2048, 1536], P('seq'), may hold values from -6 to 6
Outputs:
- hidden_out: float32 [2048, 1536], P('seq', 'head')
- grad_in: float32 [2048, 1536], P('seq', 'head')
- grad_norm_gain: float32 [2, 1536], P(None, 'head')
- grad_w_zx: float32 [2, 1536, 2, 3072], P(None, 'seq', None, 'head')
- grad_w_bc: float32 [2, 1536, 256], P(None, 'seq')
- grad_w_dt: float32 [2, 1536, 48], P(None, 'seq', 'head')
- grad_conv_x: float32 [2, 5, 3072], P(None, None, 'head')
- grad_conv_bc: float32 [2, 5, 256], replicated
- grad_head_params: float32 [2, 3, 48], P(None, None, 'head')
- grad_gate_gain: float32 [2, 3072], P(None, 'head')
- grad_w_out: float32 [2, 3072, 1536], P(None, 'head', 'seq')
The draws below stay inside these ranges and needn't reach their ends.
Inputs may be any that keep to these rules, and one draw needn't show every extreme that they name: `head_params`: rows per layer: each head's time-step bias, log decay rate and skip weight.
All inputs are finite; a program needn't handle non-finite values.
Results may differ from the reference program's by a relative error of at most 0.017.
Values may be sent and summed in bfloat16 or wider, within the bound.
A program may use at most 128 MiB of HBM per device.

```python
import math
import jax
import jax.numpy as jnp
from jax import lax

D = 1536
HEADS = 48
HEAD_DIM = 64
STATE = 128
CONV = 4
LAYERS = 2
INNER = 3072
TOKENS = 2048


def draw_head_params(key, part):
    key = jax.random.fold_in(key, 7)
    subkeys = jax.random.split(key, 5)
    row_shape = (LAYERS, 1, HEADS)
    bias_row = jax.random.uniform(subkeys[0], row_shape, jnp.float32, -6.0, -4.0)
    slow_rate = jnp.log(jax.random.uniform(subkeys[1], row_shape, jnp.float32, 0.1, 1.0) / (0.01 * TOKENS))
    fast_rate = jnp.log(jax.random.uniform(subkeys[2], row_shape, jnp.float32, 2.0, 4.0))
    chosen = jax.random.bernoulli(subkeys[3], 0.5, row_shape)
    skip_row = jax.random.uniform(subkeys[4], row_shape, jnp.float32, 0.5, 1.5)
    return jnp.concatenate([bias_row, jnp.where(chosen, slow_rate, fast_rate), skip_row], axis=1)


def shard_levels(rng, dims, shards, least, largest):
    gain, own = 1.0, jax.random.fold_in(rng, 6)
    for position, shards_of in shards:
        heights = jnp.exp(jax.random.uniform(jax.random.fold_in(own, position), (shards_of,), jnp.float32, least / len(shards), largest / len(shards)))
        gain = gain * jnp.repeat(heights, dims[position] // shards_of).reshape([-1 if axis == position else 1 for axis in range(len(dims))])
    return gain


def normal_values(own_key, dims, spread, most, shards=(), kind=jnp.bfloat16):
    drawn = spread * jax.random.normal(own_key, dims, jnp.float32)
    if shards:
        drawn = drawn * shard_levels(own_key, dims, shards, -0.22, 0.18)
    return jnp.clip(drawn, -most, most).astype(kind)


def setup_inputs(seed: int = 0) -> dict:
    key_of = jax.random.split(jax.random.key(seed), 12)
    return {
        "hidden_in": normal_values(key_of[0], (TOKENS, D), 1.0, 6.0, ((0, 8),), jnp.float32),
        "norm_gain": jnp.clip(1.0 + 0.18 * jax.random.normal(key_of[1], (LAYERS, D), jnp.float32), 0.1, 1.9),
        "gate_mixer_weight": normal_values(key_of[2], (LAYERS, D, 2, INNER), D ** -0.5, 0.15625, ((3, 16),)),
        "w_bc": normal_values(key_of[3], (LAYERS, D, 2 * STATE), D ** -0.5, 0.15625),
        "w_dt": normal_values(key_of[4], (LAYERS, D, HEADS), D ** -0.5, 0.15625, ((2, 16),)),
        "conv_x": normal_values(key_of[5], (LAYERS, CONV + 1, INNER), 0.5, 3.0, ((2, 16),), jnp.float32),
        "conv_bc": normal_values(key_of[6], (LAYERS, CONV + 1, 2 * STATE), 0.5, 3.0, (), jnp.float32),
        "head_params": draw_head_params(jax.random.fold_in(key_of[11], 71), 0),
        "gate_gain": jnp.clip(1.0 + 0.18 * jax.random.normal(key_of[8], (LAYERS, INNER), jnp.float32), 0.1, 1.9),
        "w_out": normal_values(key_of[9], (LAYERS, INNER, D), INNER ** -0.5, 0.109375, ((1, 16),)),
        "out_grad": normal_values(key_of[10], (TOKENS, D), 1.0, 6.0, ((0, 8),), jnp.float32),
    }


EPSILON = 1e-05
TOP_PRECISION = lax.Precision.HIGHEST

@jax.custom_vjp
def low(v):
    return lax.optimization_barrier(v.astype(jnp.bfloat16)).astype(jnp.float32)

@jax.custom_vjp
def lower_backward(v):
    return v

def low_keep(v):
    return (low(v), None)

def low_pass(kept, grad):
    return (grad,)

def back_keep(v):
    return (v, None)

def back_low(kept, grad):
    return (low(grad),)
low.defvjp(low_keep, low_pass)
lower_backward.defvjp(back_keep, back_low)

def rms_rows(values, gain_row):
    return values * lax.rsqrt(lax.optimization_barrier(jnp.mean(values * values, axis=-1, keepdims=True)) + EPSILON) * gain_row

def block_scan(carry_state, pieces):
    inputs, time_step, decay_log, b_matrix, c_matrix = pieces
    block_size = decay_log.shape[0]
    cumulative = jnp.cumsum(decay_log, axis=0)
    causal = (lax.broadcasted_iota(jnp.int32, (block_size, block_size), 0) >= lax.broadcasted_iota(jnp.int32, (block_size, block_size), 1))[:, :, None]
    segment = jnp.where(causal, jnp.exp(jnp.where(causal, cumulative[:, None, :] - cumulative[None, :, :], 0.0)), 0.0)
    scores = jnp.einsum('tn,sn->ts', lower_backward(c_matrix), lower_backward(b_matrix), precision=TOP_PRECISION)
    weights = scores[:, :, None] * segment * time_step[None, :, :]
    output = jnp.einsum('tsh,shp->thp', weights, inputs, precision=TOP_PRECISION) + jnp.exp(cumulative)[:, :, None] * jnp.einsum('tn,hpn->thp', c_matrix, carry_state, precision=TOP_PRECISION)
    tail_weight = jnp.exp(cumulative[-1][None, :] - cumulative) * time_step
    next_state = jnp.exp(cumulative[-1])[:, None, None] * carry_state + jnp.einsum('sh,shp,sn->hpn', tail_weight, inputs, b_matrix, precision=TOP_PRECISION)
    return (next_state, output)

def mamba_layer(residual, gain_norm, gate_input_weight, bc_weight, dt_weight, conv_xw, conv_bcw, head_rows, gain_gate, out_weight):
    length = residual.shape[0]
    normalized_rows = low(rms_rows(residual, gain_norm))
    projection_output = lower_backward(jnp.einsum('np,pwg->nwg', normalized_rows, gate_input_weight, precision=TOP_PRECISION))
    bc_raw = lower_backward(jnp.dot(normalized_rows, bc_weight, precision=TOP_PRECISION))
    step_raw = lower_backward(jnp.dot(normalized_rows, dt_weight, precision=TOP_PRECISION))
    joined = jnp.concatenate([projection_output[:, 1], bc_raw], axis=1)
    conv_weight = jnp.concatenate([conv_xw, conv_bcw], axis=1)
    padded = jnp.concatenate([jnp.zeros((CONV - 1, joined.shape[1]), jnp.float32), joined], axis=0)
    preact = conv_weight[CONV]
    for index_tap in range(CONV):
        preact = preact + conv_weight[index_tap] * padded[index_tap:index_tap + length]
    activated = jax.nn.silu(preact)
    inputs = activated[:, :INNER].reshape(length, HEADS, HEAD_DIM)
    b_matrix = low(activated[:, INNER:INNER + STATE])
    c_matrix = low(activated[:, INNER + STATE:])
    time_step = jax.nn.softplus(step_raw + head_rows[0])
    decay_log = -time_step * jnp.exp(head_rows[1])
    block_size = math.gcd(length, 256)
    block_count = length // block_size
    pieces = (inputs.reshape(block_count, block_size, HEADS, HEAD_DIM), time_step.reshape(block_count, block_size, HEADS), decay_log.reshape(block_count, block_size, HEADS), b_matrix.reshape(block_count, block_size, STATE), c_matrix.reshape(block_count, block_size, STATE))
    begin_state = jnp.zeros((HEADS, HEAD_DIM, STATE), jnp.float32)
    final_state, outputs = lax.scan(jax.checkpoint(block_scan), begin_state, pieces)
    y_full = outputs.reshape(length, HEADS, HEAD_DIM) + head_rows[2][None, :, None] * inputs
    gated_rows = y_full.reshape(length, INNER) * jax.nn.silu(projection_output[:, 0])
    gate_normed = low(gated_rows * lax.rsqrt(lax.optimization_barrier(jnp.mean(gated_rows * gated_rows, axis=1, keepdims=True)) + EPSILON) * gain_gate)
    return residual + lower_backward(jnp.dot(gate_normed, out_weight, precision=TOP_PRECISION))

def forward(residual, norm_gain, gate_mixer_weight, w_bc, w_dt, conv_x, conv_bc, head_params, gate_gain, w_out):
    for index_of_layer in range(LAYERS):
        residual = mamba_layer(residual, norm_gain[index_of_layer], gate_mixer_weight[index_of_layer], w_bc[index_of_layer], w_dt[index_of_layer], conv_x[index_of_layer], conv_bc[index_of_layer], head_params[index_of_layer], gate_gain[index_of_layer], w_out[index_of_layer])
    return residual

def reference(hidden_in, norm_gain, gate_mixer_weight, w_bc, w_dt, conv_x, conv_bc, head_params, gate_gain, w_out, out_grad):
    result, back_fn = jax.vjp(forward, hidden_in, norm_gain, gate_mixer_weight.astype(jnp.float32), w_bc.astype(jnp.float32), w_dt.astype(jnp.float32), conv_x, conv_bc, head_params, gate_gain, w_out.astype(jnp.float32))
    grads = back_fn(out_grad)
    return (result, grads[0], grads[1], grads[2], grads[3], grads[4], grads[5], grads[6], grads[7], grads[8], grads[9])
```

```python
from types import SimpleNamespace

import jax
import jax.numpy as jnp
from jax import lax
from jax.experimental import pallas as pl
from jax.experimental.pallas import tpu as pltpu
from jax.sharding import PartitionSpec as P

EPS = 1e-05
MESH = pl.DeviceIdType.MESH
HI = lax.Precision.HIGHEST
F32 = jnp.float32
BF16 = jnp.bfloat16

T = 256
R = 16
E = T + R
D = 1536
INNER = 3072
C = 192
N = 128
NH = 16
NS = 8
X = D + 128


def dot(a, b, ca, cb, precise=False):
    return lax.dot_general(
        a,
        b,
        (((ca,), (cb,)), ((), ())),
        precision=HI if precise else None,
        preferred_element_type=F32,
    )


def halves(a):
    if a.dtype == BF16:
        return (a,)
    hi = a.astype(BF16)
    return hi, (a - hi.astype(F32)).astype(BF16)


def fine(a, b, ca, cb):
    total = None
    for i, p in enumerate(halves(a)):
        for j, q in enumerate(halves(b)):
            if i + j < 2:
                term = dot(p, q, ca, cb)
                total = term if total is None else total + term
    return total


def iota(shape, dim):
    return lax.broadcasted_iota(jnp.int32, shape, dim)


def spread(col):
    rows = col.shape[0]
    lane = iota((rows, 128), 1)
    parts = [jnp.broadcast_to(col[:, 64 + k : 65 + k], (rows, 128)) for k in range(3)]
    return jnp.concatenate(
        [jnp.where(lane < 64, parts[0], parts[1]), jnp.where(lane < 64, parts[2], 0.0)], axis=1
    )


def split2(col):
    hi = col.astype(BF16)
    return hi, (col - hi.astype(F32)).astype(BF16)


def scalar_lanes(col):
    hi, lo = split2(col)
    lane = iota((col.shape[0], 128), 1)
    return jnp.where(lane == 0, hi.astype(F32), jnp.where(lane == 1, lo.astype(F32), 0.0)).astype(
        BF16
    )


def pack3(row):
    return jnp.where(iota((R, 128), 0) == 0, row, 0.0)


def unpack3(block):
    return block[0:1, :]


def decay_rows(log_row):
    e = jnp.exp(log_row)
    return jnp.concatenate(
        [jnp.broadcast_to(e[:, 64 + k : 65 + k], (64, 128)) for k in range(3)], axis=0
    )


def vm(*shape, dtype=F32):
    return pltpu.VMEM(shape, dtype)


def half(*shape):
    return pltpu.VMEM(shape, BF16)


def sem(*shape):
    return pltpu.SemaphoreType.DMA(shape)


def chain_refs():
    return dict(
        As=vm(2, C + R, N),
        Ar=vm(2, C + R, N),
        AS=sem(2),
        AR=sem(2),
        Bs=vm(2, C + R, N),
        Br=vm(2, 4, C + R, N),
        BS=sem(2, 4),
        BR=sem(2, 4),
        Cs=vm(2, C + R, N),
        Cr=vm(2, C + R, N),
        CS=sem(2),
        CR=sem(2),
    )


def weight_refs(w):
    return dict(
        s=half(2, 2, 4, C, w),
        r=half(2, 4, C, w),
        c=half(2, 4, C, w),
        x=half(2, 4, C, w),
        S=sem(2),
        R=sem(2),
        U=sem(2, 4),
        V=sem(2, 4),
    )


def both(*shape):
    return dict(S=sem(*shape), R=sem(*shape))


SCRATCH = dict(
    hid=vm(T, D),
    halo=vm(R, D),
    og=vm(T, D),
    wc=half(2, D, 768),
    wo=half(2, 256, D),
    nx0=half(E, X),
    nx1=half(E, X),
    pj=vm(2, E, 768),
    pre=vm(2, T, 512),
    x=vm(2, T, 256),
    dtb=vm(2, T, 256),
    ecb=vm(2, T, 256),
    etb=vm(2, T, 256),
    yi=vm(2, T, 256),
    yn=vm(2, T, 256),
    v=vm(2, T, 256),
    xdt=vm(2, T, 256),
    xtail=vm(2, T, 256),
    bm=half(2, T, N),
    cm=half(2, T, N),
    seg=vm(2, 3, T, T),
    vw=vm(2, 3, T, T),
    dt=vm(2, T, 128),
    cum=vm(2, T, 128),
    hl=vm(2, 256, N),
    hin=vm(2, 256, N),
    gl=vm(2, 256, N),
    gn=vm(2, 256, N),
    acc=vm(C, N),
    fc=chain_refs(),
    bc=chain_refs(),
    op=half(2, T, X),
    opr=half(2, NH, R, X),
    opq=both(2, NH),
    urow=vm(R, D),
    agq=both(NH),
    hxS=sem(NH),
    hxR=sem(1),
    h0=both(1),
    scs=vm(2, 8, T),
    scr=vm(2, NH, 8, T),
    scq=both(2, NH),
    hos=vm(NH, R, 128),
    hoq=both(NH),
    gm=half(2, T, D),
    gmq=both(NH),
    ggn=vm(2, T, 256),
    gnb=half(2, T, 256),
    gp=vm(2, T + 2 * R, 512),
    ge=half(2, E, 768),
    gq=half(2, E, D),
    gqr=half(2, 2 * NH, R, D),
    gqq=both(2, NH),
    ghS=sem(2),
    ghR=sem(2, NH),
    grow=vm(R, D),
    ngp=vm(2, 8, D),
    fas=vm(NH, 24, 128),
    far=vm(NH, 24, 128),
    faq=both(NH),
    sm=vm(2, 8, 512),
    cbs=vm(2, 8, 256),
    cbr=vm(NH, 2, 8, 256),
    cbq=both(NH),
    smr=vm(NS, 2, 8, 512),
    smq=both(NS),
    ngs=vm(8, 128),
    ngr=vm(NS, 8, 128),
    ngq=both(NS),
    we=weight_refs(512),
    wl=weight_refs(256),
    gbt=vm(2, 256, 384),
    gbr=vm(NH, 2, R, 384),
    gbq=both(NH),
    gcs=half(NS, 2, R, 256),
    gcr=half(NS, 2, R, 256),
    gcq=both(NS),
    gds=half(2, R, 256),
    gdq=both(NH),
    loc=sem(6),
)
LEAVES, TREE = jax.tree.flatten(SCRATCH)


def kernel(hid_in, og_in, ng_ref, sp_ref, wc_in, wo_in, ho, gi, wout, bct, smo, ngo, *scratch):
    m = SimpleNamespace(
        **{
            k: SimpleNamespace(**v) if isinstance(v, dict) else v
            for k, v in jax.tree.unflatten(TREE, scratch).items()
        }
    )
    s = lax.axis_index("seq")
    h = lax.axis_index("head")
    z = s // 2
    c = s % 2
    finals = []

    def rdma(src, dst, ss, rs, dev):
        return pltpu.make_async_remote_copy(
            src_ref=src, dst_ref=dst, send_sem=ss, recv_sem=rs, device_id=dev, device_id_type=MESH
        )

    def every(lo, hi, f):
        def step(d, carry):
            f(d)
            return carry

        lax.fori_loop(lo, hi, step, 0)

    class Ring:
        def __init__(self, mk, size):
            self.mk, self.size = mk, size

        def start(self):
            every(1, self.size, lambda d: self.mk(d).start())
            finals.append(lambda: every(1, self.size, lambda d: self.mk(d).wait_send()))

        def wait(self):
            every(1, self.size, lambda d: self.mk(d).wait_recv())

    def head_ring(src, dst, q, lead=()):
        def mk(d):
            t = lax.rem(h + d, NH)
            return rdma(
                src(t), dst(h), q.S.at[(*lead, d)], q.R.at[(*lead, d)], (s, t)
            )

        return Ring(mk, NH)

    def seq_ring(src, dst, q, lead=()):
        def mk(d):
            t = lax.rem(s + d, NS)
            return rdma(
                src(t), dst(s), q.S.at[(*lead, d)], q.R.at[(*lead, d)], (t, h)
            )

        return Ring(mk, NS)

    class One:
        def __init__(self, mk, sends, receives):
            self.mk, self.sends, self.receives = mk, sends, receives

        def start(self):
            @pl.when(self.sends)
            def _():
                self.mk().start()

            def last():
                @pl.when(self.sends)
                def _():
                    self.mk().wait_send()

            finals.append(last)

        def wait(self):
            @pl.when(self.receives)
            def _():
                self.mk().wait_recv()

    def rows16(t, base=0):
        return pl.ds(pl.multiple_of(base + t * R, R), R)

    loads = [
        pltpu.make_async_copy(hid_in, m.hid, m.loc.at[0]),
        pltpu.make_async_copy(wc_in.at[0], m.wc.at[0], m.loc.at[1]),
        pltpu.make_async_copy(wo_in.at[0], m.wo.at[0, pl.ds(0, C)], m.loc.at[2]),
        pltpu.make_async_copy(wc_in.at[1], m.wc.at[1], m.loc.at[3]),
        pltpu.make_async_copy(wo_in.at[1], m.wo.at[1, pl.ds(0, C)], m.loc.at[4]),
        pltpu.make_async_copy(og_in, m.og, m.loc.at[5]),
    ]
    for cp in loads:
        cp.start()

    bar = pltpu.get_barrier_semaphore()

    def greet(dev):
        pl.semaphore_signal(bar, inc=1, device_id=dev, device_id_type=MESH)

    every(1, NH, lambda d: greet((s, lax.rem(h + d, NH))))
    every(1, NS, lambda d: greet((lax.rem(s + d, NS), h)))
    back_halo = jnp.logical_and(s > 0, h < NH - 1)
    fore_halo = jnp.logical_and(s < NS - 1, h == NH - 1)

    @pl.when(back_halo)
    def _():
        greet((s - 1, NH - 1))

    @pl.when(fore_halo)
    def _():
        every(0, NH - 1, lambda t: greet((s + 1, t)))

    peers = NH - 1 + NS - 1 + jnp.where(back_halo, 1, 0) + jnp.where(fore_halo, NH - 1, 0)
    pl.semaphore_wait(bar, peers)

    halo0 = One(
        lambda: rdma(hid_in.at[pl.ds(T - R, R)], m.halo, m.h0.S.at[0], m.h0.R.at[0], (s + 1, h)),
        s < NS - 1,
        s > 0,
    )
    halo0.start()

    for l in range(2):
        m.wo[l, C:, :] = jnp.zeros((256 - C, D), BF16)

    def norm_rows(u, l):
        q = lax.rsqrt(jnp.mean(u * u, axis=1, keepdims=True) + EPS)
        return q, (u * q * ng_ref[l : l + 1, :]).astype(BF16)

    loads[0].wait()

    def norm_step(i):
        u = m.hid[pl.ds(pl.multiple_of(i * 32, 32), 32), :]
        m.nx0[pl.ds(pl.multiple_of(R + i * 32, R), 32), 0:D] = norm_rows(u, 0)[1]

    every(0, T // 32, norm_step)
    halo0.wait()

    @pl.when(s > 0)
    def _():
        m.nx0[0:R, 0:D] = norm_rows(m.halo[...], 0)[1]

    @pl.when(s == 0)
    def _():
        m.nx0[0:R, 0:D] = jnp.zeros((R, D), BF16)
        m.nx1[0:R, :] = jnp.zeros((R, X), BF16)

    nx = (m.nx0, m.nx1)
    lane = iota((T, 128), 1)
    dt_lane = jnp.logical_and(lane >= 64, lane < 67)
    lane256 = iota((T, 256), 1)
    head_lane = [jnp.logical_and(lane256 >= 64 * k, lane256 < 64 * k + 64) for k in range(3)]
    causal = iota((T, T), 0) >= iota((T, T), 1)
    tri = jnp.where(causal, 1.0, 0.0)

    def only(k, a):
        return jnp.where(head_lane[k], a, jnp.zeros_like(a))

    def chain(l, local, out, q, near, far, step):
        ld = m.cum[l, T - 1 : T, :]
        ra, rb, rc = q.Ar, q.Br, q.Cr
        sa, sb, sc = q.As, q.Bs, q.Cs
        A = One(
            lambda: rdma(sa.at[l], ra.at[l], q.AS.at[l], q.AR.at[l], (2 * z + near, h)),
            c == far,
            c == near,
        )

        def link(d):
            zz = z + step * d
            inside = jnp.logical_and(zz >= 0, zz < 4)
            prev = z - step * d
            gets = jnp.logical_and(prev >= 0, prev < 4)
            return One(
                lambda: rdma(
                    sb.at[l], rb.at[l, z], q.BS.at[l, d], q.BR.at[l, d], (2 * zz + near, h)
                ),
                jnp.logical_and(c == near, inside),
                jnp.logical_and(c == near, gets),
            )

        B = [link(d) for d in (1, 2, 3)]
        first = z == 0 if step > 0 else z == 3
        more = jnp.logical_not(first)
        Cc = One(
            lambda: rdma(sc.at[l], rc.at[l], q.CS.at[l], q.CR.at[l], (2 * z + far, h)),
            jnp.logical_and(c == near, more),
            jnp.logical_and(c == far, more),
        )

        def begin():
            @pl.when(c == far)
            def _():
                sa[l, 0:C, :] = local[l, 0:C, :]
                sa[l, C:, :] = pack3(ld)

            A.start()

        def middle():
            A.wait()

            @pl.when(c == near)
            def _():
                other = ra[l, 0:C, :].astype(F32)
                lo = unpack3(ra[l, C:, :])
                sb[l, 0:C, :] = (decay_rows(ld) * other + local[l, 0:C, :])
                sb[l, C:, :] = pack3(lo + ld)

            for b in B:
                b.start()

        def end():
            for b in B:
                b.wait()

            @pl.when(c == near)
            def _():
                m.acc[...] = jnp.zeros((C, N), F32)
                order = (0, 1, 2) if step > 0 else (3, 2, 1)
                for zz in order:

                    @pl.when(zz < z if step > 0 else zz > z)
                    def _():
                        m.acc[...] = decay_rows(unpack3(rb[l, zz, C:, :])) * m.acc[...] + rb[
                            l, zz, 0:C, :
                        ].astype(F32)

                sc[l, 0:C, :] = m.acc[...]
                sc[l, C:, :] = jnp.zeros((R, N), F32)

            Cc.start()
            out[l, C:, :] = jnp.zeros((256 - C, N), F32)

            @pl.when(c == near)
            def _():
                lo = unpack3(ra[l, C:, :])
                out[l, 0:C, :] = decay_rows(lo) * m.acc[...] + ra[l, 0:C, :].astype(F32)

            Cc.wait()

            @pl.when(c == far)
            def _():
                @pl.when(more)
                def _():
                    out[l, 0:C, :] = rc[l, 0:C, :].astype(F32)

                @pl.when(first)
                def _():
                    out[l, 0:C, :] = jnp.zeros((C, N), F32)

        return begin, middle, end

    def forward(l):
        for j in range(3):
            m.pj[l, :, 256 * j : 256 * j + 256] = dot(
                nx[l][:, 0:D], m.wc[l, :, 256 * j : 256 * j + 256], 1, 0
            )
        for pc, kc in ((0, 0), (512, 256)):
            a = sp_ref[l, 4:5, kc : kc + 256]
            for k in range(4):
                a = a + sp_ref[l, k : k + 1, kc : kc + 256] * m.pj[l, 13 + k : 13 + k + T, pc : pc + 256]
            m.pre[l, :, kc : kc + 256] = a
        a = m.pre[l, :, 0:256]
        x = a * jax.nn.sigmoid(a)
        m.x[l] = x
        a = m.pre[l, :, 256:512]
        bc = (a * jax.nn.sigmoid(a)).astype(BF16)
        m.bm[l] = bc[:, 0:N]
        m.cm[l] = bc[:, N:]
        a = m.pj[l, R:, 128:256] + sp_ref[l, 6:7, 0:128]
        dt = jnp.where(dt_lane, jax.nn.softplus(a), 0.0)
        la = -dt * jnp.exp(sp_ref[l, 7:8, 0:128])
        cum = dot(tri, la, 1, 0, True)
        m.dt[l] = dt
        m.cum[l] = cum
        dtb = spread(dt)
        etb = spread(jnp.exp(cum[T - 1 : T, :] - cum))
        m.dtb[l] = dtb
        m.etb[l] = etb
        m.ecb[l] = spread(jnp.exp(cum))
        m.xdt[l] = dtb * x
        m.xtail[l] = dtb * etb * x
        m.hl[l] = fine(m.xtail[l], m.bm[l], 0, 0)
        begin, middle, end = chain(l, m.hl, m.hin, m.fc, 1, 0, 1)
        begin()
        cumt = jnp.transpose(cum)
        scores = dot(m.cm[l], m.bm[l], 1, 1)
        for k in range(3):
            seg = jnp.where(
                causal, jnp.exp(cum[:, 64 + k : 65 + k] - cumt[64 + k : 65 + k, :]), 0.0
            )
            m.seg[l, k] = seg
            m.vw[l, k] = scores * seg
        middle()
        yi = jnp.zeros((T, 256), F32)
        for k in range(3):
            yi = yi + fine(m.vw[l, k], only(k, m.xdt[l]), 1, 0)
        m.yi[l] = yi
        end()
        yn = m.yi[l] + m.ecb[l] * fine(m.cm[l], m.hin[l], 1, 1)
        m.yn[l] = yn
        zz = m.pj[l, R:, 256:512]
        v = (yn + spread(sp_ref[l, 8:9, 0:128]) * m.x[l]) * (zz * jax.nn.sigmoid(zz))
        m.v[l] = v

    def mix_out(l):
        gain = sp_ref[l, 5:6, 0:256]
        v = m.v[l]
        vg = (v * gain).astype(BF16)
        for j in range(3):
            m.op[l, :, 512 * j : 512 * j + 512] = dot(
                vg, m.wo[l, :, 512 * j : 512 * j + 512], 1, 0
            ).astype(BF16)
        m.op[l, :, D:] = scalar_lanes(jnp.sum(v * v, axis=1, keepdims=True))
        ring = head_ring(
            lambda t: m.op.at[l, rows16(t)], lambda me: m.opr.at[l, me], m.opq, (l,)
        )
        ring.start()
        m.opr[l, h] = m.op[l, rows16(h), :]
        return ring

    def mix_sum(l, ring):
        ring.wait()
        total = m.opr[l, 0].astype(F32)
        for t in range(1, NH):
            total = total + m.opr[l, t].astype(F32)
        r = lax.rsqrt((total[:, D : D + 1] + total[:, D + 1 : D + 2]) / INNER + EPS)
        return r, total[:, 0:D]

    def scalars(l):
        v = m.v[l]
        ones = jnp.full((8, 256), 1.0, F32)
        first = dot(ones, v * v, 1, 1, True)
        second = dot(ones, m.ggn[l] * (sp_ref[l, 5:6, 0:256] * v), 1, 1, True)
        m.scs[l] = jnp.where(iota((8, T), 0) == 0, first, second)
        ring = head_ring(lambda t: m.scs.at[l], lambda me: m.scr.at[l, me], m.scq, (l,))
        ring.start()
        m.scr[l, h] = m.scs[l]
        ring.wait()
        total = m.scr[l, 0]
        for t in range(1, NH):
            total = total + m.scr[l, t]
        return jnp.transpose(jnp.concatenate([total, jnp.zeros((120, T), F32)], axis=0))

    def g_gate(l):
        return dot(m.gm[l], m.wo[l], 1, 1)

    def weight_parts(q, l, parts):
        w = q.r.shape[-1]
        for k in range(4):
            at = 0
            for left, right in parts:
                piece = dot(left(k), right, 0, 0)
                wide = piece.shape[1]
                q.s[l, 0, k, :, at : at + wide] = piece[0:C].astype(BF16)
                q.s[l, 1, k, :, at : at + wide] = piece[C:].astype(BF16)
                at += wide
        yes = jnp.bool_(True)
        pair = One(
            lambda: rdma(
                q.s.at[l, 1 - c],
                q.r.at[l],
                q.S.at[l],
                q.R.at[l],
                (2 * z + 1 - c, h),
            ),
            yes,
            yes,
        )
        pair.start()

        def mk(d):
            t = lax.rem(z + d, 4)
            return rdma(
                q.c.at[l, t],
                q.x.at[l, z],
                q.U.at[l, d],
                q.V.at[l, d],
                (2 * t + c, h),
            )

        ring = Ring(mk, 4)

        def middle():
            pair.wait()
            for k in range(4):
                q.c[l, k] = (
                    q.s[l, c, k].astype(F32) + q.r[l, k].astype(F32)
                ).astype(BF16)
            ring.start()
            q.x[l, z] = q.c[l, z]

        def end(col):
            ring.wait()
            wout[l, :, col : col + w] = (
                q.x[l, 0].astype(F32)
                + q.x[l, 1].astype(F32)
                + q.x[l, 2].astype(F32)
                + q.x[l, 3].astype(F32)
            )

        return middle, end

    def backward(l, r, s2, between):
        gain = sp_ref[l, 5:6, 0:256]
        skip = spread(sp_ref[l, 8:9, 0:128])
        v = m.v[l]
        ggn = m.ggn[l]
        rv = r * v
        m.sm[l, 5:6, 0:256] = jnp.sum(ggn * rv, axis=0, keepdims=True)
        m.gnb[l] = (rv * gain).astype(BF16)
        gv = r * (gain * ggn) - v * (r * r * r * s2 / INNER)
        zz = m.pj[l, R:, 256:512]
        sz = jax.nn.sigmoid(zz)
        x = m.x[l]
        y = m.yn[l] + skip * x
        m.ge[l, 0:R, 256:512] = jnp.zeros((R, 256), BF16)
        m.ge[l, R:, 256:512] = (gv * y * (sz * (1.0 + zz * (1.0 - sz)))).astype(BF16)
        gy = gv * (zz * sz)
        ecb = m.ecb[l]
        gyc = ecb * gy
        m.gl[l] = fine(gyc, m.cm[l], 0, 0)
        begin, middle, end = chain(l, m.gl, m.gn, m.bc, 0, 1, -1)
        begin()
        gxd = jnp.zeros((T, 256), F32)
        ds = jnp.zeros((T, T), F32)
        xdt = m.xdt[l]
        for k in range(3):
            g_k = only(k, gy)
            gxd = gxd + fine(m.vw[l, k], g_k, 0, 0)
            ds = ds + fine(g_k, xdt, 1, 1) * m.seg[l, k]
        middle()
        hin = m.hin[l]
        bm, cm = m.bm[l], m.cm[l]
        db = fine(ds, cm, 0, 0)
        dc = fine(ds, bm, 1, 0) + fine(gyc, hin, 1, 0)
        ecol = iota((256, 128), 0) // 64 + 64 == iota((256, 128), 1)
        ecol = jnp.where(jnp.logical_and(ecol, iota((256, 128), 0) < C), 1.0, 0.0)
        dcum = dot(gy * m.yn[l], ecol, 1, 0, True)
        col_in = dot(xdt * gxd, ecol, 1, 0, True)
        gskip = jnp.sum(dot(gy * x, ecol, 1, 0, True), axis=0, keepdims=True)
        between()
        end()
        gnx = m.gn[l]
        db = db + fine(m.xtail[l], gnx, 1, 0)
        rt = m.etb[l] * fine(bm, gnx, 1, 1)
        gxs = gxd + rt
        dtb = m.dtb[l]
        gx = dtb * gxs + skip * gy
        dt = m.dt[l]
        tail = dot(x * rt, ecol, 1, 0, True)
        gdt = dot(x * gxs, ecol, 1, 0, True)
        tail = dt * tail
        cum = m.cum[l]
        both = jnp.sum(gnx * m.hin[l], axis=1, keepdims=True)
        both = jnp.sum(both * ecol, axis=0, keepdims=True)
        last = jnp.sum(tail, axis=0, keepdims=True) + jnp.exp(cum[T - 1 : T, :]) * both
        dcum = dcum - col_in - tail + jnp.where(iota((T, 128), 0) == T - 1, last, 0.0)
        gla = dot(tri, dcum, 0, 0, True)
        rate = jnp.exp(sp_ref[l, 7:8, 0:128])
        gd = gdt - gla * rate
        a = m.pj[l, R:, 128:256] + sp_ref[l, 6:7, 0:128]
        gdtr = jnp.where(dt_lane, gd * jax.nn.sigmoid(a), 0.0)
        m.sm[l, 6:7, 0:128] = jnp.sum(gdtr, axis=0, keepdims=True)
        m.sm[l, 6:7, 128:256] = jnp.sum(-gla * dt * rate, axis=0, keepdims=True)
        m.sm[l, 6:7, 256:384] = gskip
        m.sm[l, 6:7, 384:512] = jnp.zeros((1, 128), F32)
        m.sm[l, 5:6, 256:512] = jnp.zeros((1, 256), F32)
        m.sm[l, 7:8, :] = jnp.zeros((1, 512), F32)
        for kc, gpost in ((0, gx), (256, jnp.concatenate([db, dc], axis=1))):
            a = m.pre[l, :, kc : kc + 256]
            sa = jax.nn.sigmoid(a)
            gpre = gpost * (sa * (1.0 + a * (1.0 - sa)))
            m.gp[l, 0:R, kc : kc + 256] = jnp.zeros((R, 256), F32)
            m.gp[l, R : R + T, kc : kc + 256] = gpre
            m.gp[l, R + T :, kc : kc + 256] = jnp.zeros((R, 256), F32)
            pc = 2 * kc
            for k in range(4):
                m.sm[l, k : k + 1, kc : kc + 256] = jnp.sum(
                    gpre * m.pj[l, 13 + k : 13 + k + T, pc : pc + 256], axis=0, keepdims=True
                )
            m.sm[l, 4:5, kc : kc + 256] = jnp.sum(gpre, axis=0, keepdims=True)
            gj = jnp.zeros((E, 256), F32)
            for k in range(4):
                gj = gj + sp_ref[l, k : k + 1, kc : kc + 256] * m.gp[l, 3 - k : 3 - k + E, kc : kc + 256]
            if kc == 0:
                more = jnp.concatenate([jnp.zeros((R, 128), F32), gdtr], axis=0)
                gj = gj + jnp.concatenate([jnp.zeros((E, 128), F32), more], axis=1)
            else:
                gt = jnp.transpose(jnp.concatenate([gj, jnp.zeros((384 - E, 256), F32)], axis=0))
                m.gbt[l] = gt
            m.ge[l, :, pc : pc + 256] = gj.astype(BF16)
        for j in range(3):
            m.gq[l, :, 512 * j : 512 * j + 512] = dot(
                m.ge[l], m.wc[l, 512 * j : 512 * j + 512, :], 1, 1
            ).astype(BF16)
        ring = head_ring(
            lambda t: m.gq.at[l, rows16(t, R)], lambda me: m.gqr.at[l, me], m.gqq, (l,)
        )
        ring.start()

        def mk(t):
            return rdma(
                m.gq.at[l, pl.ds(0, R)], m.gqr.at[l, NH + h], m.ghS.at[l], m.ghR.at[l, h], (s - 1, NH - 1)
            )

        halo = One(lambda: mk(0), s > 0, jnp.bool_(False))
        halo.start()
        m.gqr[l, h] = m.gq[l, rows16(h, R), :]

        def finish():
            ring.wait()
            total = m.gqr[l, 0].astype(F32)
            for t in range(1, NH):
                total = total + m.gqr[l, t].astype(F32)
            m.grow[...] = total

            @pl.when(fore_halo)
            def _():
                def wait_one(t):
                    rdma(
                        m.gq.at[l, pl.ds(0, R)], m.gqr.at[l, NH + t], m.ghS.at[l], m.ghR.at[l, t], (s + 1, 0)
                    ).wait_recv()

                every(0, NH, wait_one)
                more = m.gqr[l, NH].astype(F32)
                for t in range(1, NH):
                    more = more + m.gqr[l, NH + t].astype(F32)
                m.grow[...] = m.grow[...] + more

            return m.grow[...]

        return finish

    def norm_back(l, u, g, gn):
        q = lax.rsqrt(jnp.mean(u * u, axis=1, keepdims=True) + EPS)
        w = gn * ng_ref[l : l + 1, :]
        m.ngp[l, 0:1, :] = jnp.sum(gn * u * q, axis=0, keepdims=True)
        return g + q * w - u * (q * q * q * (jnp.sum(w * u, axis=1, keepdims=True) / D))

    loads[1].wait()
    forward(0)
    loads[2].wait()
    ring = mix_out(0)
    r0, o0 = mix_sum(0, ring)
    u1 = m.hid[rows16(h), :] + r0 * o0
    m.urow[...] = u1
    m.nx1[rows16(h, R), 0:D] = norm_rows(u1, 1)[1]
    m.nx1[rows16(h, R), D:] = scalar_lanes(r0)
    ag = head_ring(
        lambda t: m.nx1.at[rows16(h, R)], lambda me: m.nx1.at[rows16(me, R)], m.agq
    )
    ag.start()

    def halo1(t):
        return rdma(
            m.nx1.at[rows16(NH - 1, R)], m.nx1.at[pl.ds(0, R)], m.hxS.at[t], m.hxR.at[0], (s + 1, t)
        )

    @pl.when(fore_halo)
    def _():
        every(0, NH, lambda t: halo1(t).start())

    def halo1_sent():
        @pl.when(fore_halo)
        def _():
            every(0, NH, lambda t: halo1(t).wait_send())

    finals.append(halo1_sent)

    for cp in loads[3:]:
        cp.wait()
    m.gm[1] = m.og[...].astype(BF16)
    m.ggn[1] = g_gate(1)
    ag.wait()

    @pl.when(s > 0)
    def _():
        halo1(0).wait_recv()

    forward(1)
    cols = scalars(1)
    r1 = lax.rsqrt(cols[:, 0:1] / INNER + EPS)
    ring1 = mix_out(1)
    back1 = backward(1, r1, cols[:, 1:2], lambda: None)

    def left_n(l):
        return lambda k: nx[l][:, 384 * k : 384 * k + 384]

    def left_g(l):
        return lambda k: m.gm[l, :, 384 * k : 384 * k + 384]

    e1_mid, e1_end = weight_parts(
        m.we, 1, [(left_n(1), m.ge[1, :, 256:512]), (left_g(1), m.gnb[1])]
    )
    l1_mid, l1_end = weight_parts(m.wl, 1, [(left_n(1), m.ge[1, :, 0:256])])
    g_rows = norm_back(1, m.urow[...], m.og[rows16(h), :], back1())
    m.grow[...] = g_rows
    m.gm[0, rows16(h), :] = g_rows.astype(BF16)
    agm = head_ring(
        lambda t: m.gm.at[0, rows16(h)], lambda me: m.gm.at[0, rows16(me)], m.gmq
    )
    agm.start()

    e1_mid()
    l1_mid()
    rr, oo = mix_sum(1, ring1)
    final = m.urow[...] + rr * oo
    for t in range(NH):
        m.hos[t, :, 0:96] = final[:, 96 * t : 96 * t + 96]
        m.hos[t, :, 96:128] = jnp.zeros((R, 32), F32)
    hor = head_ring(lambda t: m.hos.at[t], lambda me: ho.at[rows16(me)], m.hoq)
    hor.start()
    ho[rows16(h), :] = m.hos[h]
    agm.wait()

    m.ggn[0] = g_gate(0)
    ex = m.nx1[R:, D:].astype(F32)
    cols = scalars(0)
    u_kept = m.grow[...]
    m.urow[...] = u_kept

    def between():
        e1_end(256)
        l1_end(0)

    back0 = backward(0, ex[:, 0:1] + ex[:, 1:2], cols[:, 1:2], between)

    gbr = head_ring(lambda t: m.gbt.at[:, rows16(t)], lambda me: m.gbr.at[me], m.gbq)
    gbr.start()
    m.gbr[h] = m.gbt[:, rows16(h), :]
    for l in range(2):
        m.cbs[l] = m.sm[l, :, 256:512]
    cbr = head_ring(lambda t: m.cbs, lambda me: m.cbr.at[me], m.cbq)
    cbr.start()
    m.cbr[h] = m.cbs[...]
    l0_mid, l0_end = weight_parts(m.wl, 0, [(left_n(0), m.ge[0, :, 0:256])])
    e0_mid, e0_end = weight_parts(
        m.we, 0, [(left_n(0), m.ge[0, :, 256:512]), (left_g(0), m.gnb[0])]
    )
    l0_mid()
    e0_mid()
    gbr.wait()
    for l in range(2):
        total = m.gbr[0, l].astype(F32)
        for t in range(1, NH):
            total = total + m.gbr[t, l].astype(F32)
        part = dot(total.astype(BF16)[:, 0:E], nx[l][:, 0:D], 1, 0).astype(BF16)
        for t in range(NS):
            m.gcs[t, l, :, 0:C] = part[:, C * t : C * t + C]
            m.gcs[t, l, :, C:] = jnp.zeros((R, 256 - C), BF16)
    gcr = seq_ring(lambda t: m.gcs.at[t], lambda me: m.gcr.at[me], m.gcq)
    gcr.start()
    m.gcr[s] = m.gcs[s]
    cbr.wait()
    total = m.cbr[0]
    for t in range(1, NH):
        total = total + m.cbr[t]
    for l in range(2):
        keep = iota((8, 256), 0) < 5
        m.sm[l, :, 256:512] = jnp.where(keep, total[l], m.sm[l, :, 256:512])
    smr = seq_ring(lambda t: m.sm, lambda me: m.smr.at[me], m.smq)
    smr.start()
    m.smr[s] = m.sm[...]
    gcr.wait()
    total = m.gcr[0].astype(F32)
    for t in range(1, NS):
        total = total + m.gcr[t].astype(F32)
    m.gds[...] = total.astype(BF16)
    gdr = head_ring(lambda t: m.gds, lambda me: bct.at[me], m.gdq)
    gdr.start()
    bct[h] = m.gds[...]
    g_rows = norm_back(0, m.hid[rows16(h), :], m.urow[...], back0())
    for t in range(NH):
        m.fas[t, 0:R, 0:96] = g_rows[:, 96 * t : 96 * t + 96]
        m.fas[t, 0:R, 96:128] = jnp.zeros((R, 32), F32)
        m.fas[t, R:, :] = jnp.zeros((8, 128), F32)
        for l in range(2):
            m.fas[t, R + l : R + l + 1, 0:96] = m.ngp[l, 0:1, 96 * t : 96 * t + 96]
    far = head_ring(lambda t: m.fas.at[t], lambda me: m.far.at[me], m.faq)
    far.start()
    m.far[h] = m.fas[h]
    l0_end(0)
    e0_end(256)
    smr.wait()
    total = m.smr[0]
    for t in range(1, NS):
        total = total + m.smr[t]
    smo[...] = total
    far.wait()
    total = m.far[0, R:, :]
    for t in range(1, NH):
        total = total + m.far[t, R:, :]
    m.ngs[...] = total
    ngr = seq_ring(lambda t: m.ngs, lambda me: m.ngr.at[me], m.ngq)
    ngr.start()
    m.ngr[s] = m.ngs[...]
    for t in range(NH):
        gi[R * t : R * t + R, :] = m.far[t, 0:R, :]
    gdr.wait()
    hor.wait()
    ngr.wait()
    total = m.ngr[0]
    for t in range(1, NS):
        total = total + m.ngr[t]
    ngo[...] = total
    for f in finals:
        f()


def on_device(
    hidden_in,
    norm_gain,
    gate_mixer_weight,
    w_bc,
    w_dt,
    conv_x,
    conv_bc,
    head_params,
    gate_gain,
    w_out,
    out_grad,
):
    def wide(a, before, total):
        pads = [(0, 0)] * (a.ndim - 1) + [(before, total - before - a.shape[-1])]
        return jnp.pad(a, pads)

    wc = jnp.concatenate(
        [
            wide(jnp.concatenate([gate_mixer_weight[:, :, 1], w_dt], axis=-1), 0, 256),
            wide(gate_mixer_weight[:, :, 0], 0, 256),
            w_bc,
        ],
        axis=-1,
    )
    sp = jnp.concatenate(
        [
            jnp.concatenate([wide(conv_x, 0, 256), conv_bc], axis=-1),
            wide(gate_gain[:, None, :], 0, 512),
            wide(head_params, 64, 512),
            jnp.zeros((2, 7, 512), F32),
        ],
        axis=1,
    )
    whole = pl.BlockSpec(memory_space=pltpu.VMEM)
    there = pl.BlockSpec(memory_space=pl.ANY)
    ho, gi, w, bct, smo, ngo = pl.pallas_call(
        kernel,
        out_shape=[
            jax.ShapeDtypeStruct((T, 128), F32),
            jax.ShapeDtypeStruct((T, 128), F32),
            jax.ShapeDtypeStruct((2, C, 768), F32),
            jax.ShapeDtypeStruct((NH, 2, R, 256), BF16),
            jax.ShapeDtypeStruct((2, 8, 512), F32),
            jax.ShapeDtypeStruct((8, 128), F32),
        ],
        in_specs=[there, there, whole, whole, there, there],
        out_specs=[whole] * 6,
        scratch_shapes=LEAVES,
        compiler_params=pltpu.CompilerParams(
            collective_id=0, has_side_effects=True, vmem_limit_bytes=60 * 2**20
        ),
        name="two_layers",
    )(hidden_in, out_grad, norm_gain, sp, wc, w_out)
    w_bc_grad = jnp.transpose(bct, (1, 3, 0, 2)).reshape(2, 256, 256)[:, :C].astype(F32)
    heads = jnp.stack([smo[:, 6, 64:67], smo[:, 6, 192:195], smo[:, 6, 320:323]], axis=1)
    return (
        ho[:, :96],
        gi[:, :96],
        ngo[0:2, :96],
        jnp.stack([w[:, :, 256:448], w[:, :, 0:192]], axis=2),
        w_bc_grad,
        w[:, :, 192:195],
        smo[:, 0:5, 0:192],
        smo[:, 0:5, 256:512],
        heads,
        smo[:, 5, 0:192],
        jnp.transpose(w[:, :, 512:704], (0, 2, 1)),
    )


def solution(mesh):
    return jax.shard_map(
        on_device,
        mesh=mesh,
        in_specs=(
            P("seq", None),
            P(),
            P(None, None, None, "head"),
            P(),
            P(None, None, "head"),
            P(None, None, "head"),
            P(),
            P(None, None, "head"),
            P(None, "head"),
            P(None, "head", None),
            P("seq", None),
        ),
        out_specs=(
            P("seq", "head"),
            P("seq", "head"),
            P(None, "head"),
            P(None, "seq", None, "head"),
            P(None, "seq", None),
            P(None, "seq", "head"),
            P(None, None, "head"),
            P(),
            P(None, None, "head"),
            P(None, "head"),
            P(None, "head", "seq"),
        ),
        check_vma=False,
    )
```

```python
from types import SimpleNamespace

import jax
import jax.numpy as jnp
from jax import lax
from jax.experimental import pallas as pl
from jax.experimental.pallas import tpu as pltpu
from jax.sharding import PartitionSpec as P

EPS = 1e-05
MESH = pl.DeviceIdType.MESH
HI = lax.Precision.HIGHEST
F32 = jnp.float32
BF16 = jnp.bfloat16

T = 256
R = 16
G = 8
D = 1536
INNER = 3072
C = 192
N = 128
NH = 16
NS = 8
X = D + 128
S = D // NH


def dot(a, b, ca, cb, precise=False):
    return lax.dot_general(
        a,
        b,
        (((ca,), (cb,)), ((), ())),
        precision=HI if precise else None,
        preferred_element_type=F32,
    )


def halves(a):
    if a.dtype == BF16:
        return (a,)
    hi = a.astype(BF16)
    return hi, (a - hi.astype(F32)).astype(BF16)


def fine(a, b, ca, cb):
    total = None
    for i, p in enumerate(halves(a)):
        for j, q in enumerate(halves(b)):
            if i + j < 2:
                term = dot(p, q, ca, cb)
                total = term if total is None else total + term
    return total


def iota(shape, dim):
    return lax.broadcasted_iota(jnp.int32, shape, dim)


def padded(a, lanes=256):
    return jnp.concatenate([a, jnp.zeros((a.shape[0], lanes - a.shape[1]), a.dtype)], axis=1)


def spread(col):
    rows = col.shape[0]
    lane = iota((rows, 128), 1)
    parts = [jnp.broadcast_to(col[:, k : k + 1], (rows, 128)) for k in range(3)]
    return jnp.concatenate(
        [jnp.where(lane < 64, parts[0], parts[1]), jnp.where(lane < 64, parts[2], 0.0)], axis=1
    )


def scalar_lanes(col):
    hi = col.astype(BF16).astype(F32)
    lane = iota((col.shape[0], 128), 1)
    return jnp.where(lane == 0, hi, jnp.where(lane == 1, col - hi, 0.0)).astype(BF16)


def decay_rows(log_row):
    e = jnp.exp(log_row)
    return jnp.concatenate(
        [jnp.broadcast_to(e[:, k : k + 1], (64, 128)) for k in range(3)], axis=0
    )


def vm(*shape, dtype=F32):
    return pltpu.VMEM(shape, dtype)


def half(*shape):
    return pltpu.VMEM(shape, BF16)


def sem(*shape):
    return pltpu.SemaphoreType.DMA(shape)


def both(*shape):
    return dict(S=sem(*shape), R=sem(*shape))


def chain_refs():
    return dict(
        As=vm(2, C + G, N),
        Ar=vm(2, C + G, N),
        AS=sem(2),
        AR=sem(2),
        Bs=vm(2, C + G, N),
        Br=vm(2, 4, C + G, N),
        BS=sem(2, 4),
        BR=sem(2, 4),
        Cs=vm(2, C, N),
        Cr=vm(2, C, N),
        CS=sem(2),
        CR=sem(2),
    )


def weight_refs(w):
    return dict(
        s=half(2, 2, 4, C, w),
        r=half(2, 4, C, w),
        c=half(2, 4, C, w),
        x=half(2, 4, C, w),
        S=sem(2),
        R=sem(2),
        U=sem(2, 4),
        V=sem(2, 4),
    )


SCRATCH = dict(
    hid=vm(T, D),
    og=vm(T, D),
    wz=half(2, 2, C, D),
    wb=half(2, D, 256),
    wo=half(2, C, D),
    sp=vm(2, 16, 512),
    q0=vm(T, 128),
    nx0=half(T, D),
    nx1=half(T, X),
    pj=vm(2, G + T, 768),
    pre=vm(2, T, 512),
    pjd=vm(2, T, 128),
    jhS=sem(2),
    jhR=sem(2),
    x=vm(2, T, 256),
    dtb=vm(2, T, 256),
    ecb=vm(2, T, 256),
    etb=vm(2, T, 256),
    yn=vm(2, T, 256),
    v=vm(2, T, 256),
    xdt=vm(2, T, 256),
    xtail=vm(2, T, 256),
    bm=half(2, T, N),
    cm=half(2, T, N),
    seg=vm(2, 3, T, T),
    vw=vm(2, 3, T, T),
    dt=vm(2, T, 128),
    cum=vm(2, T, 128),
    hl=vm(2, 256, N),
    hin=vm(2, 256, N),
    gl=vm(2, 256, N),
    gn=vm(2, 256, N),
    acc=vm(C, N),
    fc=chain_refs(),
    bc=chain_refs(),
    op=half(2, T, X),
    opr=half(2, NH, R, X),
    opq=both(2, NH),
    urow=vm(R, D),
    agq=both(NH),
    scs=vm(2, 8, T),
    scr=vm(2, NH, 8, T),
    scq=both(2, NH),
    hos=vm(NH, R, 128),
    hoq=both(NH),
    gm=half(2, T, D),
    gmq=both(NH),
    ggn=vm(2, T, 256),
    gnb=half(2, T, 256),
    gp=vm(2, T + G, 512),
    ghS=sem(2),
    ghR=sem(2),
    ge=half(2, T, 768),
    gq=half(2, T, D),
    gqr=half(2, NH, R, D),
    gqq=both(2, NH),
    grow=vm(R, D),
    ngp=vm(2, 8, D),
    fas=vm(NH, R, 128),
    faq=both(NH),
    sm=vm(2, 8, 512),
    gbs=vm(2, NH, R + G, 256),
    gbr=vm(2, NH, R + G, 256),
    gbq=both(2, NH),
    smr=vm(2, NS, 8, 512),
    smq=both(2, NS),
    gcs=half(2, NS, R, 256),
    gcr=half(2, NS, R, 256),
    gcq=both(2, NS),
    gds=half(2, R, 256),
    gdq=both(2, NH),
    we=weight_refs(512),
    wl=weight_refs(256),
    loc=sem(8),
)
LEAVES, TREE = jax.tree.flatten(SCRATCH)


def kernel(
    hid_in,
    og_in,
    ng_ref,
    cx_ref,
    cb_ref,
    hp_ref,
    gg_ref,
    wd_ref,
    wz_in,
    wb_in,
    wo_in,
    ho,
    gi,
    wout,
    bct,
    smo,
    *scratch,
):
    m = SimpleNamespace(
        **{
            k: SimpleNamespace(**v) if isinstance(v, dict) else v
            for k, v in jax.tree.unflatten(TREE, scratch).items()
        }
    )
    s = lax.axis_index("seq")
    h = lax.axis_index("head")
    z = s // 2
    c = s % 2
    finals = []

    def rdma(src, dst, ss, rs, dev):
        return pltpu.make_async_remote_copy(
            src_ref=src, dst_ref=dst, send_sem=ss, recv_sem=rs, device_id=dev, device_id_type=MESH
        )

    def every(lo, hi, f):
        def step(d, carry):
            f(d)
            return carry

        lax.fori_loop(lo, hi, step, 0)

    class Ring:
        def __init__(self, mk, size):
            self.mk, self.size = mk, size

        def start(self):
            every(1, self.size, lambda d: self.mk(d).start())
            finals.append(lambda: every(1, self.size, lambda d: self.mk(d).wait_send()))

        def wait(self):
            every(1, self.size, lambda d: self.mk(d).wait_recv())

    def head_ring(src, dst, q, lead=()):
        def mk(d):
            t = lax.rem(h + d, NH)
            return rdma(src(t), dst(h), q.S.at[(*lead, d)], q.R.at[(*lead, d)], (s, t))

        return Ring(mk, NH)

    def seq_ring(src, dst, q, lead=()):
        def mk(d):
            t = lax.rem(s + d, NS)
            return rdma(src(t), dst(s), q.S.at[(*lead, d)], q.R.at[(*lead, d)], (t, h))

        return Ring(mk, NS)

    class One:
        def __init__(self, mk, sends, receives):
            self.mk, self.sends, self.receives = mk, sends, receives

        def start(self):
            @pl.when(self.sends)
            def _():
                self.mk().start()

            def last():
                @pl.when(self.sends)
                def _():
                    self.mk().wait_send()

            finals.append(last)

        def wait(self):
            @pl.when(self.receives)
            def _():
                self.mk().wait_recv()

    def rows16(t):
        return pl.ds(pl.multiple_of(t * R, R), R)

    loads = [
        pltpu.make_async_copy(hid_in, m.hid, m.loc.at[0]),
        pltpu.make_async_copy(wz_in.at[0], m.wz.at[0], m.loc.at[1]),
        pltpu.make_async_copy(wb_in.at[0], m.wb.at[0], m.loc.at[2]),
        pltpu.make_async_copy(wo_in.at[0], m.wo.at[0], m.loc.at[3]),
        pltpu.make_async_copy(wz_in.at[1], m.wz.at[1], m.loc.at[4]),
        pltpu.make_async_copy(wb_in.at[1], m.wb.at[1], m.loc.at[5]),
        pltpu.make_async_copy(wo_in.at[1], m.wo.at[1], m.loc.at[6]),
        pltpu.make_async_copy(og_in, m.og, m.loc.at[7]),
    ]
    for cp in loads:
        cp.start()

    bar = pltpu.get_barrier_semaphore()

    def greet(dev):
        pl.semaphore_signal(bar, inc=1, device_id=dev, device_id_type=MESH)

    every(1, NS, lambda d: greet((lax.rem(s + d, NS), h)))
    every(1, NH, lambda d: greet((s, lax.rem(h + d, NH))))

    m.sp[...] = jnp.zeros((2, 16, 512), F32)
    for l in range(2):
        for k in range(5):
            m.sp[l, k : k + 1, 0:C] = cx_ref[k, l : l + 1, :]
            m.sp[l, k : k + 1, 256:512] = cb_ref[k, l : l + 1, :]
        m.sp[l, 5:6, 0:C] = gg_ref[l : l + 1, :]
        for k in range(3):
            m.sp[l, 6 + k : 7 + k, 0:3] = hp_ref[k, l : l + 1, :]
    sp = m.sp

    def norm_rows(u, l):
        q = lax.rsqrt(jnp.mean(u * u, axis=1, keepdims=True) + EPS)
        return q, (u * q * ng_ref[l : l + 1, :]).astype(BF16)

    loads[0].wait()

    def norm_step(i):
        at = pl.ds(pl.multiple_of(i * 32, 32), 32)
        q, n = norm_rows(m.hid[at, :], 0)
        m.nx0[at, :] = n
        m.q0[at, :] = jnp.broadcast_to(q, (32, 128))

    every(0, T // 32, norm_step)

    nx = (m.nx0, m.nx1)
    lane = iota((T, 128), 1)
    dt_lane = lane < 3
    lane256 = iota((T, 256), 1)
    head_lane = [jnp.logical_and(lane256 >= 64 * k, lane256 < 64 * k + 64) for k in range(3)]
    causal = iota((T, T), 0) >= iota((T, T), 1)
    tri = jnp.where(causal, 1.0, 0.0)
    ecol = jnp.where(iota((256, 128), 0) // 64 == iota((256, 128), 1), 1.0, 0.0)
    ecol = jnp.where(iota((256, 128), 1) < 3, ecol, 0.0)

    def only(k, a):
        return jnp.where(head_lane[k], a, jnp.zeros_like(a))

    def silu_slope(a):
        sa = jax.nn.sigmoid(a)
        return sa * (1.0 + a * (1.0 - sa))

    def chain(l, local, out, q, near, far, step):
        ld = m.cum[l, T - 1 : T, :]
        ra, rb, rc = q.Ar, q.Br, q.Cr
        sa, sb, sc = q.As, q.Bs, q.Cs
        A = One(
            lambda: rdma(sa.at[l], ra.at[l], q.AS.at[l], q.AR.at[l], (2 * z + near, h)),
            c == far,
            c == near,
        )

        def link(d):
            zz = z + step * d
            inside = jnp.logical_and(zz >= 0, zz < 4)
            prev = z - step * d
            gets = jnp.logical_and(prev >= 0, prev < 4)
            return One(
                lambda: rdma(
                    sb.at[l], rb.at[l, z], q.BS.at[l, d], q.BR.at[l, d], (2 * zz + near, h)
                ),
                jnp.logical_and(c == near, inside),
                jnp.logical_and(c == near, gets),
            )

        B = [link(d) for d in (1, 2, 3)]
        first = z == 0 if step > 0 else z == 3
        more = jnp.logical_not(first)
        Cc = One(
            lambda: rdma(sc.at[l], rc.at[l], q.CS.at[l], q.CR.at[l], (2 * z + far, h)),
            jnp.logical_and(c == near, more),
            jnp.logical_and(c == far, more),
        )

        def begin():
            @pl.when(c == far)
            def _():
                sa[l, 0:C, :] = local[l, 0:C, :]
                sa[l, C:, :] = jnp.broadcast_to(ld, (G, N))

            A.start()

        def middle():
            A.wait()

            @pl.when(c == near)
            def _():
                other = ra[l, 0:C, :]
                lo = ra[l, C : C + 1, :]
                sb[l, 0:C, :] = decay_rows(ld) * other + local[l, 0:C, :]
                sb[l, C:, :] = jnp.broadcast_to(lo + ld, (G, N))

            for b in B:
                b.start()

        def end():
            for b in B:
                b.wait()

            @pl.when(c == near)
            def _():
                m.acc[...] = jnp.zeros((C, N), F32)
                order = (0, 1, 2) if step > 0 else (3, 2, 1)
                for zz in order:

                    @pl.when(zz < z if step > 0 else zz > z)
                    def _():
                        m.acc[...] = decay_rows(rb[l, zz, C : C + 1, :]) * m.acc[...] + rb[
                            l, zz, 0:C, :
                        ]

                sc[l] = m.acc[...]

            Cc.start()
            out[l, C:, :] = jnp.zeros((256 - C, N), F32)

            @pl.when(c == near)
            def _():
                lo = ra[l, C : C + 1, :]
                out[l, 0:C, :] = decay_rows(lo) * m.acc[...] + ra[l, 0:C, :]

            Cc.wait()

            @pl.when(c == far)
            def _():
                @pl.when(more)
                def _():
                    out[l, 0:C, :] = rc[l]

                @pl.when(first)
                def _():
                    out[l, 0:C, :] = jnp.zeros((C, N), F32)

        return begin, middle, end

    def forward(l, ready):
        n = nx[l][:, 0:D]
        m.pj[l, G:, 0:256] = padded(dot(n, m.wz[l, 1], 1, 1))
        m.pj[l, G:, 256:512] = dot(n, m.wb[l], 1, 0)
        ready()
        halo = One(
            lambda: rdma(
                m.pj.at[l, pl.ds(T, G), pl.ds(0, 512)],
                m.pj.at[l, pl.ds(0, G), pl.ds(0, 512)],
                m.jhS.at[l],
                m.jhR.at[l],
                (s + 1, h),
            ),
            s < NS - 1,
            s > 0,
        )
        halo.start()
        m.pjd[l] = padded(dot(n, wd_ref[l], 1, 1), 128)
        m.pj[l, G:, 512:768] = padded(dot(n, m.wz[l, 0], 1, 1))
        dt = jnp.where(dt_lane, jax.nn.softplus(m.pjd[l] + sp[l, 6:7, 0:128]), 0.0)
        la = -dt * jnp.exp(sp[l, 7:8, 0:128])
        cum = dot(tri, la, 1, 0, True)
        m.dt[l] = dt
        m.cum[l] = cum
        dtb = spread(dt)
        etb = spread(jnp.exp(cum[T - 1 : T, :] - cum))
        m.dtb[l] = dtb
        m.etb[l] = etb
        m.ecb[l] = spread(jnp.exp(cum))
        cumt = jnp.transpose(cum)
        for k in range(3):
            m.seg[l, k] = jnp.where(causal, jnp.exp(cum[:, k : k + 1] - cumt[k : k + 1, :]), 0.0)

        @pl.when(s == 0)
        def _():
            m.pj[l, 0:G, 0:512] = jnp.zeros((G, 512), F32)

        halo.wait()
        for kc in (256, 0):
            a = sp[l, 4:5, kc : kc + 256]
            for k in range(4):
                at = G - 3 + k
                a = a + sp[l, k : k + 1, kc : kc + 256] * m.pj[l, at : at + T, kc : kc + 256]
            m.pre[l, :, kc : kc + 256] = a
            post = a * jax.nn.sigmoid(a)
            if kc:
                m.bm[l] = post[:, 0:N].astype(BF16)
                m.cm[l] = post[:, N:].astype(BF16)
        x = post
        m.x[l] = x
        m.xdt[l] = dtb * x
        m.xtail[l] = dtb * etb * x
        m.hl[l] = fine(m.xtail[l], m.bm[l], 0, 0)
        begin, middle, end = chain(l, m.hl, m.hin, m.fc, 1, 0, 1)
        begin()
        scores = dot(m.cm[l], m.bm[l], 1, 1)
        for k in range(3):
            m.vw[l, k] = scores * m.seg[l, k]
        middle()
        yi = jnp.zeros((T, 256), F32)
        for k in range(3):
            yi = yi + fine(m.vw[l, k], only(k, m.xdt[l]), 1, 0)
        m.yn[l] = yi
        end()
        yn = m.yn[l] + m.ecb[l] * fine(m.cm[l], m.hin[l], 1, 1)
        m.yn[l] = yn
        zz = m.pj[l, G:, 512:768]
        m.v[l] = (yn + spread(sp[l, 8:9, 0:128]) * m.x[l]) * (zz * jax.nn.sigmoid(zz))

    def mix_out(l):
        v = m.v[l]
        vg = (v * sp[l, 5:6, 0:256])[:, 0:C].astype(BF16)
        for j in range(3):
            at = slice(512 * j, 512 * j + 512)
            m.op[l, :, at] = dot(vg, m.wo[l, :, at], 1, 0).astype(BF16)
        m.op[l, :, D:] = scalar_lanes(jnp.sum(v * v, axis=1, keepdims=True))
        ring = head_ring(
            lambda t: m.op.at[l, rows16(t)], lambda me: m.opr.at[l, me], m.opq, (l,)
        )
        ring.start()
        m.opr[l, h] = m.op[l, rows16(h), :]
        return ring

    def total_of(ref, count):
        total = ref[0].astype(F32)
        for t in range(1, count):
            total = total + ref[t].astype(F32)
        return total

    def mix_sum(l, ring):
        ring.wait()
        total = total_of(m.opr.at[l], NH)
        r = lax.rsqrt((total[:, D : D + 1] + total[:, D + 1 : D + 2]) / INNER + EPS)
        return r, total[:, 0:D]

    def scalars(l):
        v = m.v[l]
        ones = jnp.full((8, 256), 1.0, F32)
        first = dot(ones, v * v, 1, 1, True)
        second = dot(ones, m.ggn[l] * (sp[l, 5:6, 0:256] * v), 1, 1, True)
        m.scs[l] = jnp.where(iota((8, T), 0) == 0, first, second)
        ring = head_ring(lambda t: m.scs.at[l], lambda me: m.scr.at[l, me], m.scq, (l,))
        ring.start()
        m.scr[l, h] = m.scs[l]

        def end():
            ring.wait()
            total = total_of(m.scr.at[l], NH)
            return jnp.transpose(jnp.concatenate([total, jnp.zeros((120, T), F32)], axis=0))

        return end

    def g_gate(l):
        m.ggn[l] = padded(dot(m.gm[l], m.wo[l], 1, 1))

    def weight_parts(q, l, parts):
        w = q.r.shape[-1]
        for k in range(4):
            at = 0
            for left, right in parts:
                piece = dot(left[:, 384 * k : 384 * k + 384], right, 0, 0)
                wide = piece.shape[1]
                q.s[l, 0, k, :, at : at + wide] = piece[0:C].astype(BF16)
                q.s[l, 1, k, :, at : at + wide] = piece[C:].astype(BF16)
                at += wide
        yes = jnp.bool_(True)
        pair = One(
            lambda: rdma(
                q.s.at[l, 1 - c], q.r.at[l], q.S.at[l], q.R.at[l], (2 * z + 1 - c, h)
            ),
            yes,
            yes,
        )
        pair.start()

        def mk(d):
            t = lax.rem(z + d, 4)
            return rdma(
                q.c.at[l, t], q.x.at[l, z], q.U.at[l, d], q.V.at[l, d], (2 * t + c, h)
            )

        ring = Ring(mk, 4)

        def middle():
            pair.wait()
            for k in range(4):
                q.c[l, k] = (q.s[l, c, k].astype(F32) + q.r[l, k].astype(F32)).astype(BF16)
            ring.start()
            q.x[l, z] = q.c[l, z]

        def end(col):
            ring.wait()
            wout[l, :, col : col + w] = total_of(q.x.at[l], 4)

        return middle, end

    def backward(l, r, s2, early, late):
        gain = sp[l, 5:6, 0:256]
        skip = spread(sp[l, 8:9, 0:128])
        v = m.v[l]
        ggn = m.ggn[l]
        rv = r * v
        gv = r * (gain * ggn) - v * (r * r * r * s2 / INNER)
        zz = m.pj[l, G:, 512:768]
        sz = jax.nn.sigmoid(zz)
        x = m.x[l]
        y = m.yn[l] + skip * x
        gy = gv * (zz * sz)
        gyc = m.ecb[l] * gy
        m.gl[l] = fine(gyc, m.cm[l], 0, 0)
        begin, middle, end = chain(l, m.gl, m.gn, m.bc, 0, 1, -1)
        begin()
        m.sm[l, 5:6, 0:256] = jnp.sum(ggn * rv, axis=0, keepdims=True)
        m.gnb[l] = (rv * gain).astype(BF16)
        m.ge[l, :, 512:768] = (gv * y * (sz * (1.0 + zz * (1.0 - sz)))).astype(BF16)
        gxd = jnp.zeros((T, 256), F32)
        ds = jnp.zeros((T, T), F32)
        xdt = m.xdt[l]
        for k in range(3):
            g_k = only(k, gy)
            gxd = gxd + fine(m.vw[l, k], g_k, 0, 0)
            ds = ds + fine(g_k, xdt, 1, 1) * m.seg[l, k]
        middle()
        weight_mid, weight_end = weight_parts(
            m.we, l, [(nx[l], m.ge[l, :, 512:768]), (m.gm.at[l], m.gnb[l])]
        )
        bm, cm = m.bm[l], m.cm[l]
        db = fine(ds, cm, 0, 0)
        dc = fine(ds, bm, 1, 0) + fine(gyc, m.hin[l], 1, 0)
        dcum = dot(gy * m.yn[l], ecol, 1, 0, True)
        col_in = dot(xdt * gxd, ecol, 1, 0, True)
        gskip = jnp.sum(dot(gy * x, ecol, 1, 0, True), axis=0, keepdims=True)
        early()
        end()
        weight_mid()
        gnx = m.gn[l]
        db = db + fine(m.xtail[l], gnx, 1, 0)
        rt = m.etb[l] * fine(bm, gnx, 1, 1)
        gxs = gxd + rt
        gx = m.dtb[l] * gxs + skip * gy
        for kc, gpost in ((0, gx), (256, jnp.concatenate([db, dc], axis=1))):
            gpre = gpost * silu_slope(m.pre[l, :, kc : kc + 256])
            m.gp[l, 0:T, kc : kc + 256] = gpre
        halo = One(
            lambda: rdma(
                m.gp.at[l, pl.ds(0, G)], m.gp.at[l, pl.ds(T, G)], m.ghS.at[l], m.ghR.at[l], (s - 1, h)
            ),
            s > 0,
            s < NS - 1,
        )
        halo.start()
        dt = m.dt[l]
        tail = dot(x * rt, ecol, 1, 0, True)
        gdt = dot(x * gxs, ecol, 1, 0, True)
        tail = dt * tail
        cum = m.cum[l]
        inner = jnp.sum(gnx * m.hin[l], axis=1, keepdims=True)
        inner = jnp.sum(inner * ecol, axis=0, keepdims=True)
        last = jnp.sum(tail, axis=0, keepdims=True) + jnp.exp(cum[T - 1 : T, :]) * inner
        dcum = dcum - col_in - tail + jnp.where(iota((T, 128), 0) == T - 1, last, 0.0)
        gla = dot(tri, dcum, 0, 0, True)
        rate = jnp.exp(sp[l, 7:8, 0:128])
        gd = gdt - gla * rate
        gdtr = jnp.where(dt_lane, gd * jax.nn.sigmoid(m.pjd[l] + sp[l, 6:7, 0:128]), 0.0)
        m.sm[l, 5:6, 256:512] = jnp.zeros((1, 256), F32)
        m.sm[l, 6:7, 0:128] = jnp.sum(gdtr, axis=0, keepdims=True)
        m.sm[l, 6:7, 128:256] = jnp.sum(-gla * dt * rate, axis=0, keepdims=True)
        m.sm[l, 6:7, 256:384] = gskip
        m.sm[l, 6:7, 384:512] = jnp.zeros((1, 128), F32)
        m.sm[l, 7:8, :] = jnp.zeros((1, 512), F32)
        for kc in (0, 256):
            gpre = m.gp[l, 0:T, kc : kc + 256]
            for k in range(4):
                at = G - 3 + k
                m.sm[l, k : k + 1, kc : kc + 256] = jnp.sum(
                    gpre * m.pj[l, at : at + T, kc : kc + 256], axis=0, keepdims=True
                )
            m.sm[l, 4:5, kc : kc + 256] = jnp.sum(gpre, axis=0, keepdims=True)

        @pl.when(s == NS - 1)
        def _():
            m.gp[l, T:, :] = jnp.zeros((G, 512), F32)

        halo.wait()
        for kc in (0, 256):
            gj = jnp.zeros((T, 256), F32)
            for k in range(4):
                gj = gj + sp[l, k : k + 1, kc : kc + 256] * m.gp[l, 3 - k : 3 - k + T, kc : kc + 256]
            if kc == 0:
                gj = jnp.concatenate([gj[:, 0:C], gdtr[:, 0:64]], axis=1)
            else:
                gt = jnp.transpose(gj)
                for t in range(NH):
                    m.gbs[l, t, 0:R, :] = gt[R * t : R * t + R, :]
            m.ge[l, :, kc : kc + 256] = gj.astype(BF16)
        low = gdtr[:, 0:R].astype(BF16)
        for j in range(3):
            at = slice(512 * j, 512 * j + 512)
            part = (
                dot(m.ge[l, :, 0:C], m.wz[l, 1, :, at], 1, 0)
                + dot(m.ge[l, :, 512 : 512 + C], m.wz[l, 0, :, at], 1, 0)
                + dot(m.ge[l, :, 256:512], m.wb[l, at, :], 1, 1)
                + dot(low, wd_ref[l, :, at], 1, 0)
            )
            if l == 0:
                m.ngp[l, 0:1, at] = jnp.sum(part * (m.hid[:, at] * m.q0[:, 0:1]), axis=0, keepdims=True)
            m.gq[l, :, at] = part.astype(BF16)
        ring = head_ring(
            lambda t: m.gq.at[l, rows16(t)], lambda me: m.gqr.at[l, me], m.gqq, (l,)
        )
        ring.start()
        m.gqr[l, h] = m.gq[l, rows16(h), :]
        late()
        last_mid, last_end = weight_parts(m.wl, l, [(nx[l], m.ge[l, :, 0:256])])

        def finish():
            ring.wait()
            return total_of(m.gqr.at[l], NH)

        return finish, weight_end, last_mid, last_end

    def norm_back(l, u, g, gn):
        q = lax.rsqrt(jnp.mean(u * u, axis=1, keepdims=True) + EPS)
        w = gn * ng_ref[l : l + 1, :]
        if l:
            m.ngp[l, 0:1, :] = jnp.sum(gn * u * q, axis=0, keepdims=True)
        return g + q * w - u * (q * q * q * (jnp.sum(w * u, axis=1, keepdims=True) / D))

    class Small:
        def __init__(self, l):
            self.l = l
            self.a = head_ring(
                lambda t: m.gbs.at[l, t], lambda me: m.gbr.at[l, me], m.gbq, (l,)
            )
            self.b = seq_ring(lambda t: m.gcs.at[l, t], lambda me: m.gcr.at[l, me], m.gcq, (l,))
            self.c = seq_ring(lambda t: m.sm.at[l], lambda me: m.smr.at[l, me], m.smq, (l,))
            self.d = head_ring(lambda t: m.gds.at[l], lambda me: bct.at[l, me], m.gdq, (l,))

        def first(self):
            l = self.l
            for t in range(NH):
                m.gbs[l, t, R : R + 5, :] = m.sm[l, 0:5, 256:512]
                m.gbs[l, t, R + 5 : R + 6, 0:S] = m.ngp[l, 0:1, S * t : S * t + S]
                m.gbs[l, t, R + 5 : R + 6, S:] = jnp.zeros((1, 256 - S), F32)
                m.gbs[l, t, R + 6 :, :] = jnp.zeros((2, 256), F32)
            self.a.start()
            m.gbr[l, h] = m.gbs[l, h]

        def second(self):
            l = self.l
            self.a.wait()
            total = total_of(m.gbr.at[l], NH)
            m.sm[l, 0:5, 256:512] = total[R : R + 5]
            m.sm[l, 7:8, 0:256] = total[R + 5 : R + 6]
            part = dot(total[0:R].astype(BF16), nx[l][:, 0:D], 1, 0).astype(BF16)
            for t in range(NS):
                m.gcs[l, t] = padded(part[:, C * t : C * t + C])
            self.b.start()
            self.c.start()
            m.gcr[l, s] = m.gcs[l, s]
            m.smr[l, s] = m.sm[l]

        def third(self):
            l = self.l
            self.b.wait()
            m.gds[l] = total_of(m.gcr.at[l], NS).astype(BF16)
            self.d.start()
            bct[l, h] = m.gds[l]
            self.c.wait()
            smo[l] = total_of(m.smr.at[l], NS)

    small = [Small(0), Small(1)]

    loads[1].wait()
    loads[2].wait()
    forward(0, lambda: pl.semaphore_wait(bar, NH - 1 + NS - 1))
    loads[3].wait()
    r0, o0 = mix_sum(0, mix_out(0))
    u1 = m.hid[rows16(h), :] + r0 * o0
    m.urow[...] = u1
    m.nx1[rows16(h), 0:D] = norm_rows(u1, 1)[1]
    m.nx1[rows16(h), D:] = scalar_lanes(r0)
    ag = head_ring(lambda t: m.nx1.at[rows16(h)], lambda me: m.nx1.at[rows16(me)], m.agq)
    ag.start()

    for cp in loads[4:]:
        cp.wait()
    m.gm[1] = m.og[...].astype(BF16)
    g_gate(1)
    ag.wait()

    forward(1, lambda: None)
    cols = scalars(1)()
    r1 = lax.rsqrt(cols[:, 0:1] / INNER + EPS)
    rings = []

    def hidden_rows():
        rr, oo = mix_sum(1, rings[0])
        final = m.urow[...] + rr * oo
        for t in range(NH):
            m.hos[t] = padded(final[:, S * t : S * t + S], 128)

    back1, e1_end, l1_mid, l1_end = backward(
        1, r1, cols[:, 1:2], lambda: rings.append(mix_out(1)), lambda: None
    )
    l1_mid()
    hidden_rows()
    g_rows = norm_back(1, m.urow[...], m.og[rows16(h), :], back1())
    m.grow[...] = g_rows
    m.gm[0, rows16(h), :] = g_rows.astype(BF16)
    agm = head_ring(
        lambda t: m.gm.at[0, rows16(h)], lambda me: m.gm.at[0, rows16(me)], m.gmq
    )
    agm.start()
    ex = m.nx1[:, D:].astype(F32)
    r0 = ex[:, 0:1] + ex[:, 1:2]
    e1_end(256)
    l1_end(0)
    agm.wait()

    g_gate(0)
    cols = scalars(0)()
    hor = head_ring(lambda t: m.hos.at[t], lambda me: ho.at[rows16(me)], m.hoq)

    def early0():
        hor.start()
        ho[rows16(h), :] = m.hos[h]
        small[1].first()

    back0, e0_end, l0_mid, l0_end = backward(0, r0, cols[:, 1:2], early0, small[0].first)
    small[1].second()
    small[0].second()
    l0_mid()
    small[1].third()
    g_rows = norm_back(0, m.hid[rows16(h), :], m.grow[...], back0())
    for t in range(NH):
        m.fas[t] = padded(g_rows[:, S * t : S * t + S], 128)
    far = head_ring(lambda t: m.fas.at[t], lambda me: gi.at[rows16(me)], m.faq)
    far.start()
    gi[rows16(h), :] = m.fas[h]
    small[0].third()
    e0_end(256)
    l0_end(0)
    hor.wait()
    small[1].d.wait()
    small[0].d.wait()
    far.wait()
    for f in finals:
        f()


def arrange(ho, gi, w, bct, smo, o_ho, o_gi, o_ng, o_zx, o_bc, o_dt, o_cx, o_cb, o_hp, o_gg, o_wo):
    o_ho[...] = jnp.transpose(ho[...])[0:S, :]
    o_gi[...] = jnp.transpose(gi[...])[0:S, :]
    for l in range(2):
        o_ng[l : l + 1, :] = smo[l, 7:8, 0:S]
        o_zx[l, :, 0, :] = w[l, :, 256 : 256 + C]
        o_zx[l, :, 1, :] = w[l, :, 0:C]
        rows = jnp.concatenate([bct[l, t].astype(F32) for t in range(NH)], axis=0)
        o_bc[l] = jnp.transpose(rows)[0:C, :]
        dts = jnp.transpose(w[l, :, 128:256])
        for k in range(3):
            o_dt[k, l : l + 1, :] = dts[64 + k : 65 + k, :]
            o_hp[k, l : l + 1, :] = smo[l, 6:7, 128 * k : 128 * k + 3]
        for k in range(5):
            o_cx[k, l : l + 1, :] = smo[l, k : k + 1, 0:C]
            o_cb[k, l : l + 1, :] = smo[l, k : k + 1, 256:512]
        o_gg[l : l + 1, :] = smo[l, 5:6, 0:C]
        o_wo[l] = jnp.transpose(w[l, :, 512:768])[0:C, :]


def on_device(
    hidden_in,
    norm_gain,
    gate_mixer_weight,
    w_bc,
    w_dt,
    conv_x,
    conv_bc,
    head_params,
    gate_gain,
    w_out,
    out_grad,
):
    wd = jnp.pad(jnp.transpose(w_dt, (0, 2, 1)), ((0, 0), (0, R - 3), (0, 0)))
    whole = pl.BlockSpec(memory_space=pltpu.VMEM)
    there = pl.BlockSpec(memory_space=pl.ANY)

    def out(*shape, dtype=F32):
        return jax.ShapeDtypeStruct(shape, dtype)

    raw = pl.pallas_call(
        kernel,
        out_shape=[
            out(T, 128),
            out(T, 128),
            out(2, C, 768),
            out(2, NH, R, 256, dtype=BF16),
            out(2, 8, 512),
        ],
        in_specs=[there] * 2 + [whole] * 6 + [there] * 3,
        out_specs=[whole] * 5,
        scratch_shapes=LEAVES,
        compiler_params=pltpu.CompilerParams(
            collective_id=0, has_side_effects=True, vmem_limit_bytes=60 * 2**20
        ),
        name="two_layers",
    )(
        hidden_in,
        out_grad,
        norm_gain,
        jnp.transpose(conv_x, (1, 0, 2)),
        jnp.transpose(conv_bc, (1, 0, 2)),
        jnp.transpose(head_params, (1, 0, 2)),
        gate_gain,
        wd,
        jnp.transpose(gate_mixer_weight, (0, 2, 3, 1)),
        w_bc,
        w_out,
    )
    ho, gi, ng, zx, bc, dt, cx, cb, hp, gg, wo = pl.pallas_call(
        arrange,
        out_shape=[
            out(S, T),
            out(S, T),
            out(2, S),
            out(2, C, 2, C),
            out(2, C, 256),
            out(3, 2, C),
            out(5, 2, C),
            out(5, 2, 256),
            out(3, 2, 3),
            out(2, C),
            out(2, C, C),
        ],
        in_specs=[whole] * 5,
        out_specs=[whole] * 11,
        compiler_params=pltpu.CompilerParams(vmem_limit_bytes=40 * 2**20),
        name="arrange",
    )(*raw)
    return (
        jnp.transpose(ho),
        jnp.transpose(gi),
        ng,
        zx,
        bc,
        jnp.transpose(dt, (1, 2, 0)),
        jnp.transpose(cx, (1, 0, 2)),
        jnp.transpose(cb, (1, 0, 2)),
        jnp.transpose(hp, (1, 0, 2)),
        gg,
        wo,
    )


def solution(mesh):
    return jax.shard_map(
        on_device,
        mesh=mesh,
        in_specs=(
            P("seq", None),
            P(),
            P(None, None, None, "head"),
            P(),
            P(None, None, "head"),
            P(None, None, "head"),
            P(),
            P(None, None, "head"),
            P(None, "head"),
            P(None, "head", None),
            P("seq", None),
        ),
        out_specs=(
            P("seq", "head"),
            P("seq", "head"),
            P(None, "head"),
            P(None, "seq", None, "head"),
            P(None, "seq", None),
            P(None, "seq", "head"),
            P(None, None, "head"),
            P(),
            P(None, None, "head"),
            P(None, "head"),
            P(None, "head", "seq"),
        ),
        check_vma=False,
    )
```

```python
from types import SimpleNamespace

import jax
import jax.numpy as jnp
from jax import lax
from jax.experimental import pallas as pl
from jax.experimental.pallas import tpu as pltpu
from jax.sharding import PartitionSpec as P

EPS = 1e-05
MESH = pl.DeviceIdType.MESH
HI = lax.Precision.HIGHEST
F32 = jnp.float32
BF16 = jnp.bfloat16

T = 256
R = 16
G = 8
D = 1536
INNER = 3072
C = 192
N = 128
NH = 16
NS = 8
X = D + 128
S = D // NH


def dot(a, b, ca, cb, precise=False):
    return lax.dot_general(
        a,
        b,
        (((ca,), (cb,)), ((), ())),
        precision=HI if precise else None,
        preferred_element_type=F32,
    )


def halves(a):
    if a.dtype == BF16:
        return (a,)
    hi = a.astype(BF16)
    return hi, (a - hi.astype(F32)).astype(BF16)


def fine(a, b, ca, cb):
    total = None
    for i, p in enumerate(halves(a)):
        for j, q in enumerate(halves(b)):
            if i + j < 2:
                term = dot(p, q, ca, cb)
                total = term if total is None else total + term
    return total


def iota(shape, dim):
    return lax.broadcasted_iota(jnp.int32, shape, dim)


def padded(a, lanes=256):
    return jnp.concatenate([a, jnp.zeros((a.shape[0], lanes - a.shape[1]), a.dtype)], axis=1)


def spread(col):
    rows = col.shape[0]
    lane = iota((rows, 128), 1)
    parts = [jnp.broadcast_to(col[:, k : k + 1], (rows, 128)) for k in range(3)]
    return jnp.concatenate(
        [jnp.where(lane < 64, parts[0], parts[1]), jnp.where(lane < 64, parts[2], 0.0)], axis=1
    )


def scalar_lanes(col):
    hi = col.astype(BF16).astype(F32)
    lane = iota((col.shape[0], 128), 1)
    return jnp.where(lane == 0, hi, jnp.where(lane == 1, col - hi, 0.0)).astype(BF16)


def decay_rows(log_row):
    e = jnp.exp(log_row)
    return jnp.concatenate(
        [jnp.broadcast_to(e[:, k : k + 1], (64, 128)) for k in range(3)], axis=0
    )


def vm(*shape, dtype=F32):
    return pltpu.VMEM(shape, dtype)


def half(*shape):
    return pltpu.VMEM(shape, BF16)


def sem(*shape):
    return pltpu.SemaphoreType.DMA(shape)


def both(*shape):
    return dict(S=sem(*shape), R=sem(*shape))


def chain_refs():
    return dict(
        As=vm(2, C + G, N),
        Ar=vm(2, C + G, N),
        AS=sem(2),
        AR=sem(2),
        Bs=vm(2, C + G, N),
        Br=vm(2, 4, C + G, N),
        BS=sem(2, 4),
        BR=sem(2, 4),
        Cs=vm(2, C, N),
        Cr=vm(2, C, N),
        CS=sem(2),
        CR=sem(2),
    )


def weight_refs(w):
    return dict(
        s=half(2, 2, 4, C, w),
        r=half(2, 4, C, w),
        c=half(2, 4, C, w),
        x=half(2, 4, C, w),
        S=sem(2),
        R=sem(2),
        U=sem(2, 4),
        V=sem(2, 4),
    )


SCRATCH = dict(
    hid=vm(T, D),
    og=vm(T, D),
    wz=half(2, 2, C, D),
    wb=half(2, D, 256),
    wo=half(2, C, D),
    sp=vm(2, 16, 512),
    wd=half(2, R, D),
    q0=vm(T, 128),
    nx0=half(T, D),
    nx1=half(T, D),
    pj=vm(2, G + T, 768),
    pre=vm(2, T, 512),
    pjd=vm(2, T, 128),
    jhS=sem(2),
    jhR=sem(2),
    x=vm(2, T, 256),
    dtb=vm(2, T, 256),
    ecb=vm(2, T, 256),
    etb=vm(2, T, 256),
    yn=vm(2, T, 256),
    v=vm(2, T, 256),
    xdt=vm(2, T, 256),
    xtail=vm(2, T, 256),
    bm=half(2, T, N),
    cm=half(2, T, N),
    seg=vm(2, 3, T, T),
    vw=vm(2, 3, T, T),
    dt=vm(2, T, 128),
    cum=vm(2, T, 128),
    hl=vm(2, 256, N),
    hin=vm(2, 256, N),
    gl=vm(2, 256, N),
    gn=vm(2, 256, N),
    acc=vm(C, N),
    fc=chain_refs(),
    bc=chain_refs(),
    op0=vm(T, D),
    opr0=vm(NH, R, D),
    op1=half(T, D),
    opr1=half(NH, R, D),
    opq=both(2, NH),
    lo=half(T, D),
    lor=half(NH, R, D),
    loq=both(NH),
    r0=vm(T, 128),
    urow=vm(R, D),
    orow=vm(R, D),
    agq=both(NH),
    scs=vm(2, 8, 128),
    scr=vm(2, NH, 8, 128),
    scq=both(2, NH),
    hos=vm(NH, R, 128),
    hoq=both(NH),
    gm0=half(T, X),
    gm1=half(T, D),
    gmq=both(NH),
    ggn=vm(2, T, 256),
    gnb=half(2, T, 256),
    gp=vm(2, T + G, 512),
    ghS=sem(2),
    ghR=sem(2),
    ge=half(2, T, 768),
    gq=half(2, T, D),
    gqr=half(2, NH, R, D),
    gqq=both(2, NH),
    grow=vm(R, D),
    ngp=vm(2, 8, D),
    fas=vm(NH, R, 128),
    faq=both(NH),
    sm=vm(2, 8, 512),
    gbs=vm(2, NH, R + G, 256),
    gbr=vm(2, NH, R + G, 256),
    gbq=both(2, NH),
    smr=vm(2, NS, 8, 512),
    smq=both(2, NS),
    gcs=half(2, NS, R, 256),
    gcr=half(2, NS, R, 256),
    gcq=both(2, NS),
    gds=half(2, R, 256),
    gdq=both(2, NH),
    we=weight_refs(512),
    wl=weight_refs(256),
    loc=sem(8),
)
LEAVES, TREE = jax.tree.flatten(SCRATCH)


def kernel(
    hid_in,
    og_in,
    ng_ref,
    cx_ref,
    cb_ref,
    hp_ref,
    gg_ref,
    wd_ref,
    wz_in,
    wb_in,
    wo_in,
    ho,
    gi,
    wout,
    bct,
    smo,
    *scratch,
):
    m = SimpleNamespace(
        **{
            k: SimpleNamespace(**v) if isinstance(v, dict) else v
            for k, v in jax.tree.unflatten(TREE, scratch).items()
        }
    )
    s = lax.axis_index("seq")
    h = lax.axis_index("head")
    z = s // 2
    c = s % 2
    hx = h // 4
    hy = h % 4
    finals = []

    def rdma(src, dst, ss, rs, dev):
        return pltpu.make_async_remote_copy(
            src_ref=src, dst_ref=dst, send_sem=ss, recv_sem=rs, device_id=dev, device_id_type=MESH
        )

    def every(lo, hi, f):
        def step(d, carry):
            f(d)
            return carry

        lax.fori_loop(lo, hi, step, 0)

    class Ring:
        def __init__(self, mk, size, send):
            self.mk, self.size, self.send = mk, size, send

        def start(self):
            self.send(lambda d: self.mk(d).start())
            finals.append(lambda: every(1, self.size, lambda d: self.mk(d).wait_send()))

        def wait(self):
            every(1, self.size, lambda d: self.mk(d).wait_recv())

    def far_first(f):
        def step(i):
            d = (6 - i // 4) % 4 * 4 + (6 - i % 4) % 4

            @pl.when(d > 0)
            def _():
                f(d)

        every(0, NH, step)

    def head_ring(src, dst, q, lead=()):
        def mk(d):
            t = (hx + d // 4) % 4 * 4 + (hy + d % 4) % 4
            return rdma(src(t), dst(h), q.S.at[(*lead, d)], q.R.at[(*lead, d)], (s, t))

        return Ring(mk, NH, far_first)

    def seq_ring(src, dst, q, lead=()):
        def mk(d):
            t = lax.rem(s + d, NS)
            return rdma(src(t), dst(s), q.S.at[(*lead, d)], q.R.at[(*lead, d)], (t, h))

        return Ring(mk, NS, lambda f: every(1, NS, f))

    class One:
        def __init__(self, mk, sends, receives):
            self.mk, self.sends, self.receives = mk, sends, receives

        def start(self):
            @pl.when(self.sends)
            def _():
                self.mk().start()

            def last():
                @pl.when(self.sends)
                def _():
                    self.mk().wait_send()

            finals.append(last)

        def wait(self):
            @pl.when(self.receives)
            def _():
                self.mk().wait_recv()

    def rows16(t):
        return pl.ds(pl.multiple_of(t * R, R), R)

    loads = [
        pltpu.make_async_copy(hid_in, m.hid, m.loc.at[0]),
        pltpu.make_async_copy(wz_in.at[0], m.wz.at[0], m.loc.at[1]),
        pltpu.make_async_copy(wb_in.at[0], m.wb.at[0], m.loc.at[2]),
        pltpu.make_async_copy(wo_in.at[0], m.wo.at[0], m.loc.at[3]),
        pltpu.make_async_copy(wz_in.at[1], m.wz.at[1], m.loc.at[4]),
        pltpu.make_async_copy(wb_in.at[1], m.wb.at[1], m.loc.at[5]),
        pltpu.make_async_copy(wo_in.at[1], m.wo.at[1], m.loc.at[6]),
        pltpu.make_async_copy(og_in, m.og, m.loc.at[7]),
    ]
    for cp in loads[:4]:
        cp.start()

    bar = pltpu.get_barrier_semaphore()

    def greet(dev):
        pl.semaphore_signal(bar, inc=1, device_id=dev, device_id_type=MESH)

    every(1, NS, lambda d: greet((lax.rem(s + d, NS), h)))
    every(1, NH, lambda d: greet((s, lax.rem(h + d, NH))))

    m.sp[...] = jnp.zeros((2, 16, 512), F32)
    for l in range(2):
        for k in range(5):
            m.sp[l, k : k + 1, 0:C] = cx_ref[k, l : l + 1, :]
            m.sp[l, k : k + 1, 256:512] = cb_ref[k, l : l + 1, :]
        m.sp[l, 5:6, 0:C] = gg_ref[l : l + 1, :]
        for k in range(3):
            m.sp[l, 6 + k : 7 + k, 0:3] = hp_ref[k, l : l + 1, :]
        rows = [wd_ref[k, l : l + 1, :].astype(F32) for k in range(3)]
        m.wd[l] = jnp.concatenate(rows + [jnp.zeros((R - 3, D), F32)], axis=0).astype(BF16)
    sp = m.sp

    def norm_rows(u, l):
        q = lax.rsqrt(jnp.mean(u * u, axis=1, keepdims=True) + EPS)
        return q, (u * q * ng_ref[l : l + 1, :]).astype(BF16)

    loads[0].wait()

    def norm_step(i):
        at = pl.ds(pl.multiple_of(i * 32, 32), 32)
        q, n = norm_rows(m.hid[at, :], 0)
        m.nx0[at, :] = n
        m.q0[at, :] = jnp.broadcast_to(q, (32, 128))

    every(0, T // 32, norm_step)

    nx = (m.nx0, m.nx1)
    gm = (m.gm0, m.gm1)
    lane = iota((T, 128), 1)
    dt_lane = lane < 3
    lane256 = iota((T, 256), 1)
    head_lane = [jnp.logical_and(lane256 >= 64 * k, lane256 < 64 * k + 64) for k in range(3)]
    causal = iota((T, T), 0) >= iota((T, T), 1)
    tri = jnp.where(causal, 1.0, 0.0)
    ecol = jnp.where(iota((256, 128), 0) // 64 == iota((256, 128), 1), 1.0, 0.0)
    ecol = jnp.where(iota((256, 128), 1) < 3, ecol, 0.0)

    def only(k, a):
        return jnp.where(head_lane[k], a, jnp.zeros_like(a))

    def silu_slope(a):
        sa = jax.nn.sigmoid(a)
        return sa * (1.0 + a * (1.0 - sa))

    def chain(l, local, out, q, near, far, step):
        ld = m.cum[l, T - 1 : T, :]
        ra, rb, rc = q.Ar, q.Br, q.Cr
        sa, sb, sc = q.As, q.Bs, q.Cs
        A = One(
            lambda: rdma(sa.at[l], ra.at[l], q.AS.at[l], q.AR.at[l], (2 * z + near, h)),
            c == far,
            c == near,
        )

        def link(d):
            zz = z + step * d
            inside = jnp.logical_and(zz >= 0, zz < 4)
            prev = z - step * d
            gets = jnp.logical_and(prev >= 0, prev < 4)
            return One(
                lambda: rdma(
                    sb.at[l], rb.at[l, z], q.BS.at[l, d], q.BR.at[l, d], (2 * zz + near, h)
                ),
                jnp.logical_and(c == near, inside),
                jnp.logical_and(c == near, gets),
            )

        B = [link(d) for d in (1, 2, 3)]
        first = z == 0 if step > 0 else z == 3
        more = jnp.logical_not(first)
        Cc = One(
            lambda: rdma(sc.at[l], rc.at[l], q.CS.at[l], q.CR.at[l], (2 * z + far, h)),
            jnp.logical_and(c == near, more),
            jnp.logical_and(c == far, more),
        )

        def begin():
            @pl.when(c == far)
            def _():
                sa[l, 0:C, :] = local[l, 0:C, :]
                sa[l, C:, :] = jnp.broadcast_to(ld, (G, N))

            A.start()

        def middle():
            A.wait()

            @pl.when(c == near)
            def _():
                other = ra[l, 0:C, :]
                lo = ra[l, C : C + 1, :]
                sb[l, 0:C, :] = decay_rows(ld) * other + local[l, 0:C, :]
                sb[l, C:, :] = jnp.broadcast_to(lo + ld, (G, N))

            for b in B:
                b.start()

        def end():
            for b in B:
                b.wait()

            @pl.when(c == near)
            def _():
                m.acc[...] = jnp.zeros((C, N), F32)
                order = (0, 1, 2) if step > 0 else (3, 2, 1)
                for zz in order:

                    @pl.when(zz < z if step > 0 else zz > z)
                    def _():
                        m.acc[...] = decay_rows(rb[l, zz, C : C + 1, :]) * m.acc[...] + rb[
                            l, zz, 0:C, :
                        ]

                sc[l] = m.acc[...]

            Cc.start()
            out[l, C:, :] = jnp.zeros((256 - C, N), F32)

            @pl.when(c == near)
            def _():
                lo = ra[l, C : C + 1, :]
                out[l, 0:C, :] = decay_rows(lo) * m.acc[...] + ra[l, 0:C, :]

            Cc.wait()

            @pl.when(c == far)
            def _():
                @pl.when(more)
                def _():
                    out[l, 0:C, :] = rc[l]

                @pl.when(first)
                def _():
                    out[l, 0:C, :] = jnp.zeros((C, N), F32)

        return begin, middle, end

    def forward(l, ready):
        n = nx[l][...]
        m.pj[l, G:, 0:256] = padded(dot(n, m.wz[l, 1], 1, 1))
        m.pj[l, G:, 256:512] = dot(n, m.wb[l], 1, 0)
        ready()
        halo = One(
            lambda: rdma(
                m.pj.at[l, pl.ds(T, G), pl.ds(0, 512)],
                m.pj.at[l, pl.ds(0, G), pl.ds(0, 512)],
                m.jhS.at[l],
                m.jhR.at[l],
                (s + 1, h),
            ),
            s < NS - 1,
            s > 0,
        )
        halo.start()
        if l == 0:
            for cp in loads[4:]:
                cp.start()
        m.pjd[l] = padded(dot(n, m.wd[l], 1, 1), 128)
        m.pj[l, G:, 512:768] = padded(dot(n, m.wz[l, 0], 1, 1))
        dt = jnp.where(dt_lane, jax.nn.softplus(m.pjd[l] + sp[l, 6:7, 0:128]), 0.0)
        la = -dt * jnp.exp(sp[l, 7:8, 0:128])
        cum = dot(tri, la, 1, 0, True)
        m.dt[l] = dt
        m.cum[l] = cum
        dtb = spread(dt)
        etb = spread(jnp.exp(cum[T - 1 : T, :] - cum))
        m.dtb[l] = dtb
        m.etb[l] = etb
        m.ecb[l] = spread(jnp.exp(cum))
        cumt = jnp.transpose(cum)
        for k in range(3):
            m.seg[l, k] = jnp.where(causal, jnp.exp(cum[:, k : k + 1] - cumt[k : k + 1, :]), 0.0)

        @pl.when(s == 0)
        def _():
            m.pj[l, 0:G, 0:512] = jnp.zeros((G, 512), F32)

        halo.wait()
        for kc in (256, 0):
            a = sp[l, 4:5, kc : kc + 256]
            for k in range(4):
                at = G - 3 + k
                a = a + sp[l, k : k + 1, kc : kc + 256] * m.pj[l, at : at + T, kc : kc + 256]
            m.pre[l, :, kc : kc + 256] = a
            post = a * jax.nn.sigmoid(a)
            if kc:
                m.bm[l] = post[:, 0:N].astype(BF16)
                m.cm[l] = post[:, N:].astype(BF16)
        x = post
        m.x[l] = x
        m.xdt[l] = dtb * x
        m.xtail[l] = dtb * etb * x
        m.hl[l] = fine(m.xtail[l], m.bm[l], 0, 0)
        begin, middle, end = chain(l, m.hl, m.hin, m.fc, 1, 0, 1)
        begin()
        scores = dot(m.cm[l], m.bm[l], 1, 1)
        for k in range(3):
            m.vw[l, k] = scores * m.seg[l, k]
        middle()
        yi = jnp.zeros((T, 256), F32)
        for k in range(3):
            yi = yi + fine(m.vw[l, k], only(k, m.xdt[l]), 1, 0)
        m.yn[l] = yi
        end()
        yn = m.yn[l] + m.ecb[l] * fine(m.cm[l], m.hin[l], 1, 1)
        m.yn[l] = yn
        zz = m.pj[l, G:, 512:768]
        m.v[l] = (yn + spread(sp[l, 8:9, 0:128]) * m.x[l]) * (zz * jax.nn.sigmoid(zz))

    def gate_norm(l, r):
        exact = r * m.v[l] * sp[l, 5:6, 0:256]
        m.gnb[l] = exact.astype(BF16)
        return exact - m.gnb[l].astype(F32)

    def mix_out(l):
        op, opr = ((m.op0, m.opr0), (m.op1, m.opr1))[l]
        for j in range(3):
            at = slice(512 * j, 512 * j + 512)
            op[:, at] = dot(m.gnb[l, :, 0:C], m.wo[l, :, at], 1, 0).astype(op.dtype)
        ring = head_ring(lambda t: op.at[rows16(t)], lambda me: opr.at[me], m.opq, (l,))
        ring.start()
        opr[h] = op[rows16(h), :]

        def end():
            ring.wait()
            return total_of(opr, NH)

        return end

    def total_of(ref, count):
        total = ref[0].astype(F32)
        for t in range(1, count):
            total = total + ref[t].astype(F32)
        return total

    def scalars(i, *values):
        ones = jnp.full((8, 256), 1.0, F32)
        row = iota((8, 128), 0)
        packed = jnp.zeros((8, 128), F32)
        for k, value in enumerate(values):
            sums = dot(ones, value, 1, 1, True)
            packed = jnp.where(row == 2 * k, sums[:, 0:128], packed)
            packed = jnp.where(row == 2 * k + 1, sums[:, 128:256], packed)
        m.scs[i] = packed
        ring = head_ring(lambda t: m.scs.at[i], lambda me: m.scr.at[i, me], m.scq, (i,))
        ring.start()
        m.scr[i, h] = m.scs[i]
        ring.wait()
        total = total_of(m.scr.at[i], NH)
        cols = jnp.transpose(jnp.concatenate([total, jnp.zeros((120, 128), F32)], axis=0))
        return [
            jnp.concatenate([cols[:, 2 * k : 2 * k + 1], cols[:, 2 * k + 1 : 2 * k + 2]], axis=0)
            for k in range(len(values))
        ]

    def g_gate(l):
        m.ggn[l] = padded(dot(gm[l][:, 0:D], m.wo[l], 1, 1))

    def weight_parts(q, l, parts):
        w = q.r.shape[-1]
        for k in range(4):
            at = 0
            for left, right in parts:
                piece = dot(left[:, 384 * k : 384 * k + 384], right, 0, 0)
                wide = piece.shape[1]
                q.s[l, 0, k, :, at : at + wide] = piece[0:C].astype(BF16)
                q.s[l, 1, k, :, at : at + wide] = piece[C:].astype(BF16)
                at += wide
        yes = jnp.bool_(True)
        pair = One(
            lambda: rdma(
                q.s.at[l, 1 - c], q.r.at[l], q.S.at[l], q.R.at[l], (2 * z + 1 - c, h)
            ),
            yes,
            yes,
        )
        pair.start()

        def mk(d):
            t = lax.rem(z + d, 4)
            return rdma(
                q.c.at[l, t], q.x.at[l, z], q.U.at[l, d], q.V.at[l, d], (2 * t + c, h)
            )

        ring = Ring(mk, 4, lambda f: every(1, 4, f))

        def middle():
            pair.wait()
            for k in range(4):
                q.c[l, k] = (q.s[l, c, k].astype(F32) + q.r[l, k].astype(F32)).astype(BF16)
            ring.start()
            q.x[l, z] = q.c[l, z]

        def end(col):
            ring.wait()
            wout[l, :, col : col + w] = total_of(q.x.at[l], 4)

        return middle, end

    def backward(l, r, s2, early, late):
        gain = sp[l, 5:6, 0:256]
        skip = spread(sp[l, 8:9, 0:128])
        v = m.v[l]
        ggn = m.ggn[l]
        rv = r * v
        gv = r * (gain * ggn) - v * (r * r * s2 / INNER)
        zz = m.pj[l, G:, 512:768]
        sz = jax.nn.sigmoid(zz)
        x = m.x[l]
        y = m.yn[l] + skip * x
        gy = gv * (zz * sz)
        gyc = m.ecb[l] * gy
        m.gl[l] = fine(gyc, m.cm[l], 0, 0)
        begin, middle, end = chain(l, m.gl, m.gn, m.bc, 0, 1, -1)
        begin()
        m.sm[l, 5:6, 0:256] = jnp.sum(ggn * rv, axis=0, keepdims=True)
        if l:
            gate_norm(l, r)
        m.ge[l, :, 512:768] = (gv * y * (sz * (1.0 + zz * (1.0 - sz)))).astype(BF16)
        gxd = jnp.zeros((T, 256), F32)
        ds = jnp.zeros((T, T), F32)
        xdt = m.xdt[l]
        for k in range(3):
            g_k = only(k, gy)
            gxd = gxd + fine(m.vw[l, k], g_k, 0, 0)
            ds = ds + fine(g_k, xdt, 1, 1) * m.seg[l, k]
        middle()
        weight_mid, weight_end = weight_parts(
            m.we, l, [(nx[l], m.ge[l, :, 512:768]), (gm[l], m.gnb[l])]
        )
        bm, cm = m.bm[l], m.cm[l]
        db = fine(ds, cm, 0, 0)
        dc = fine(ds, bm, 1, 0) + fine(gyc, m.hin[l], 1, 0)
        dcum = dot(gy * m.yn[l], ecol, 1, 0, True)
        col_in = dot(xdt * gxd, ecol, 1, 0, True)
        gskip = jnp.sum(dot(gy * x, ecol, 1, 0, True), axis=0, keepdims=True)
        early()
        end()
        weight_mid()
        gnx = m.gn[l]
        db = db + fine(m.xtail[l], gnx, 1, 0)
        rt = m.etb[l] * fine(bm, gnx, 1, 1)
        gxs = gxd + rt
        gx = m.dtb[l] * gxs + skip * gy
        for kc, gpost in ((0, gx), (256, jnp.concatenate([db, dc], axis=1))):
            gpre = gpost * silu_slope(m.pre[l, :, kc : kc + 256])
            m.gp[l, 0:T, kc : kc + 256] = gpre
        halo = One(
            lambda: rdma(
                m.gp.at[l, pl.ds(0, G)], m.gp.at[l, pl.ds(T, G)], m.ghS.at[l], m.ghR.at[l], (s - 1, h)
            ),
            s > 0,
            s < NS - 1,
        )
        halo.start()
        dt = m.dt[l]
        tail = dot(x * rt, ecol, 1, 0, True)
        gdt = dot(x * gxs, ecol, 1, 0, True)
        tail = dt * tail
        cum = m.cum[l]
        inner = jnp.sum(gnx * m.hin[l], axis=1, keepdims=True)
        inner = jnp.sum(inner * ecol, axis=0, keepdims=True)
        last = jnp.sum(tail, axis=0, keepdims=True) + jnp.exp(cum[T - 1 : T, :]) * inner
        dcum = dcum - col_in - tail + jnp.where(iota((T, 128), 0) == T - 1, last, 0.0)
        gla = dot(tri, dcum, 0, 0, True)
        rate = jnp.exp(sp[l, 7:8, 0:128])
        gd = gdt - gla * rate
        gdtr = jnp.where(dt_lane, gd * jax.nn.sigmoid(m.pjd[l] + sp[l, 6:7, 0:128]), 0.0)
        m.sm[l, 5:6, 256:512] = jnp.zeros((1, 256), F32)
        m.sm[l, 6:7, 0:128] = jnp.sum(gdtr, axis=0, keepdims=True)
        m.sm[l, 6:7, 128:256] = jnp.sum(-gla * dt * rate, axis=0, keepdims=True)
        m.sm[l, 6:7, 256:384] = gskip
        m.sm[l, 6:7, 384:512] = jnp.zeros((1, 128), F32)
        m.sm[l, 7:8, :] = jnp.zeros((1, 512), F32)
        @pl.when(s == NS - 1)
        def _():
            m.gp[l, T:, :] = jnp.zeros((G, 512), F32)

        halo.wait()
        for kc in (0, 256):
            gj = jnp.zeros((T, 256), F32)
            for k in range(4):
                gj = gj + sp[l, k : k + 1, kc : kc + 256] * m.gp[l, 3 - k : 3 - k + T, kc : kc + 256]
            if kc == 0:
                gj = jnp.concatenate([gj[:, 0:C], gdtr[:, 0:64]], axis=1)
            else:
                gt = jnp.transpose(gj)
                for t in range(NH):
                    m.gbs[l, t, 0:R, :] = gt[R * t : R * t + R, :]
            m.ge[l, :, kc : kc + 256] = gj.astype(BF16)
        low = gdtr[:, 0:R].astype(BF16)
        for j in range(3):
            at = slice(512 * j, 512 * j + 512)
            part = (
                dot(m.ge[l, :, 0:C], m.wz[l, 1, :, at], 1, 0)
                + dot(m.ge[l, :, 512 : 512 + C], m.wz[l, 0, :, at], 1, 0)
                + dot(m.ge[l, :, 256:512], m.wb[l, at, :], 1, 1)
                + dot(low, m.wd[l, :, at], 1, 0)
            )
            if l == 0:
                m.ngp[l, 0:1, at] = jnp.sum(part * (m.hid[:, at] * m.q0[:, 0:1]), axis=0, keepdims=True)
            m.gq[l, :, at] = part.astype(BF16)
        ring = head_ring(
            lambda t: m.gq.at[l, rows16(t)], lambda me: m.gqr.at[l, me], m.gqq, (l,)
        )
        ring.start()
        m.gqr[l, h] = m.gq[l, rows16(h), :]
        for kc in (0, 256):
            gpre = m.gp[l, 0:T, kc : kc + 256]
            for k in range(4):
                at = G - 3 + k
                m.sm[l, k : k + 1, kc : kc + 256] = jnp.sum(
                    gpre * m.pj[l, at : at + T, kc : kc + 256], axis=0, keepdims=True
                )
            m.sm[l, 4:5, kc : kc + 256] = jnp.sum(gpre, axis=0, keepdims=True)
        late()
        last_mid, last_end = weight_parts(m.wl, l, [(nx[l], m.ge[l, :, 0:256])])

        def finish():
            ring.wait()
            return total_of(m.gqr.at[l], NH)

        return finish, weight_end, last_mid, last_end

    def norm_back(l, u, g, gn):
        q = lax.rsqrt(jnp.mean(u * u, axis=1, keepdims=True) + EPS)
        w = gn * ng_ref[l : l + 1, :]
        if l:
            m.ngp[l, 0:1, :] = jnp.sum(gn * u * q, axis=0, keepdims=True)
        return g + q * w - u * (q * q * q * (jnp.sum(w * u, axis=1, keepdims=True) / D))

    class Small:
        def __init__(self, l):
            self.l = l
            self.a = head_ring(
                lambda t: m.gbs.at[l, t], lambda me: m.gbr.at[l, me], m.gbq, (l,)
            )
            self.b = seq_ring(lambda t: m.gcs.at[l, t], lambda me: m.gcr.at[l, me], m.gcq, (l,))
            self.c = seq_ring(lambda t: m.sm.at[l], lambda me: m.smr.at[l, me], m.smq, (l,))
            self.d = head_ring(lambda t: m.gds.at[l], lambda me: bct.at[l, me], m.gdq, (l,))

        def first(self):
            l = self.l
            for t in range(NH):
                m.gbs[l, t, R : R + 5, :] = m.sm[l, 0:5, 256:512]
                m.gbs[l, t, R + 5 : R + 6, 0:S] = m.ngp[l, 0:1, S * t : S * t + S]
                m.gbs[l, t, R + 5 : R + 6, S:] = jnp.zeros((1, 256 - S), F32)
                m.gbs[l, t, R + 6 :, :] = jnp.zeros((2, 256), F32)
            self.a.start()
            m.gbr[l, h] = m.gbs[l, h]

        def second(self):
            l = self.l
            self.a.wait()
            total = total_of(m.gbr.at[l], NH)
            m.sm[l, 0:5, 256:512] = total[R : R + 5]
            m.sm[l, 7:8, 0:256] = total[R + 5 : R + 6]
            part = dot(total[0:R].astype(BF16), nx[l][...], 1, 0).astype(BF16)
            for t in range(NS):
                m.gcs[l, t] = padded(part[:, C * t : C * t + C])
            self.b.start()
            self.c.start()
            m.gcr[l, s] = m.gcs[l, s]
            m.smr[l, s] = m.sm[l]

        def third(self):
            l = self.l
            self.b.wait()
            m.gds[l] = total_of(m.gcr.at[l], NS).astype(BF16)
            self.d.start()
            bct[l, h] = m.gds[l]
            self.c.wait()
            smo[l] = total_of(m.smr.at[l], NS)

    small = [Small(0), Small(1)]

    loads[1].wait()
    loads[2].wait()
    forward(0, lambda: pl.semaphore_wait(bar, NH - 1 + NS - 1))
    loads[3].wait()
    r0 = lax.rsqrt(scalars(0, m.v[0] * m.v[0])[0] / INNER + EPS)
    m.r0[...] = jnp.broadcast_to(r0, (T, 128))
    rest = gate_norm(0, r0)[:, 0:C].astype(BF16)
    end0 = mix_out(0)
    for j in range(3):
        at = slice(512 * j, 512 * j + 512)
        m.lo[:, at] = dot(rest, m.wo[0, :, at], 1, 0).astype(BF16)
    o0 = end0()
    m.orow[...] = o0
    u1 = m.hid[rows16(h), :] + o0
    m.urow[...] = u1
    m.nx1[rows16(h), :] = norm_rows(u1, 1)[1]
    ag = head_ring(lambda t: m.nx1.at[rows16(h)], lambda me: m.nx1.at[rows16(me)], m.agq)
    ag.start()

    for cp in loads[4:]:
        cp.wait()
    m.gm1[...] = m.og[...].astype(BF16)
    g_gate(1)
    ag.wait()

    low = head_ring(lambda t: m.lo.at[rows16(t)], lambda me: m.lor.at[me], m.loq)
    low.start()
    m.lor[h] = m.lo[rows16(h), :]
    forward(1, lambda: None)
    v = m.v[1]
    sq, s2 = scalars(1, v * v, m.ggn[1] * (sp[1, 5:6, 0:256] * v))
    r1 = lax.rsqrt(sq / INNER + EPS)
    rings = []

    def hidden_rows():
        final = m.urow[...] + rings[0]()
        for t in range(NH):
            m.hos[t] = padded(final[:, S * t : S * t + S], 128)

    back1, e1_end, l1_mid, l1_end = backward(
        1, r1, r1 * s2, lambda: rings.append(mix_out(1)), lambda: None
    )
    l1_mid()
    hidden_rows()
    low.wait()
    m.orow[...] = m.orow[...] + total_of(m.lor, NH)
    g_rows = norm_back(1, m.urow[...], m.og[rows16(h), :], back1())
    m.grow[...] = g_rows
    rounded = g_rows.astype(BF16)
    m.gm0[rows16(h), 0:D] = rounded
    m.gm0[rows16(h), D:] = scalar_lanes(
        jnp.sum(rounded.astype(F32) * m.orow[...], axis=1, keepdims=True)
    )
    agm = head_ring(lambda t: m.gm0.at[rows16(h)], lambda me: m.gm0.at[rows16(me)], m.gmq)
    agm.start()
    e1_end(256)
    l1_end(0)
    agm.wait()

    g_gate(0)
    s2 = m.gm0[:, D:].astype(F32)
    hor = head_ring(lambda t: m.hos.at[t], lambda me: ho.at[rows16(me)], m.hoq)

    def early0():
        hor.start()
        ho[rows16(h), :] = m.hos[h]
        small[1].first()

    back0, e0_end, l0_mid, l0_end = backward(0, m.r0[:, 0:1], s2[:, 0:1] + s2[:, 1:2], early0, small[0].first)
    small[1].second()
    small[0].second()
    l0_mid()
    small[1].third()
    g_rows = norm_back(0, m.hid[rows16(h), :], m.grow[...], back0())
    for t in range(NH):
        m.fas[t] = padded(g_rows[:, S * t : S * t + S], 128)
    far = head_ring(lambda t: m.fas.at[t], lambda me: gi.at[rows16(me)], m.faq)
    far.start()
    gi[rows16(h), :] = m.fas[h]
    small[0].third()
    e0_end(256)
    l0_end(0)
    hor.wait()
    small[1].d.wait()
    small[0].d.wait()
    far.wait()
    for f in finals:
        f()


def arrange(
    ho_in, gi_in, w_in, bct_in, smo_in, o_ho, o_gi, o_ng, o_zx, o_bc, o_dt, o_cx, o_cb, o_hp, o_gg, o_wo, ho, gi, w, bct, smo, sems
):
    pairs = ((w_in, w), (ho_in, ho), (gi_in, gi), (bct_in, bct), (smo_in, smo))
    copies = [pltpu.make_async_copy(a, b, sems.at[i]) for i, (a, b) in enumerate(pairs)]
    for cp in copies:
        cp.start()
    for cp in copies:
        cp.wait()
    o_ho[...] = jnp.transpose(ho[...])[0:S, :]
    o_gi[...] = jnp.transpose(gi[...])[0:S, :]
    for l in range(2):
        o_ng[l : l + 1, :] = smo[l, 7:8, 0:S]
        o_zx[l, :, 0, :] = w[l, :, 256 : 256 + C]
        o_zx[l, :, 1, :] = w[l, :, 0:C]
        rows = jnp.concatenate([bct[l, t].astype(F32) for t in range(NH)], axis=0)
        o_bc[l] = jnp.transpose(rows)[0:C, :]
        dts = jnp.transpose(w[l, :, 128:256])
        for k in range(3):
            o_dt[k, l : l + 1, :] = dts[64 + k : 65 + k, :]
            o_hp[k, l : l + 1, :] = smo[l, 6:7, 128 * k : 128 * k + 3]
        for k in range(5):
            o_cx[k, l : l + 1, :] = smo[l, k : k + 1, 0:C]
            o_cb[k, l : l + 1, :] = smo[l, k : k + 1, 256:512]
        o_gg[l : l + 1, :] = smo[l, 5:6, 0:C]
        o_wo[l] = jnp.transpose(w[l, :, 512:768])[0:C, :]


def on_device(
    hidden_in,
    norm_gain,
    gate_mixer_weight,
    w_bc,
    w_dt,
    conv_x,
    conv_bc,
    head_params,
    gate_gain,
    w_out,
    out_grad,
):
    whole = pl.BlockSpec(memory_space=pltpu.VMEM)
    there = pl.BlockSpec(memory_space=pl.ANY)

    def out(*shape, dtype=F32):
        return jax.ShapeDtypeStruct(shape, dtype)

    raw = pl.pallas_call(
        kernel,
        out_shape=[
            out(T, 128),
            out(T, 128),
            out(2, C, 768),
            out(2, NH, R, 256, dtype=BF16),
            out(2, 8, 512),
        ],
        in_specs=[there] * 2 + [whole] * 6 + [there] * 3,
        out_specs=[whole] * 5,
        scratch_shapes=LEAVES,
        compiler_params=pltpu.CompilerParams(
            collective_id=0, has_side_effects=True, vmem_limit_bytes=60 * 2**20
        ),
        name="two_layers",
    )(
        hidden_in,
        out_grad,
        norm_gain,
        jnp.transpose(conv_x, (1, 0, 2)),
        jnp.transpose(conv_bc, (1, 0, 2)),
        jnp.transpose(head_params, (1, 0, 2)),
        gate_gain,
        jnp.transpose(w_dt, (2, 0, 1)),
        jnp.transpose(gate_mixer_weight, (0, 2, 3, 1)),
        w_bc,
        w_out,
    )
    ho, gi, ng, zx, bc, dt, cx, cb, hp, gg, wo = pl.pallas_call(
        arrange,
        out_shape=[
            out(S, T),
            out(S, T),
            out(2, S),
            out(2, C, 2, C),
            out(2, C, 256),
            out(3, 2, C),
            out(5, 2, C),
            out(5, 2, 256),
            out(3, 2, 3),
            out(2, C),
            out(2, C, C),
        ],
        in_specs=[there] * 5,
        out_specs=[whole] * 11,
        scratch_shapes=[vm(T, 128), vm(T, 128), vm(2, C, 768), half(2, NH, R, 256), vm(2, 8, 512), sem(5)],
        compiler_params=pltpu.CompilerParams(vmem_limit_bytes=60 * 2**20),
        name="arrange",
    )(*raw)
    return (
        jnp.transpose(ho),
        jnp.transpose(gi),
        ng,
        zx,
        bc,
        jnp.transpose(dt, (1, 2, 0)),
        jnp.transpose(cx, (1, 0, 2)),
        jnp.transpose(cb, (1, 0, 2)),
        jnp.transpose(hp, (1, 0, 2)),
        gg,
        wo,
    )


def solution(mesh):
    return jax.shard_map(
        on_device,
        mesh=mesh,
        in_specs=(
            P("seq", None),
            P(),
            P(None, None, None, "head"),
            P(),
            P(None, None, "head"),
            P(None, None, "head"),
            P(),
            P(None, None, "head"),
            P(None, "head"),
            P(None, "head", None),
            P("seq", None),
        ),
        out_specs=(
            P("seq", "head"),
            P("seq", "head"),
            P(None, "head"),
            P(None, "seq", None, "head"),
            P(None, "seq", None),
            P(None, "seq", "head"),
            P(None, None, "head"),
            P(),
            P(None, None, "head"),
            P(None, "head"),
            P(None, "head", "seq"),
        ),
        check_vma=False,
    )
```

```python
from types import SimpleNamespace

import jax
import jax.numpy as jnp
from jax import lax
from jax.experimental import pallas as pl
from jax.experimental.pallas import tpu as pltpu
from jax.sharding import PartitionSpec as P

EPS = 1e-05
MESH = pl.DeviceIdType.MESH
F32 = jnp.float32
BF16 = jnp.bfloat16

T = 256
R = 16
G = 8
D = 1536
INNER = 3072
C = 192
N = 128
NH = 16
NS = 8
X = D + 128
S = D // NH


def dot(a, b, ca, cb):
    return lax.dot_general(a, b, (((ca,), (cb,)), ((), ())), preferred_element_type=F32)


def halves(a):
    if a.dtype == BF16:
        return (a,)
    hi = a.astype(BF16)
    return hi, (a - hi.astype(F32)).astype(BF16)


def fine(a, b, ca, cb):
    total = None
    for i, p in enumerate(halves(a)):
        for j, q in enumerate(halves(b)):
            if i + j < 2:
                term = dot(p, q, ca, cb)
                total = term if total is None else total + term
    return total


def sums(ones, value, ca, cb):
    hi, lo = halves(value)
    rest = (value - hi.astype(F32) - lo.astype(F32)).astype(BF16)
    return dot(ones, hi, ca, cb) + dot(ones, lo, ca, cb) + dot(ones, rest, ca, cb)


def iota(shape, dim):
    return lax.broadcasted_iota(jnp.int32, shape, dim)


def padded(a, lanes=256):
    return jnp.concatenate([a, jnp.zeros((a.shape[0], lanes - a.shape[1]), a.dtype)], axis=1)


def spread(col):
    rows = col.shape[0]
    lane = iota((rows, 128), 1)
    parts = [jnp.broadcast_to(col[:, k : k + 1], (rows, 128)) for k in range(3)]
    return jnp.concatenate(
        [jnp.where(lane < 64, parts[0], parts[1]), jnp.where(lane < 64, parts[2], 0.0)], axis=1
    )


def scalar_lanes(col):
    hi = col.astype(BF16).astype(F32)
    lane = iota((col.shape[0], 128), 1)
    return jnp.where(lane == 0, hi, jnp.where(lane == 1, col - hi, 0.0)).astype(BF16)


def decay_rows(log_row):
    e = jnp.exp(log_row)
    return jnp.concatenate(
        [jnp.broadcast_to(e[:, k : k + 1], (64, 128)) for k in range(3)], axis=0
    )


def vm(*shape, dtype=F32):
    return pltpu.VMEM(shape, dtype)


def half(*shape):
    return pltpu.VMEM(shape, BF16)


def sem(*shape):
    return pltpu.SemaphoreType.DMA(shape)


def both(*shape):
    return dict(S=sem(*shape), R=sem(*shape))


def chain_refs():
    return dict(
        As=vm(2, C + G, N),
        Ar=vm(2, C + G, N),
        AS=sem(2),
        AR=sem(2),
        Bs=vm(2, C + G, N),
        Br=vm(2, 4, C + G, N),
        BS=sem(2, 4),
        BR=sem(2, 4),
        Cs=vm(2, C, N),
        Cr=vm(2, C, N),
        CS=sem(2),
        CR=sem(2),
    )


def weight_refs(w):
    return dict(
        s=half(2, 2, 4, C, w),
        r=half(2, 4, C, w),
        c=half(2, 4, C, w),
        x=half(2, 4, C, w),
        S=sem(2),
        R=sem(2),
        U=sem(2, 4),
        V=sem(2, 4),
    )


SCRATCH = dict(
    hid=vm(T, D),
    og=vm(T, D),
    wz=half(2, 2, C, D),
    wb=half(2, D, 256),
    wo=half(2, C, D),
    sp=vm(2, 16, 512),
    wd=half(2, R, D),
    q0=vm(T, 128),
    nx0=half(T, D),
    nx1=half(T, D),
    pj=vm(2, G + T, 768),
    pre=vm(2, T, 512),
    pjd=vm(2, T, 128),
    jhS=sem(2),
    jhR=sem(2),
    x=vm(2, T, 256),
    dtb=vm(2, T, 256),
    ecb=vm(2, T, 256),
    etb=vm(2, T, 256),
    yn=vm(2, T, 256),
    v=vm(2, T, 256),
    xdt=vm(2, T, 256),
    xtail=vm(2, T, 256),
    bm=half(2, T, N),
    cm=half(2, T, N),
    seg=vm(2, 3, T, T),
    vw=vm(2, 3, T, T),
    dt=vm(2, T, 128),
    cum=vm(2, T, 128),
    hl=vm(2, 256, N),
    hin=vm(2, 256, N),
    gl=vm(2, 256, N),
    gn=vm(2, 256, N),
    acc=vm(C, N),
    fc=chain_refs(),
    bc=chain_refs(),
    op0=vm(T, D),
    oph=half(T, D),
    opr0=half(NH, R, D),
    opl=half(T, D),
    oplr=half(NH, R, D),
    oplq=both(NH),
    op1=half(T, D),
    opr1=half(NH, R, D),
    opq=both(2, NH),
    lo=half(T, D),
    lor=half(NH, R, D),
    loq=both(NH),
    r0=vm(T, 128),
    urow=vm(R, D),
    orow=vm(R, D),
    agq=dict(LS=sem(NH), LR=sem(NH), RS=sem(NH), RR=sem(NH)),
    scs=vm(2, 8, 128),
    scr=vm(2, NH, 8, 128),
    scq=both(2, NH),
    hos=vm(NH, R, 128),
    hoq=both(NH),
    gm0=half(T, X),
    gm1=half(T, D),
    gmq=dict(LS=sem(NH), LR=sem(NH), RS=sem(NH), RR=sem(NH)),
    ggn=vm(2, T, 256),
    gnb=half(2, T, 256),
    gp=vm(2, T + G, 512),
    ghS=sem(2),
    ghR=sem(2),
    ge=half(2, T, 768),
    gq=half(2, T, D),
    gqr=half(2, NH, R, D),
    gqq=both(2, NH),
    grow=vm(R, D),
    ngp=vm(2, 8, D),
    fas=vm(NH, R, 128),
    faq=both(NH),
    sm=vm(2, 8, 512),
    gbs=vm(2, NH, R, 256),
    gbr=vm(2, NH, R, 256),
    gbq=both(2, NH),
    gss=vm(2, NH, G, 256),
    gsr=vm(2, NH, G, 256),
    gsq=both(2, NH),
    smr=vm(2, NS, 8, 512),
    smq=both(2, NS),
    gcs=half(2, NS, R, 256),
    gcr=half(2, NS, R, 256),
    gcq=both(2, NS),
    gds=half(2, R, 256),
    gdq=both(2, NH),
    we=weight_refs(512),
    wl=weight_refs(256),
    loc=sem(8),
)
LEAVES, TREE = jax.tree.flatten(SCRATCH)


def kernel(
    hid_in,
    og_in,
    ng_ref,
    cx_ref,
    cb_ref,
    hp_ref,
    gg_ref,
    wd_ref,
    wz_in,
    wb_in,
    wo_in,
    ho,
    gi,
    wout,
    bct,
    smo,
    *scratch,
):
    m = SimpleNamespace(
        **{
            k: SimpleNamespace(**v) if isinstance(v, dict) else v
            for k, v in jax.tree.unflatten(TREE, scratch).items()
        }
    )
    s = lax.axis_index("seq")
    h = lax.axis_index("head")
    z = s // 2
    c = s % 2
    hx = h // 4
    hy = h % 4
    finals = []

    def rdma(src, dst, ss, rs, dev):
        return pltpu.make_async_remote_copy(
            src_ref=src, dst_ref=dst, send_sem=ss, recv_sem=rs, device_id=dev, device_id_type=MESH
        )

    def every(lo, hi, f):
        def step(d, carry):
            f(d)
            return carry

        lax.fori_loop(lo, hi, step, 0)

    class Ring:
        def __init__(self, mk, size, send):
            self.mk, self.size, self.send = mk, size, send

        def start(self):
            self.send(lambda d: self.mk(d).start())
            finals.append(lambda: every(1, self.size, lambda d: self.mk(d).wait_send()))

        def wait(self):
            every(1, self.size, lambda d: self.mk(d).wait_recv())

    def far_first(f):
        def step(i):
            d = (6 - i // 4) % 4 * 4 + (6 - i % 4) % 4

            @pl.when(d > 0)
            def _():
                f(d)

        every(0, NH, step)

    def head_ring(src, dst, q, lead=()):
        def mk(d):
            t = (hx + d // 4) % 4 * 4 + (hy + d % 4) % 4
            return rdma(src(t), dst(h), q.S.at[(*lead, d)], q.R.at[(*lead, d)], (s, t))

        return Ring(mk, NH, far_first)

    def seq_ring(src, dst, q, lead=()):
        def mk(d):
            t = lax.rem(s + d, NS)
            return rdma(src(t), dst(s), q.S.at[(*lead, d)], q.R.at[(*lead, d)], (t, h))

        return Ring(mk, NS, lambda f: every(1, NS, f))

    class One:
        def __init__(self, mk, sends, receives):
            self.mk, self.sends, self.receives = mk, sends, receives

        def start(self):
            @pl.when(self.sends)
            def _():
                self.mk().start()

            def last():
                @pl.when(self.sends)
                def _():
                    self.mk().wait_send()

            finals.append(last)

        def wait(self):
            @pl.when(self.receives)
            def _():
                self.mk().wait_recv()

    def rows16(t):
        return pl.ds(pl.multiple_of(t * R, R), R)

    loads = [
        pltpu.make_async_copy(hid_in, m.hid, m.loc.at[0]),
        pltpu.make_async_copy(wz_in.at[0], m.wz.at[0], m.loc.at[1]),
        pltpu.make_async_copy(wb_in.at[0], m.wb.at[0], m.loc.at[2]),
        pltpu.make_async_copy(wo_in.at[0], m.wo.at[0], m.loc.at[3]),
        pltpu.make_async_copy(wz_in.at[1], m.wz.at[1], m.loc.at[4]),
        pltpu.make_async_copy(wb_in.at[1], m.wb.at[1], m.loc.at[5]),
        pltpu.make_async_copy(wo_in.at[1], m.wo.at[1], m.loc.at[6]),
        pltpu.make_async_copy(og_in, m.og, m.loc.at[7]),
    ]
    for cp in loads[:4]:
        cp.start()

    bar = pltpu.get_barrier_semaphore()

    def greet(dev):
        pl.semaphore_signal(bar, inc=1, device_id=dev, device_id_type=MESH)

    every(1, NS, lambda d: greet((lax.rem(s + d, NS), h)))
    every(1, NH, lambda d: greet((s, lax.rem(h + d, NH))))

    m.sp[...] = jnp.zeros((2, 16, 512), F32)
    for l in range(2):
        for k in range(5):
            m.sp[l, k : k + 1, 0:C] = cx_ref[k, l : l + 1, :]
            m.sp[l, k : k + 1, 256:512] = cb_ref[k, l : l + 1, :]
        m.sp[l, 5:6, 0:C] = gg_ref[l : l + 1, :]
        for k in range(3):
            m.sp[l, 6 + k : 7 + k, 0:3] = hp_ref[k, l : l + 1, :]
        rows = [wd_ref[k, l : l + 1, :].astype(F32) for k in range(3)]
        m.wd[l] = jnp.concatenate(rows + [jnp.zeros((R - 3, D), F32)], axis=0).astype(BF16)
    sp = m.sp

    def norm_rows(u, l):
        q = lax.rsqrt(jnp.mean(u * u, axis=1, keepdims=True) + EPS)
        return q, (u * q * ng_ref[l : l + 1, :]).astype(BF16)

    loads[0].wait()

    def norm_step(i):
        at = pl.ds(pl.multiple_of(i * 32, 32), 32)
        q, n = norm_rows(m.hid[at, :], 0)
        m.nx0[at, :] = n
        m.q0[at, :] = jnp.broadcast_to(q, (32, 128))

    every(0, T // 32, norm_step)

    nx = (m.nx0, m.nx1)
    gm = (m.gm0, m.gm1)
    lane = iota((T, 128), 1)
    dt_lane = lane < 3
    lane256 = iota((T, 256), 1)
    head_lane = [jnp.logical_and(lane256 >= 64 * k, lane256 < 64 * k + 64) for k in range(3)]
    causal = iota((T, T), 0) >= iota((T, T), 1)
    tri = jnp.where(causal, 1.0, 0.0).astype(BF16)
    ecol = jnp.where(iota((256, 128), 0) // 64 == iota((256, 128), 1), 1.0, 0.0)
    ecol = jnp.where(iota((256, 128), 1) < 3, ecol, 0.0)
    ecolb = ecol.astype(BF16)

    def only(k, a):
        return jnp.where(head_lane[k], a, jnp.zeros_like(a))

    def silu_slope(a):
        sa = jax.nn.sigmoid(a)
        return sa * (1.0 + a * (1.0 - sa))

    def chain(l, local, out, q, near, far, step):
        ld = m.cum[l, T - 1 : T, :]
        ra, rb, rc = q.Ar, q.Br, q.Cr
        sa, sb, sc = q.As, q.Bs, q.Cs
        A = One(
            lambda: rdma(sa.at[l], ra.at[l], q.AS.at[l], q.AR.at[l], (2 * z + near, h)),
            c == far,
            c == near,
        )

        def link(d):
            zz = z + step * d
            inside = jnp.logical_and(zz >= 0, zz < 4)
            prev = z - step * d
            gets = jnp.logical_and(prev >= 0, prev < 4)
            return One(
                lambda: rdma(
                    sb.at[l], rb.at[l, z], q.BS.at[l, d], q.BR.at[l, d], (2 * zz + near, h)
                ),
                jnp.logical_and(c == near, inside),
                jnp.logical_and(c == near, gets),
            )

        B = [link(d) for d in (2, 1, 3)]
        first = z == 0 if step > 0 else z == 3
        more = jnp.logical_not(first)
        Cc = One(
            lambda: rdma(sc.at[l], rc.at[l], q.CS.at[l], q.CR.at[l], (2 * z + far, h)),
            jnp.logical_and(c == near, more),
            jnp.logical_and(c == far, more),
        )

        def begin():
            @pl.when(c == far)
            def _():
                sa[l, 0:C, :] = local[l, 0:C, :]
                sa[l, C:, :] = jnp.broadcast_to(ld, (G, N))

            A.start()

        def middle():
            A.wait()

            @pl.when(c == near)
            def _():
                other = ra[l, 0:C, :]
                lo = ra[l, C : C + 1, :]
                sb[l, 0:C, :] = decay_rows(ld) * other + local[l, 0:C, :]
                sb[l, C:, :] = jnp.broadcast_to(lo + ld, (G, N))

            for b in B:
                b.start()

        def end():
            for b in B:
                b.wait()

            @pl.when(c == near)
            def _():
                m.acc[...] = jnp.zeros((C, N), F32)
                order = (0, 1, 2) if step > 0 else (3, 2, 1)
                for zz in order:

                    @pl.when(zz < z if step > 0 else zz > z)
                    def _():
                        m.acc[...] = decay_rows(rb[l, zz, C : C + 1, :]) * m.acc[...] + rb[
                            l, zz, 0:C, :
                        ]

                sc[l] = m.acc[...]

            Cc.start()
            out[l, C:, :] = jnp.zeros((256 - C, N), F32)

            @pl.when(c == near)
            def _():
                lo = ra[l, C : C + 1, :]
                out[l, 0:C, :] = decay_rows(lo) * m.acc[...] + ra[l, 0:C, :]

            Cc.wait()

            @pl.when(c == far)
            def _():
                @pl.when(more)
                def _():
                    out[l, 0:C, :] = rc[l]

                @pl.when(first)
                def _():
                    out[l, 0:C, :] = jnp.zeros((C, N), F32)

        return begin, middle, end

    def forward(l, ready):
        n = nx[l][...]
        m.pj[l, G:, 0:256] = padded(dot(n, m.wz[l, 1], 1, 1))
        m.pj[l, G:, 256:512] = dot(n, m.wb[l], 1, 0)
        ready()
        halo = One(
            lambda: rdma(
                m.pj.at[l, pl.ds(T, G), pl.ds(0, 512)],
                m.pj.at[l, pl.ds(0, G), pl.ds(0, 512)],
                m.jhS.at[l],
                m.jhR.at[l],
                (s + 1, h),
            ),
            s < NS - 1,
            s > 0,
        )
        halo.start()
        if l == 0:
            for cp in loads[4:]:
                cp.start()
        m.pjd[l] = padded(dot(n, m.wd[l], 1, 1), 128)
        m.pj[l, G:, 512:768] = padded(dot(n, m.wz[l, 0], 1, 1))
        dt = jnp.where(dt_lane, jax.nn.softplus(m.pjd[l] + sp[l, 6:7, 0:128]), 0.0)
        la = -dt * jnp.exp(sp[l, 7:8, 0:128])
        cum = sums(tri, la, 1, 0)
        m.dt[l] = dt
        m.cum[l] = cum
        dtb = spread(dt)
        etb = spread(jnp.exp(cum[T - 1 : T, :] - cum))
        m.dtb[l] = dtb
        m.etb[l] = etb
        m.ecb[l] = spread(jnp.exp(cum))
        cumt = jnp.transpose(cum)
        for k in range(3):
            m.seg[l, k] = jnp.where(causal, jnp.exp(cum[:, k : k + 1] - cumt[k : k + 1, :]), 0.0)

        @pl.when(s == 0)
        def _():
            m.pj[l, 0:G, 0:512] = jnp.zeros((G, 512), F32)

        halo.wait()
        for kc in (256, 0):
            a = sp[l, 4:5, kc : kc + 256]
            for k in range(4):
                at = G - 3 + k
                a = a + sp[l, k : k + 1, kc : kc + 256] * m.pj[l, at : at + T, kc : kc + 256]
            m.pre[l, :, kc : kc + 256] = a
            post = a * jax.nn.sigmoid(a)
            if kc:
                m.bm[l] = post[:, 0:N].astype(BF16)
                m.cm[l] = post[:, N:].astype(BF16)
        x = post
        m.x[l] = x
        m.xdt[l] = dtb * x
        m.xtail[l] = dtb * etb * x
        m.hl[l] = fine(m.xtail[l], m.bm[l], 0, 0)
        begin, middle, end = chain(l, m.hl, m.hin, m.fc, 1, 0, 1)
        begin()
        scores = dot(m.cm[l], m.bm[l], 1, 1)
        for k in range(3):
            m.vw[l, k] = scores * m.seg[l, k]
        middle()
        yi = jnp.zeros((T, 256), F32)
        for k in range(3):
            yi = yi + fine(m.vw[l, k], only(k, m.xdt[l]), 1, 0)
        m.yn[l] = yi
        end()
        yn = m.yn[l] + m.ecb[l] * fine(m.cm[l], m.hin[l], 1, 1)
        m.yn[l] = yn
        zz = m.pj[l, G:, 512:768]
        m.v[l] = (yn + spread(sp[l, 8:9, 0:128]) * m.x[l]) * (zz * jax.nn.sigmoid(zz))

    def gate_norm(l, r):
        exact = r * m.v[l] * sp[l, 5:6, 0:256]
        m.gnb[l] = exact.astype(BF16)
        return exact - m.gnb[l].astype(F32)

    def gather_rows(buf, cut, width, q):
        def place(dx, dy):
            return (hx + dx) % 4 * 4 + (hy + dy) % 4

        def left(d):
            dx, dy = d // 4, d % 4
            source = rows16(jnp.where(dy == 0, h, place(4 - dx, 0)))
            to = jnp.where(dy == 0, place(dx, 0), place(0, dy))
            part = buf.at[source, pl.ds(0, cut)]
            return rdma(part, part, q.LS.at[d], q.LR.at[d], (s, to))

        def right(d):
            dx, dy = d // 4, d % 4
            source = rows16(jnp.where(dx == 0, h, place(0, 4 - dy)))
            to = jnp.where(dx == 0, place(0, dy), place(dx, 0))
            part = buf.at[source, pl.ds(cut, width - cut)]
            return rdma(part, part, q.RS.at[d], q.RR.at[d], (s, to))

        def all_sent():
            every(1, NH, lambda d: left(d).wait_send())
            every(1, NH, lambda d: right(d).wait_send())

        finals.append(all_sent)
        order = (2, 1, 3)
        for k in order:
            left(4 * k).start()
            right(k).start()
        for k in order:
            left(k).start()
            right(4 * k).start()

        def end():
            for k in (1, 3, 2):
                left(4 * k).wait_recv()
                for j in order:
                    left(4 * k + j).start()
                right(k).wait_recv()
                for j in order:
                    right(4 * j + k).start()

            def rest(d):
                @pl.when(d % 4 > 0)
                def _():
                    left(d).wait_recv()

                @pl.when(d // 4 > 0)
                def _():
                    right(d).wait_recv()

            every(1, NH, rest)

        return end

    def rows_sum(src, dst, q, lead=()):
        ring = head_ring(lambda t: src.at[rows16(t)], lambda me: dst.at[me], q, lead)
        ring.start()
        dst[h] = src[rows16(h), :]

        def end():
            ring.wait()
            return total_of(dst, NH)

        return end

    def mix_out(l):
        for j in range(3):
            at = slice(512 * j, 512 * j + 512)
            m.op1[:, at] = dot(m.gnb[l, :, 0:C], m.wo[l, :, at], 1, 0).astype(BF16)
        return rows_sum(m.op1, m.opr1, m.opq, (l,))

    def total_of(ref, count):
        total = ref[0].astype(F32)
        for t in range(1, count):
            total = total + ref[t].astype(F32)
        return total

    def scalars(i, *values, beside=lambda: None):
        ones = jnp.full((R, 256), 1.0, BF16)
        row = iota((8, 128), 0)
        packed = jnp.zeros((8, 128), F32)
        for k, value in enumerate(values):
            over = sums(ones, value, 1, 1)[0:8]
            packed = jnp.where(row == 2 * k, over[:, 0:128], packed)
            packed = jnp.where(row == 2 * k + 1, over[:, 128:256], packed)
        m.scs[i] = packed
        ring = head_ring(lambda t: m.scs.at[i], lambda me: m.scr.at[i, me], m.scq, (i,))
        ring.start()
        m.scr[i, h] = m.scs[i]
        beside()
        ring.wait()
        total = total_of(m.scr.at[i], NH)
        cols = jnp.transpose(jnp.concatenate([total, jnp.zeros((120, 128), F32)], axis=0))
        return [
            jnp.concatenate([cols[:, 2 * k : 2 * k + 1], cols[:, 2 * k + 1 : 2 * k + 2]], axis=0)
            for k in range(len(values))
        ]

    def g_gate(l):
        m.ggn[l] = padded(dot(gm[l][:, 0:D], m.wo[l], 1, 1))

    def weight_parts(q, l, parts):
        w = q.r.shape[-1]
        for k in range(4):
            at = 0
            for left, right in parts:
                piece = dot(left[:, 384 * k : 384 * k + 384], right, 0, 0)
                wide = piece.shape[1]
                q.s[l, 0, k, :, at : at + wide] = piece[0:C].astype(BF16)
                q.s[l, 1, k, :, at : at + wide] = piece[C:].astype(BF16)
                at += wide
        yes = jnp.bool_(True)
        pair = One(
            lambda: rdma(
                q.s.at[l, 1 - c], q.r.at[l], q.S.at[l], q.R.at[l], (2 * z + 1 - c, h)
            ),
            yes,
            yes,
        )

        def mk(d):
            t = lax.rem(z + d, 4)
            return rdma(
                q.c.at[l, t], q.x.at[l, z], q.U.at[l, d], q.V.at[l, d], (2 * t + c, h)
            )

        ring = Ring(mk, 4, lambda f: every(1, 4, f))

        def middle():
            pair.wait()
            for k in range(4):
                q.c[l, k] = (q.s[l, c, k].astype(F32) + q.r[l, k].astype(F32)).astype(BF16)
            ring.start()
            q.x[l, z] = q.c[l, z]

        def end(col):
            ring.wait()
            wout[l, :, col : col + w] = total_of(q.x.at[l], 4)

        return pair.start, middle, end

    def backward(l, r, s2, early, late, last_of_all):
        gain = sp[l, 5:6, 0:256]
        skip = spread(sp[l, 8:9, 0:128])
        v = m.v[l]
        ggn = m.ggn[l]
        rv = r * v
        gv = r * (gain * ggn) - v * (r * r * s2 / INNER)
        zz = m.pj[l, G:, 512:768]
        sz = jax.nn.sigmoid(zz)
        x = m.x[l]
        y = m.yn[l] + skip * x
        gy = gv * (zz * sz)
        gyc = m.ecb[l] * gy
        m.gl[l] = fine(gyc, m.cm[l], 0, 0)
        begin, middle, end = chain(l, m.gl, m.gn, m.bc, 0, 1, -1)
        begin()
        m.sm[l, 5:6, 0:256] = jnp.sum(ggn * rv, axis=0, keepdims=True)
        if l:
            gate_norm(l, r)
        m.ge[l, :, 512:768] = (gv * y * (sz * (1.0 + zz * (1.0 - sz)))).astype(BF16)
        gxd = jnp.zeros((T, 256), F32)
        ds = jnp.zeros((T, T), F32)
        xdt = m.xdt[l]
        for k in range(3):
            g_k = only(k, gy)
            gxd = gxd + fine(m.vw[l, k], g_k, 0, 0)
            ds = ds + fine(g_k, xdt, 1, 1) * m.seg[l, k]
        middle()
        weight_go, weight_mid, weight_end = weight_parts(
            m.we, l, [(nx[l], m.ge[l, :, 512:768]), (gm[l], m.gnb[l])]
        )
        bm, cm = m.bm[l], m.cm[l]
        db = fine(ds, cm, 0, 0)
        dc = fine(ds, bm, 1, 0) + fine(gyc, m.hin[l], 1, 0)
        gskip = jnp.sum(gy * x, axis=0, keepdims=True)
        early()
        end()
        weight_go()
        gnx = m.gn[l]
        db = db + fine(m.xtail[l], gnx, 1, 0)
        rt = m.etb[l] * fine(bm, gnx, 1, 1)
        gxs = gxd + rt
        gx = m.dtb[l] * gxs + skip * gy
        for kc, gpost in ((0, gx), (256, jnp.concatenate([db, dc], axis=1))):
            gpre = gpost * silu_slope(m.pre[l, :, kc : kc + 256])
            m.gp[l, 0:T, kc : kc + 256] = gpre
        halo = One(
            lambda: rdma(
                m.gp.at[l, pl.ds(0, G)], m.gp.at[l, pl.ds(T, G)], m.ghS.at[l], m.ghR.at[l], (s - 1, h)
            ),
            s > 0,
            s < NS - 1,
        )
        halo.start()
        dt = m.dt[l]
        gdt = fine(x * gxs, ecolb, 1, 0)
        cum = m.cum[l]
        inner = jnp.sum(gnx * m.hin[l], axis=1, keepdims=True)
        inner = jnp.sum(inner * ecol, axis=0, keepdims=True)
        tail = jnp.sum(xdt * rt, axis=0, keepdims=True)
        both = fine(jnp.concatenate([tail, gskip, jnp.zeros((6, 256), F32)], axis=0), ecolb, 1, 0)
        last = both[0:1] + jnp.exp(cum[T - 1 : T, :]) * inner
        pairs = gy * m.yn[l] - xdt * gxs
        hi, lo = halves(pairs)
        rest = (pairs - hi.astype(F32) - lo.astype(F32)).astype(BF16)
        dcum = fine(pairs, ecolb, 1, 0) + dot(rest, ecolb, 1, 0)
        dcum = dcum + jnp.where(iota((T, 128), 0) == T - 1, last, 0.0)
        gla = sums(tri, dcum, 0, 0)
        rate = jnp.exp(sp[l, 7:8, 0:128])
        gd = gdt - gla * rate
        gdtr = jnp.where(dt_lane, gd * jax.nn.sigmoid(m.pjd[l] + sp[l, 6:7, 0:128]), 0.0)
        weight_mid()
        m.sm[l, 5:6, 256:512] = jnp.zeros((1, 256), F32)
        m.sm[l, 6:7, 0:128] = jnp.sum(gdtr, axis=0, keepdims=True)
        m.sm[l, 6:7, 128:256] = jnp.sum(-gla * dt * rate, axis=0, keepdims=True)
        m.sm[l, 6:7, 256:384] = both[1:2]
        m.sm[l, 6:7, 384:512] = jnp.zeros((1, 128), F32)
        m.sm[l, 7:8, :] = jnp.zeros((1, 512), F32)
        @pl.when(s == NS - 1)
        def _():
            m.gp[l, T:, :] = jnp.zeros((G, 512), F32)

        halo.wait()
        for kc in (0, 256):
            gj = jnp.zeros((T, 256), F32)
            for k in range(4):
                gj = gj + sp[l, k : k + 1, kc : kc + 256] * m.gp[l, 3 - k : 3 - k + T, kc : kc + 256]
            if kc == 0:
                gj = jnp.concatenate([gj[:, 0:C], gdtr[:, 0:64]], axis=1)
            else:
                gt = jnp.transpose(gj)
                for t in range(NH):
                    m.gbs[l, t] = gt[R * t : R * t + R, :]
            m.ge[l, :, kc : kc + 256] = gj.astype(BF16)
        late()
        low = gdtr[:, 0:R].astype(BF16)
        for j in range(3):
            at = slice(512 * j, 512 * j + 512)
            part = (
                dot(m.ge[l, :, 0:C], m.wz[l, 1, :, at], 1, 0)
                + dot(m.ge[l, :, 512 : 512 + C], m.wz[l, 0, :, at], 1, 0)
                + dot(m.ge[l, :, 256:512], m.wb[l, at, :], 1, 1)
                + dot(low, m.wd[l, :, at], 1, 0)
            )
            if l == 0:
                m.ngp[l, 0:1, at] = jnp.sum(part * (m.hid[:, at] * m.q0[:, 0:1]), axis=0, keepdims=True)
            m.gq[l, :, at] = part.astype(BF16)
        ring = head_ring(
            lambda t: m.gq.at[l, rows16(t)], lambda me: m.gqr.at[l, me], m.gqq, (l,)
        )
        ring.start()
        m.gqr[l, h] = m.gq[l, rows16(h), :]
        for kc in (0, 256):
            gpre = m.gp[l, 0:T, kc : kc + 256]
            for k in range(4):
                at = G - 3 + k
                m.sm[l, k : k + 1, kc : kc + 256] = jnp.sum(
                    gpre * m.pj[l, at : at + T, kc : kc + 256], axis=0, keepdims=True
                )
            m.sm[l, 4:5, kc : kc + 256] = jnp.sum(gpre, axis=0, keepdims=True)
        last_of_all()
        last_go, last_mid, last_end = weight_parts(m.wl, l, [(nx[l], m.ge[l, :, 0:256])])
        last_go()

        def finish():
            ring.wait()
            return total_of(m.gqr.at[l], NH)

        return finish, weight_end, last_mid, last_end

    def norm_back(l, u, g, gn):
        q = lax.rsqrt(jnp.mean(u * u, axis=1, keepdims=True) + EPS)
        w = gn * ng_ref[l : l + 1, :]
        if l:
            m.ngp[l, 0:1, :] = jnp.sum(gn * u * q, axis=0, keepdims=True)
        return g + q * w - u * (q * q * q * (jnp.sum(w * u, axis=1, keepdims=True) / D))

    class Small:
        def __init__(self, l):
            self.l = l
            self.a = head_ring(
                lambda t: m.gbs.at[l, t], lambda me: m.gbr.at[l, me], m.gbq, (l,)
            )
            self.e = head_ring(
                lambda t: m.gss.at[l, t], lambda me: m.gsr.at[l, me], m.gsq, (l,)
            )
            self.b = seq_ring(lambda t: m.gcs.at[l, t], lambda me: m.gcr.at[l, me], m.gcq, (l,))
            self.c = seq_ring(lambda t: m.sm.at[l], lambda me: m.smr.at[l, me], m.smq, (l,))
            self.d = head_ring(lambda t: m.gds.at[l], lambda me: bct.at[l, me], m.gdq, (l,))

        def first(self):
            l = self.l
            self.a.start()
            m.gbr[l, h] = m.gbs[l, h]

        def first_small(self):
            l = self.l
            for t in range(NH):
                m.gss[l, t, 0:5, :] = m.sm[l, 0:5, 256:512]
                m.gss[l, t, 5:6, 0:S] = m.ngp[l, 0:1, S * t : S * t + S]
                m.gss[l, t, 5:6, S:] = jnp.zeros((1, 256 - S), F32)
                m.gss[l, t, 6:, :] = jnp.zeros((2, 256), F32)
            self.e.start()
            m.gsr[l, h] = m.gss[l, h]

        def second(self):
            l = self.l
            self.a.wait()
            total = total_of(m.gbr.at[l], NH)
            part = dot(total.astype(BF16), nx[l][...], 1, 0).astype(BF16)
            for t in range(NS):
                m.gcs[l, t] = padded(part[:, C * t : C * t + C])
            self.b.start()
            m.gcr[l, s] = m.gcs[l, s]

        def second_small(self):
            l = self.l
            self.e.wait()
            total = total_of(m.gsr.at[l], NH)
            m.sm[l, 0:5, 256:512] = total[0:5]
            m.sm[l, 7:8, 0:256] = total[5:6]
            self.c.start()
            m.smr[l, s] = m.sm[l]

        def third(self):
            l = self.l
            self.b.wait()
            m.gds[l] = total_of(m.gcr.at[l], NS).astype(BF16)
            self.d.start()
            bct[l, h] = m.gds[l]

        def third_small(self):
            self.c.wait()
            smo[self.l] = total_of(m.smr.at[self.l], NS)

    small = [Small(0), Small(1)]

    loads[1].wait()
    loads[2].wait()
    forward(0, lambda: pl.semaphore_wait(bar, NH - 1 + NS - 1))
    loads[3].wait()
    ends = []

    def high_parts():
        vg = (m.v[0] * sp[0, 5:6, 0:256])[:, 0:C]
        for j in range(3):
            at = slice(512 * j, 512 * j + 512)
            m.op0[:, at] = fine(vg, m.wo[0, :, at], 1, 0)
            m.oph[:, at] = m.op0[:, at].astype(BF16)
        ends.append(rows_sum(m.oph, m.opr0, m.opq, (0,)))

    sq = scalars(0, m.v[0] * m.v[0], beside=high_parts)[0]
    r0 = lax.rsqrt(sq / INNER + EPS)
    m.r0[...] = jnp.broadcast_to(r0, (T, 128))
    rest = gate_norm(0, r0)[:, 0:C].astype(BF16)
    for j in range(3):
        at = slice(512 * j, 512 * j + 512)
        left = dot(rest, m.wo[0, :, at], 1, 0)
        m.lo[:, at] = left.astype(BF16)
        m.opl[:, at] = (r0 * (m.op0[:, at] - m.oph[:, at].astype(F32)) - left).astype(BF16)
    ends.append(rows_sum(m.opl, m.oplr, m.oplq))
    o0 = m.r0[rows16(h), 0:1] * ends[0]() + ends[1]()
    m.orow[...] = o0
    u1 = m.hid[rows16(h), :] + o0
    m.urow[...] = u1
    m.nx1[rows16(h), :] = norm_rows(u1, 1)[1]
    ag_end = gather_rows(m.nx1, D // 2, D, m.agq)

    for cp in loads[4:]:
        cp.wait()
    m.gm1[...] = m.og[...].astype(BF16)
    g_gate(1)
    ag_end()

    low = head_ring(lambda t: m.lo.at[rows16(t)], lambda me: m.lor.at[me], m.loq)
    low.start()
    m.lor[h] = m.lo[rows16(h), :]
    forward(1, lambda: None)
    v = m.v[1]
    sq, s2 = scalars(1, v * v, m.ggn[1] * (sp[1, 5:6, 0:256] * v))
    r1 = lax.rsqrt(sq / INNER + EPS)
    rings = []

    def hidden_rows():
        final = m.urow[...] + rings[0]()
        for t in range(NH):
            m.hos[t] = padded(final[:, S * t : S * t + S], 128)

    back1, e1_end, l1_mid, l1_end = backward(
        1, r1, r1 * s2, lambda: rings.append(mix_out(1)), lambda: None, lambda: None
    )
    l1_mid()
    hidden_rows()
    low.wait()
    m.orow[...] = m.orow[...] + total_of(m.lor, NH)
    g_rows = norm_back(1, m.urow[...], m.og[rows16(h), :], back1())
    m.grow[...] = g_rows
    rounded = g_rows.astype(BF16)
    m.gm0[rows16(h), 0:D] = rounded
    m.gm0[rows16(h), D:] = scalar_lanes(
        jnp.sum(rounded.astype(F32) * m.orow[...], axis=1, keepdims=True)
    )
    agm_end = gather_rows(m.gm0, D // 2, X, m.gmq)
    e1_end(256)
    l1_end(0)
    agm_end()

    g_gate(0)
    s2 = m.gm0[:, D:].astype(F32)
    hor = head_ring(lambda t: m.hos.at[t], lambda me: ho.at[rows16(me)], m.hoq)

    def early0():
        hor.start()
        ho[rows16(h), :] = m.hos[h]
        small[1].first()
        small[1].first_small()

    back0, e0_end, l0_mid, l0_end = backward(0, m.r0[:, 0:1], s2[:, 0:1] + s2[:, 1:2], early0, small[0].first, small[0].first_small)
    small[1].second()
    small[1].second_small()
    small[0].second()
    l0_mid()
    small[0].second_small()
    small[1].third()
    small[0].third()
    g_rows = norm_back(0, m.hid[rows16(h), :], m.grow[...], back0())
    for t in range(NH):
        m.fas[t] = padded(g_rows[:, S * t : S * t + S], 128)
    far = head_ring(lambda t: m.fas.at[t], lambda me: gi.at[rows16(me)], m.faq)
    far.start()
    gi[rows16(h), :] = m.fas[h]
    small[1].third_small()
    small[0].third_small()
    e0_end(256)
    l0_end(0)
    hor.wait()
    small[1].d.wait()
    small[0].d.wait()
    far.wait()
    for f in finals:
        f()


def arrange(
    ho_in, gi_in, w_in, bct_in, smo_in, o_ho, o_gi, o_ng, o_zx, o_bc, o_dt, o_cx, o_cb, o_hp, o_gg, o_wo, ho, gi, w, bct, smo, sems
):
    pairs = ((w_in, w), (ho_in, ho), (gi_in, gi), (bct_in, bct), (smo_in, smo))
    copies = [pltpu.make_async_copy(a, b, sems.at[i]) for i, (a, b) in enumerate(pairs)]
    for cp in copies:
        cp.start()
    for cp in copies:
        cp.wait()
    o_ho[...] = jnp.transpose(ho[...])[0:S, :]
    o_gi[...] = jnp.transpose(gi[...])[0:S, :]
    for l in range(2):
        o_ng[l : l + 1, :] = smo[l, 7:8, 0:S]
        o_zx[l, :, 0, :] = w[l, :, 256 : 256 + C]
        o_zx[l, :, 1, :] = w[l, :, 0:C]
        rows = jnp.concatenate([bct[l, t].astype(F32) for t in range(NH)], axis=0)
        o_bc[l] = jnp.transpose(rows)[0:C, :]
        dts = jnp.transpose(w[l, :, 128:256])
        for k in range(3):
            o_dt[k, l : l + 1, :] = dts[64 + k : 65 + k, :]
            o_hp[k, l : l + 1, :] = smo[l, 6:7, 128 * k : 128 * k + 3]
        for k in range(5):
            o_cx[k, l : l + 1, :] = smo[l, k : k + 1, 0:C]
            o_cb[k, l : l + 1, :] = smo[l, k : k + 1, 256:512]
        o_gg[l : l + 1, :] = smo[l, 5:6, 0:C]
        o_wo[l] = jnp.transpose(w[l, :, 512:768])[0:C, :]


def on_device(
    hidden_in,
    norm_gain,
    gate_mixer_weight,
    w_bc,
    w_dt,
    conv_x,
    conv_bc,
    head_params,
    gate_gain,
    w_out,
    out_grad,
):
    whole = pl.BlockSpec(memory_space=pltpu.VMEM)
    there = pl.BlockSpec(memory_space=pl.ANY)

    def out(*shape, dtype=F32):
        return jax.ShapeDtypeStruct(shape, dtype)

    raw = pl.pallas_call(
        kernel,
        out_shape=[
            out(T, 128),
            out(T, 128),
            out(2, C, 768),
            out(2, NH, R, 256, dtype=BF16),
            out(2, 8, 512),
        ],
        in_specs=[there] * 2 + [whole] * 6 + [there] * 3,
        out_specs=[whole] * 5,
        scratch_shapes=LEAVES,
        compiler_params=pltpu.CompilerParams(
            collective_id=0, has_side_effects=True, vmem_limit_bytes=60 * 2**20
        ),
        name="two_layers",
    )(
        hidden_in,
        out_grad,
        norm_gain,
        jnp.transpose(conv_x, (1, 0, 2)),
        jnp.transpose(conv_bc, (1, 0, 2)),
        jnp.transpose(head_params, (1, 0, 2)),
        gate_gain,
        jnp.transpose(w_dt, (2, 0, 1)),
        jnp.transpose(gate_mixer_weight, (0, 2, 3, 1)),
        w_bc,
        w_out,
    )
    ho, gi, ng, zx, bc, dt, cx, cb, hp, gg, wo = pl.pallas_call(
        arrange,
        out_shape=[
            out(S, T),
            out(S, T),
            out(2, S),
            out(2, C, 2, C),
            out(2, C, 256),
            out(3, 2, C),
            out(5, 2, C),
            out(5, 2, 256),
            out(3, 2, 3),
            out(2, C),
            out(2, C, C),
        ],
        in_specs=[there] * 5,
        out_specs=[whole] * 11,
        scratch_shapes=[vm(T, 128), vm(T, 128), vm(2, C, 768), half(2, NH, R, 256), vm(2, 8, 512), sem(5)],
        compiler_params=pltpu.CompilerParams(vmem_limit_bytes=60 * 2**20),
        name="arrange",
    )(*raw)
    return (
        jnp.transpose(ho),
        jnp.transpose(gi),
        ng,
        zx,
        bc,
        jnp.transpose(dt, (1, 2, 0)),
        jnp.transpose(cx, (1, 0, 2)),
        jnp.transpose(cb, (1, 0, 2)),
        jnp.transpose(hp, (1, 0, 2)),
        gg,
        wo,
    )


def solution(mesh):
    return jax.shard_map(
        on_device,
        mesh=mesh,
        in_specs=(
            P("seq", None),
            P(),
            P(None, None, None, "head"),
            P(),
            P(None, None, "head"),
            P(None, None, "head"),
            P(),
            P(None, None, "head"),
            P(None, "head"),
            P(None, "head", None),
            P("seq", None),
        ),
        out_specs=(
            P("seq", "head"),
            P("seq", "head"),
            P(None, "head"),
            P(None, "seq", None, "head"),
            P(None, "seq", None),
            P(None, "seq", "head"),
            P(None, None, "head"),
            P(),
            P(None, None, "head"),
            P(None, "head"),
            P(None, "head", "seq"),
        ),
        check_vma=False,
    )
```

```python
from types import SimpleNamespace

import jax
import jax.numpy as jnp
from jax import lax
from jax.experimental import pallas as pl
from jax.experimental.pallas import tpu as pltpu
from jax.sharding import PartitionSpec as P

EPS = 1e-05
MESH = pl.DeviceIdType.MESH
F32 = jnp.float32
BF16 = jnp.bfloat16

T = 256
R = 16
G = 8
D = 1536
INNER = 3072
C = 192
N = 128
NH = 16
NS = 8
X = D + 128
S = D // NH


def dot(a, b, ca, cb):
    return lax.dot_general(a, b, (((ca,), (cb,)), ((), ())), preferred_element_type=F32)


def halves(a):
    if a.dtype == BF16:
        return (a,)
    hi = a.astype(BF16)
    return hi, (a - hi.astype(F32)).astype(BF16)


def fine(a, b, ca, cb):
    total = None
    for i, p in enumerate(halves(a)):
        for j, q in enumerate(halves(b)):
            if i + j < 2:
                term = dot(p, q, ca, cb)
                total = term if total is None else total + term
    return total


def sums(ones, value, ca, cb):
    hi, lo = halves(value)
    rest = (value - hi.astype(F32) - lo.astype(F32)).astype(BF16)
    return dot(ones, hi, ca, cb) + dot(ones, lo, ca, cb) + dot(ones, rest, ca, cb)


def iota(shape, dim):
    return lax.broadcasted_iota(jnp.int32, shape, dim)


def padded(a, lanes=256):
    return jnp.concatenate([a, jnp.zeros((a.shape[0], lanes - a.shape[1]), a.dtype)], axis=1)


def spread(col):
    rows = col.shape[0]
    lane = iota((rows, 128), 1)
    parts = [jnp.broadcast_to(col[:, k : k + 1], (rows, 128)) for k in range(3)]
    return jnp.concatenate(
        [jnp.where(lane < 64, parts[0], parts[1]), jnp.where(lane < 64, parts[2], 0.0)], axis=1
    )


def scalar_lanes(col):
    hi = col.astype(BF16).astype(F32)
    lane = iota((col.shape[0], 128), 1)
    return jnp.where(lane == 0, hi, jnp.where(lane == 1, col - hi, 0.0)).astype(BF16)


def decay_rows(log_row):
    e = jnp.exp(log_row)
    return jnp.concatenate(
        [jnp.broadcast_to(e[:, k : k + 1], (64, 128)) for k in range(3)], axis=0
    )


def vm(*shape, dtype=F32):
    return pltpu.VMEM(shape, dtype)


def half(*shape):
    return pltpu.VMEM(shape, BF16)


def sem(*shape):
    return pltpu.SemaphoreType.DMA(shape)


def both(*shape):
    return dict(S=sem(*shape), R=sem(*shape))


def chain_refs():
    return dict(
        As=vm(2, C + G, N),
        Ar=vm(2, C + G, N),
        AS=sem(2),
        AR=sem(2),
        Bs=vm(2, C + G, N),
        Br=vm(2, 4, C + G, N),
        BS=sem(2, 4),
        BR=sem(2, 4),
        Cs=vm(2, C, N),
        Cr=vm(2, C, N),
        CS=sem(2),
        CR=sem(2),
    )


def weight_refs(w):
    return dict(
        s=half(2, 2, 4, C, w),
        r=half(2, 4, C, w),
        c=half(2, 4, C, w),
        x=half(2, 4, C, w),
        S=sem(2),
        R=sem(2),
        U=sem(2, 4),
        V=sem(2, 4),
    )


SCRATCH = dict(
    hid=vm(T, D),
    og=vm(T, D),
    wz=half(2, 2, C, D),
    wb=half(2, D, 256),
    wo=half(2, C, D),
    sp=vm(2, 16, 512),
    wd=half(2, R, D),
    q0=vm(T, 128),
    nx0=half(T, D),
    nx1=half(T, D),
    pj=vm(2, G + T, 768),
    pre=vm(2, T, 512),
    pjd=vm(2, T, 128),
    jhS=sem(2),
    jhR=sem(2),
    x=vm(2, T, 256),
    dtb=vm(2, T, 256),
    ecb=vm(2, T, 256),
    etb=vm(2, T, 256),
    yn=vm(2, T, 256),
    v=vm(2, T, 256),
    xdt=vm(2, T, 256),
    xtail=vm(2, T, 256),
    bm=half(2, T, N),
    cm=half(2, T, N),
    seg=vm(2, 3, T, T),
    vw=vm(2, 3, T, T),
    dt=vm(2, T, 128),
    cum=vm(2, T, 128),
    hl=vm(2, 256, N),
    hin=vm(2, 256, N),
    gl=vm(2, 256, N),
    gn=vm(2, 256, N),
    acc=vm(C, N),
    fc=chain_refs(),
    bc=chain_refs(),
    op0=vm(T, D),
    oph=half(T, D),
    opr0=half(NH, R, D),
    opl=half(T, D),
    oplr=half(NH, R, D),
    oplq=both(NH),
    op1=half(T, D),
    opr1=half(NH, R, D),
    opq=both(2, NH),
    lo=half(T, D),
    lor=half(NH, R, D),
    loq=both(NH),
    r0=vm(T, 128),
    urow=vm(R, D),
    orow=vm(R, D),
    agq=dict(LS=sem(NH), LR=sem(NH), RS=sem(NH), RR=sem(NH)),
    scs=vm(2, 8, 128),
    scr=vm(2, NH, 8, 128),
    scq=both(2, NH),
    hos=vm(NH, R, 128),
    hoq=both(NH),
    gm0=half(T, X),
    gm1=half(T, D),
    gmq=dict(LS=sem(NH), LR=sem(NH), RS=sem(NH), RR=sem(NH)),
    ggn=vm(2, T, 256),
    gnb=half(2, T, 256),
    gp=vm(2, T + G, 512),
    ghS=sem(2),
    ghR=sem(2),
    ge=half(2, T, 768),
    gq=half(2, T, D),
    gqr=half(2, NH, R, D),
    gqq=both(2, NH),
    grow=vm(R, D),
    ngp=vm(2, 8, D),
    fas=vm(NH, R, 128),
    faq=both(NH),
    sm=vm(2, 8, 512),
    gbs=vm(2, NH, R, 256),
    gbr=vm(2, NH, R, 256),
    gbq=both(2, NH),
    gss=vm(2, NH, G, 256),
    gsr=vm(2, NH, G, 256),
    gsq=both(2, NH),
    smr=vm(2, NS, 8, 512),
    smq=both(2, NS),
    gcs=half(2, NS, R, 256),
    gcr=half(2, NS, R, 256),
    gcq=both(2, NS),
    gds=half(2, R, 256),
    gdq=both(2, NH),
    we=weight_refs(512),
    wl=weight_refs(256),
    ngv=vm(2, D),
    cxv=vm(5, 2, C),
    cbv=vm(5, 2, 256),
    hpv=vm(3, 2, 3),
    ggv=vm(2, C),
    hov=vm(T, 128),
    giv=vm(T, 128),
    wv=vm(2, C, 768),
    bctv=half(2, NH, R, 256),
    smov=vm(2, 8, 512),
    loc=sem(18),
)
LEAVES, TREE = jax.tree.flatten(SCRATCH)


def kernel(
    hid_in,
    og_in,
    ng_in,
    cx_in,
    cb_in,
    hp_in,
    gg_in,
    wd_ref,
    wz_in,
    wb_in,
    wo_in,
    ho_out,
    gi_out,
    w_out,
    bct_out,
    smo_out,
    *scratch,
):
    m = SimpleNamespace(
        **{
            k: SimpleNamespace(**v) if isinstance(v, dict) else v
            for k, v in jax.tree.unflatten(TREE, scratch).items()
        }
    )
    s = lax.axis_index("seq")
    h = lax.axis_index("head")
    z = s // 2
    c = s % 2
    hx = h // 4
    hy = h % 4
    finals = []

    def rdma(src, dst, ss, rs, dev):
        return pltpu.make_async_remote_copy(
            src_ref=src, dst_ref=dst, send_sem=ss, recv_sem=rs, device_id=dev, device_id_type=MESH
        )

    def every(lo, hi, f):
        def step(d, carry):
            f(d)
            return carry

        lax.fori_loop(lo, hi, step, 0)

    class Ring:
        def __init__(self, mk, size, send):
            self.mk, self.size, self.send = mk, size, send

        def start(self):
            self.send(lambda d: self.mk(d).start())
            finals.append(lambda: every(1, self.size, lambda d: self.mk(d).wait_send()))

        def wait(self):
            every(1, self.size, lambda d: self.mk(d).wait_recv())

    def far_first(f):
        for d in (10, 6, 9, 14, 11, 5, 15, 7, 13, 8, 2, 4, 1, 12, 3):
            f(d)

    def head_ring(src, dst, q, lead=()):
        def mk(d):
            t = (hx + d // 4) % 4 * 4 + (hy + d % 4) % 4
            return rdma(src(t), dst(h), q.S.at[(*lead, d)], q.R.at[(*lead, d)], (s, t))

        return Ring(mk, NH, far_first)

    def seq_ring(src, dst, q, lead=()):
        def mk(d):
            t = lax.rem(s + d, NS)
            return rdma(src(t), dst(s), q.S.at[(*lead, d)], q.R.at[(*lead, d)], (t, h))

        return Ring(mk, NS, lambda f: every(1, NS, f))

    class One:
        def __init__(self, mk, sends, receives):
            self.mk, self.sends, self.receives = mk, sends, receives

        def start(self):
            @pl.when(self.sends)
            def _():
                self.mk().start()

            def last():
                @pl.when(self.sends)
                def _():
                    self.mk().wait_send()

            finals.append(last)

        def wait(self):
            @pl.when(self.receives)
            def _():
                self.mk().wait_recv()

    def rows16(t):
        return pl.ds(pl.multiple_of(t * R, R), R)

    ng_ref, cx_ref, cb_ref, hp_ref, gg_ref = m.ngv, m.cxv, m.cbv, m.hpv, m.ggv
    ho, gi, wout, bct, smo = m.hov, m.giv, m.wv, m.bctv, m.smov

    few = [
        pltpu.make_async_copy(a, b, m.loc.at[8 + i])
        for i, (a, b) in enumerate(
            zip((cx_in, cb_in, hp_in, gg_in, ng_in), (cx_ref, cb_ref, hp_ref, gg_ref, ng_ref))
        )
    ]
    for cp in few:
        cp.start()
    loads = [
        pltpu.make_async_copy(hid_in, m.hid, m.loc.at[0]),
        pltpu.make_async_copy(wz_in.at[0], m.wz.at[0], m.loc.at[1]),
        pltpu.make_async_copy(wb_in.at[0], m.wb.at[0], m.loc.at[2]),
        pltpu.make_async_copy(wo_in.at[0], m.wo.at[0], m.loc.at[3]),
        pltpu.make_async_copy(wz_in.at[1], m.wz.at[1], m.loc.at[4]),
        pltpu.make_async_copy(wb_in.at[1], m.wb.at[1], m.loc.at[5]),
        pltpu.make_async_copy(wo_in.at[1], m.wo.at[1], m.loc.at[6]),
        pltpu.make_async_copy(og_in, m.og, m.loc.at[7]),
    ]
    for cp in loads[:4]:
        cp.start()

    bar = pltpu.get_barrier_semaphore()

    def greet(dev):
        pl.semaphore_signal(bar, inc=1, device_id=dev, device_id_type=MESH)

    every(1, NS, lambda d: greet((lax.rem(s + d, NS), h)))
    every(1, NH, lambda d: greet((s, lax.rem(h + d, NH))))

    m.sp[...] = jnp.zeros((2, 16, 512), F32)
    for cp in few:
        cp.wait()
    for l in range(2):
        for k in range(5):
            m.sp[l, k : k + 1, 0:C] = cx_ref[k, l : l + 1, :]
            m.sp[l, k : k + 1, 256:512] = cb_ref[k, l : l + 1, :]
        m.sp[l, 5:6, 0:C] = gg_ref[l : l + 1, :]
        for k in range(3):
            m.sp[l, 6 + k : 7 + k, 0:3] = hp_ref[k, l : l + 1, :]
        rows = [wd_ref[k, l : l + 1, :].astype(F32) for k in range(3)]
        m.wd[l] = jnp.concatenate(rows + [jnp.zeros((R - 3, D), F32)], axis=0).astype(BF16)
    sp = m.sp

    def norm_rows(u, l):
        q = lax.rsqrt(jnp.mean(u * u, axis=1, keepdims=True) + EPS)
        return q, (u * q * ng_ref[l : l + 1, :]).astype(BF16)

    loads[0].wait()

    def norm_step(i):
        at = pl.ds(pl.multiple_of(i * 32, 32), 32)
        q, n = norm_rows(m.hid[at, :], 0)
        m.nx0[at, :] = n
        m.q0[at, :] = jnp.broadcast_to(q, (32, 128))

    every(0, T // 32, norm_step)

    nx = (m.nx0, m.nx1)
    gm = (m.gm0, m.gm1)
    lane = iota((T, 128), 1)
    dt_lane = lane < 3
    lane256 = iota((T, 256), 1)
    head_lane = [jnp.logical_and(lane256 >= 64 * k, lane256 < 64 * k + 64) for k in range(3)]
    causal = iota((T, T), 0) >= iota((T, T), 1)
    tri = jnp.where(causal, 1.0, 0.0).astype(BF16)
    ecol = jnp.where(iota((256, 128), 0) // 64 == iota((256, 128), 1), 1.0, 0.0)
    ecol = jnp.where(iota((256, 128), 1) < 3, ecol, 0.0)
    ecolb = ecol.astype(BF16)

    def only(k, a):
        return jnp.where(head_lane[k], a, jnp.zeros_like(a))

    def silu_slope(a):
        sa = jax.nn.sigmoid(a)
        return sa * (1.0 + a * (1.0 - sa))

    def chain(l, local, out, q, near, far, step):
        ld = m.cum[l, T - 1 : T, :]
        ra, rb, rc = q.Ar, q.Br, q.Cr
        sa, sb, sc = q.As, q.Bs, q.Cs
        A = One(
            lambda: rdma(sa.at[l], ra.at[l], q.AS.at[l], q.AR.at[l], (2 * z + near, h)),
            c == far,
            c == near,
        )

        def link(d):
            zz = z + step * d
            inside = jnp.logical_and(zz >= 0, zz < 4)
            prev = z - step * d
            gets = jnp.logical_and(prev >= 0, prev < 4)
            return One(
                lambda: rdma(
                    sb.at[l], rb.at[l, z], q.BS.at[l, d], q.BR.at[l, d], (2 * zz + near, h)
                ),
                jnp.logical_and(c == near, inside),
                jnp.logical_and(c == near, gets),
            )

        B = [link(d) for d in (2, 1, 3)]
        first = z == 0 if step > 0 else z == 3
        more = jnp.logical_not(first)
        Cc = One(
            lambda: rdma(sc.at[l], rc.at[l], q.CS.at[l], q.CR.at[l], (2 * z + far, h)),
            jnp.logical_and(c == near, more),
            jnp.logical_and(c == far, more),
        )

        def begin():
            @pl.when(c == far)
            def _():
                sa[l, 0:C, :] = local[l, 0:C, :]
                sa[l, C:, :] = jnp.broadcast_to(ld, (G, N))

            A.start()

        def middle():
            A.wait()

            @pl.when(c == near)
            def _():
                other = ra[l, 0:C, :]
                lo = ra[l, C : C + 1, :]
                sb[l, 0:C, :] = decay_rows(ld) * other + local[l, 0:C, :]
                sb[l, C:, :] = jnp.broadcast_to(lo + ld, (G, N))

            for b in B:
                b.start()

        def end():
            for b in B:
                b.wait()

            @pl.when(c == near)
            def _():
                m.acc[...] = jnp.zeros((C, N), F32)
                order = (0, 1, 2) if step > 0 else (3, 2, 1)
                for zz in order:

                    @pl.when(zz < z if step > 0 else zz > z)
                    def _():
                        m.acc[...] = decay_rows(rb[l, zz, C : C + 1, :]) * m.acc[...] + rb[
                            l, zz, 0:C, :
                        ]

                sc[l] = m.acc[...]

            Cc.start()
            out[l, C:, :] = jnp.zeros((256 - C, N), F32)

            @pl.when(c == near)
            def _():
                lo = ra[l, C : C + 1, :]
                out[l, 0:C, :] = decay_rows(lo) * m.acc[...] + ra[l, 0:C, :]

            Cc.wait()

            @pl.when(c == far)
            def _():
                @pl.when(more)
                def _():
                    out[l, 0:C, :] = rc[l]

                @pl.when(first)
                def _():
                    out[l, 0:C, :] = jnp.zeros((C, N), F32)

        return begin, middle, end

    def forward(l, ready):
        n = nx[l][...]
        m.pj[l, G:, 0:256] = padded(dot(n, m.wz[l, 1], 1, 1))
        m.pj[l, G:, 256:512] = dot(n, m.wb[l], 1, 0)
        ready()
        halo = One(
            lambda: rdma(
                m.pj.at[l, pl.ds(T, G), pl.ds(0, 512)],
                m.pj.at[l, pl.ds(0, G), pl.ds(0, 512)],
                m.jhS.at[l],
                m.jhR.at[l],
                (s + 1, h),
            ),
            s < NS - 1,
            s > 0,
        )
        halo.start()
        if l == 0:
            for cp in loads[4:]:
                cp.start()
        m.pjd[l] = padded(dot(n, m.wd[l], 1, 1), 128)
        m.pj[l, G:, 512:768] = padded(dot(n, m.wz[l, 0], 1, 1))
        dt = jnp.where(dt_lane, jax.nn.softplus(m.pjd[l] + sp[l, 6:7, 0:128]), 0.0)
        la = -dt * jnp.exp(sp[l, 7:8, 0:128])
        cum = sums(tri, la, 1, 0)
        m.dt[l] = dt
        m.cum[l] = cum
        dtb = spread(dt)
        etb = spread(jnp.exp(cum[T - 1 : T, :] - cum))
        m.dtb[l] = dtb
        m.etb[l] = etb
        m.ecb[l] = spread(jnp.exp(cum))
        cumt = jnp.transpose(cum)
        for k in range(3):
            m.seg[l, k] = jnp.where(causal, jnp.exp(cum[:, k : k + 1] - cumt[k : k + 1, :]), 0.0)

        @pl.when(s == 0)
        def _():
            m.pj[l, 0:G, 0:512] = jnp.zeros((G, 512), F32)

        halo.wait()
        for kc in (256, 0):
            a = sp[l, 4:5, kc : kc + 256]
            for k in range(4):
                at = G - 3 + k
                a = a + sp[l, k : k + 1, kc : kc + 256] * m.pj[l, at : at + T, kc : kc + 256]
            m.pre[l, :, kc : kc + 256] = a
            post = a * jax.nn.sigmoid(a)
            if kc:
                m.bm[l] = post[:, 0:N].astype(BF16)
                m.cm[l] = post[:, N:].astype(BF16)
        x = post
        m.x[l] = x
        m.xdt[l] = dtb * x
        m.xtail[l] = dtb * etb * x
        m.hl[l] = fine(m.xtail[l], m.bm[l], 0, 0)
        begin, middle, end = chain(l, m.hl, m.hin, m.fc, 1, 0, 1)
        begin()
        scores = dot(m.cm[l], m.bm[l], 1, 1)
        for k in range(3):
            m.vw[l, k] = scores * m.seg[l, k]
        middle()
        yi = jnp.zeros((T, 256), F32)
        for k in range(3):
            yi = yi + fine(m.vw[l, k], only(k, m.xdt[l]), 1, 0)
        m.yn[l] = yi
        end()
        yn = m.yn[l] + m.ecb[l] * fine(m.cm[l], m.hin[l], 1, 1)
        m.yn[l] = yn
        zz = m.pj[l, G:, 512:768]
        m.v[l] = (yn + spread(sp[l, 8:9, 0:128]) * m.x[l]) * (zz * jax.nn.sigmoid(zz))

    def gate_norm(l, r):
        exact = r * m.v[l] * sp[l, 5:6, 0:256]
        m.gnb[l] = exact.astype(BF16)
        return exact - m.gnb[l].astype(F32)

    def gather_rows(buf, cut, width, q):
        def place(dx, dy):
            return (hx + dx) % 4 * 4 + (hy + dy) % 4

        def left(d):
            dx, dy = d // 4, d % 4
            source = rows16(jnp.where(dy == 0, h, place(4 - dx, 0)))
            to = jnp.where(dy == 0, place(dx, 0), place(0, dy))
            part = buf.at[source, pl.ds(0, cut)]
            return rdma(part, part, q.LS.at[d], q.LR.at[d], (s, to))

        def right(d):
            dx, dy = d // 4, d % 4
            source = rows16(jnp.where(dx == 0, h, place(0, 4 - dy)))
            to = jnp.where(dx == 0, place(0, dy), place(dx, 0))
            part = buf.at[source, pl.ds(cut, width - cut)]
            return rdma(part, part, q.RS.at[d], q.RR.at[d], (s, to))

        def all_sent():
            every(1, NH, lambda d: left(d).wait_send())
            every(1, NH, lambda d: right(d).wait_send())

        finals.append(all_sent)
        order = (2, 1, 3)
        for k in order:
            left(4 * k).start()
            right(k).start()
        for k in order:
            left(k).start()
            right(4 * k).start()

        def end():
            for k in (1, 3, 2):
                left(4 * k).wait_recv()
                for j in order:
                    left(4 * k + j).start()
                right(k).wait_recv()
                for j in order:
                    right(4 * j + k).start()

            def rest(d):
                @pl.when(d % 4 > 0)
                def _():
                    left(d).wait_recv()

                @pl.when(d // 4 > 0)
                def _():
                    right(d).wait_recv()

            every(1, NH, rest)

        return end

    def rows_sum(src, dst, q, lead=()):
        ring = head_ring(lambda t: src.at[rows16(t)], lambda me: dst.at[me], q, lead)
        ring.start()
        dst[h] = src[rows16(h), :]

        def end():
            ring.wait()
            return total_of(dst, NH)

        return end

    def mix_out(l):
        for j in range(3):
            at = slice(512 * j, 512 * j + 512)
            m.op1[:, at] = dot(m.gnb[l, :, 0:C], m.wo[l, :, at], 1, 0).astype(BF16)
        return rows_sum(m.op1, m.opr1, m.opq, (l,))

    def total_of(ref, count):
        total = ref[0].astype(F32)
        for t in range(1, count):
            total = total + ref[t].astype(F32)
        return total

    def scalars(i, *values, beside=lambda: None):
        ones = jnp.full((R, 256), 1.0, BF16)
        row = iota((8, 128), 0)
        packed = jnp.zeros((8, 128), F32)
        for k, value in enumerate(values):
            over = sums(ones, value, 1, 1)[0:8]
            packed = jnp.where(row == 2 * k, over[:, 0:128], packed)
            packed = jnp.where(row == 2 * k + 1, over[:, 128:256], packed)
        m.scs[i] = packed
        ring = head_ring(lambda t: m.scs.at[i], lambda me: m.scr.at[i, me], m.scq, (i,))
        ring.start()
        m.scr[i, h] = m.scs[i]
        beside()
        ring.wait()
        total = total_of(m.scr.at[i], NH)
        cols = jnp.transpose(jnp.concatenate([total, jnp.zeros((120, 128), F32)], axis=0))
        return [
            jnp.concatenate([cols[:, 2 * k : 2 * k + 1], cols[:, 2 * k + 1 : 2 * k + 2]], axis=0)
            for k in range(len(values))
        ]

    def g_gate(l):
        m.ggn[l] = padded(dot(gm[l][:, 0:D], m.wo[l], 1, 1))

    def weight_parts(q, l, parts):
        w = q.r.shape[-1]
        for k in range(4):
            at = 0
            for left, right in parts:
                piece = dot(left[:, 384 * k : 384 * k + 384], right, 0, 0)
                wide = piece.shape[1]
                q.s[l, 0, k, :, at : at + wide] = piece[0:C].astype(BF16)
                q.s[l, 1, k, :, at : at + wide] = piece[C:].astype(BF16)
                at += wide
        yes = jnp.bool_(True)
        pair = One(
            lambda: rdma(
                q.s.at[l, 1 - c], q.r.at[l], q.S.at[l], q.R.at[l], (2 * z + 1 - c, h)
            ),
            yes,
            yes,
        )

        def mk(d):
            t = lax.rem(z + d, 4)
            return rdma(
                q.c.at[l, t], q.x.at[l, z], q.U.at[l, d], q.V.at[l, d], (2 * t + c, h)
            )

        ring = Ring(mk, 4, lambda f: every(1, 4, f))

        def middle():
            pair.wait()
            for k in range(4):
                q.c[l, k] = (q.s[l, c, k].astype(F32) + q.r[l, k].astype(F32)).astype(BF16)
            ring.start()
            q.x[l, z] = q.c[l, z]

        def end(col):
            ring.wait()
            wout[l, :, col : col + w] = total_of(q.x.at[l], 4)

        return pair.start, middle, end

    def backward(l, r, s2, early, late, last_of_all):
        gain = sp[l, 5:6, 0:256]
        skip = spread(sp[l, 8:9, 0:128])
        v = m.v[l]
        ggn = m.ggn[l]
        rv = r * v
        gv = r * (gain * ggn) - v * (r * r * s2 / INNER)
        zz = m.pj[l, G:, 512:768]
        sz = jax.nn.sigmoid(zz)
        x = m.x[l]
        y = m.yn[l] + skip * x
        gy = gv * (zz * sz)
        gyc = m.ecb[l] * gy
        m.gl[l] = fine(gyc, m.cm[l], 0, 0)
        begin, middle, end = chain(l, m.gl, m.gn, m.bc, 0, 1, -1)
        begin()
        m.sm[l, 5:6, 0:256] = jnp.sum(ggn * rv, axis=0, keepdims=True)
        if l:
            gate_norm(l, r)
        m.ge[l, :, 512:768] = (gv * y * (sz * (1.0 + zz * (1.0 - sz)))).astype(BF16)
        gxd = jnp.zeros((T, 256), F32)
        ds = jnp.zeros((T, T), F32)
        xdt = m.xdt[l]
        for k in range(3):
            g_k = only(k, gy)
            gxd = gxd + fine(m.vw[l, k], g_k, 0, 0)
            ds = ds + fine(g_k, xdt, 1, 1) * m.seg[l, k]
        middle()
        weight_go, weight_mid, weight_end = weight_parts(
            m.we, l, [(nx[l], m.ge[l, :, 512:768]), (gm[l], m.gnb[l])]
        )
        bm, cm = m.bm[l], m.cm[l]
        db = fine(ds, cm, 0, 0)
        dc = fine(ds, bm, 1, 0) + fine(gyc, m.hin[l], 1, 0)
        gskip = jnp.sum(gy * x, axis=0, keepdims=True)
        early()
        end()
        weight_go()
        gnx = m.gn[l]
        db = db + fine(m.xtail[l], gnx, 1, 0)
        rt = m.etb[l] * fine(bm, gnx, 1, 1)
        gxs = gxd + rt
        gx = m.dtb[l] * gxs + skip * gy
        for kc, gpost in ((0, gx), (256, jnp.concatenate([db, dc], axis=1))):
            gpre = gpost * silu_slope(m.pre[l, :, kc : kc + 256])
            m.gp[l, 0:T, kc : kc + 256] = gpre
        halo = One(
            lambda: rdma(
                m.gp.at[l, pl.ds(0, G)], m.gp.at[l, pl.ds(T, G)], m.ghS.at[l], m.ghR.at[l], (s - 1, h)
            ),
            s > 0,
            s < NS - 1,
        )
        halo.start()
        dt = m.dt[l]
        gdt = fine(x * gxs, ecolb, 1, 0)
        cum = m.cum[l]
        inner = jnp.sum(gnx * m.hin[l], axis=1, keepdims=True)
        inner = jnp.sum(inner * ecol, axis=0, keepdims=True)
        tail = jnp.sum(xdt * rt, axis=0, keepdims=True)
        both = fine(jnp.concatenate([tail, gskip, jnp.zeros((6, 256), F32)], axis=0), ecolb, 1, 0)
        last = both[0:1] + jnp.exp(cum[T - 1 : T, :]) * inner
        pairs = gy * m.yn[l] - xdt * gxs
        hi, lo = halves(pairs)
        rest = (pairs - hi.astype(F32) - lo.astype(F32)).astype(BF16)
        dcum = fine(pairs, ecolb, 1, 0) + dot(rest, ecolb, 1, 0)
        dcum = dcum + jnp.where(iota((T, 128), 0) == T - 1, last, 0.0)
        gla = sums(tri, dcum, 0, 0)
        rate = jnp.exp(sp[l, 7:8, 0:128])
        gd = gdt - gla * rate
        gdtr = jnp.where(dt_lane, gd * jax.nn.sigmoid(m.pjd[l] + sp[l, 6:7, 0:128]), 0.0)
        weight_mid()
        m.sm[l, 5:6, 256:512] = jnp.zeros((1, 256), F32)
        m.sm[l, 6:7, 0:128] = jnp.sum(gdtr, axis=0, keepdims=True)
        m.sm[l, 6:7, 128:256] = jnp.sum(-gla * dt * rate, axis=0, keepdims=True)
        m.sm[l, 6:7, 256:384] = both[1:2]
        m.sm[l, 6:7, 384:512] = jnp.zeros((1, 128), F32)
        m.sm[l, 7:8, :] = jnp.zeros((1, 512), F32)
        @pl.when(s == NS - 1)
        def _():
            m.gp[l, T:, :] = jnp.zeros((G, 512), F32)

        halo.wait()
        for kc in (0, 256):
            gj = jnp.zeros((T, 256), F32)
            for k in range(4):
                gj = gj + sp[l, k : k + 1, kc : kc + 256] * m.gp[l, 3 - k : 3 - k + T, kc : kc + 256]
            if kc == 0:
                gj = jnp.concatenate([gj[:, 0:C], gdtr[:, 0:64]], axis=1)
            else:
                gt = jnp.transpose(gj)
                for t in range(NH):
                    m.gbs[l, t] = gt[R * t : R * t + R, :]
            m.ge[l, :, kc : kc + 256] = gj.astype(BF16)
        late()
        low = gdtr[:, 0:R].astype(BF16)
        for j in range(3):
            at = slice(512 * j, 512 * j + 512)
            part = (
                dot(m.ge[l, :, 0:C], m.wz[l, 1, :, at], 1, 0)
                + dot(m.ge[l, :, 512 : 512 + C], m.wz[l, 0, :, at], 1, 0)
                + dot(m.ge[l, :, 256:512], m.wb[l, at, :], 1, 1)
                + dot(low, m.wd[l, :, at], 1, 0)
            )
            if l == 0:
                m.ngp[l, 0:1, at] = jnp.sum(part * (m.hid[:, at] * m.q0[:, 0:1]), axis=0, keepdims=True)
            m.gq[l, :, at] = part.astype(BF16)
        ring = head_ring(
            lambda t: m.gq.at[l, rows16(t)], lambda me: m.gqr.at[l, me], m.gqq, (l,)
        )
        ring.start()
        m.gqr[l, h] = m.gq[l, rows16(h), :]
        for kc in (0, 256):
            gpre = m.gp[l, 0:T, kc : kc + 256]
            for k in range(4):
                at = G - 3 + k
                m.sm[l, k : k + 1, kc : kc + 256] = jnp.sum(
                    gpre * m.pj[l, at : at + T, kc : kc + 256], axis=0, keepdims=True
                )
            m.sm[l, 4:5, kc : kc + 256] = jnp.sum(gpre, axis=0, keepdims=True)
        last_of_all()
        last_go, last_mid, last_end = weight_parts(m.wl, l, [(nx[l], m.ge[l, :, 0:256])])
        last_go()

        def finish():
            ring.wait()
            return total_of(m.gqr.at[l], NH)

        return finish, weight_end, last_mid, last_end

    def norm_back(l, u, g, gn):
        q = lax.rsqrt(jnp.mean(u * u, axis=1, keepdims=True) + EPS)
        w = gn * ng_ref[l : l + 1, :]
        if l:
            m.ngp[l, 0:1, :] = jnp.sum(gn * u * q, axis=0, keepdims=True)
        return g + q * w - u * (q * q * q * (jnp.sum(w * u, axis=1, keepdims=True) / D))

    class Small:
        def __init__(self, l):
            self.l = l
            self.a = head_ring(
                lambda t: m.gbs.at[l, t], lambda me: m.gbr.at[l, me], m.gbq, (l,)
            )
            self.e = head_ring(
                lambda t: m.gss.at[l, t], lambda me: m.gsr.at[l, me], m.gsq, (l,)
            )
            self.b = seq_ring(lambda t: m.gcs.at[l, t], lambda me: m.gcr.at[l, me], m.gcq, (l,))
            self.c = seq_ring(lambda t: m.sm.at[l], lambda me: m.smr.at[l, me], m.smq, (l,))
            self.d = head_ring(lambda t: m.gds.at[l], lambda me: bct.at[l, me], m.gdq, (l,))

        def first(self):
            l = self.l
            self.a.start()
            m.gbr[l, h] = m.gbs[l, h]

        def first_small(self):
            l = self.l
            for t in range(NH):
                m.gss[l, t, 0:5, :] = m.sm[l, 0:5, 256:512]
                m.gss[l, t, 5:6, 0:S] = m.ngp[l, 0:1, S * t : S * t + S]
                m.gss[l, t, 5:6, S:] = jnp.zeros((1, 256 - S), F32)
                m.gss[l, t, 6:, :] = jnp.zeros((2, 256), F32)
            self.e.start()
            m.gsr[l, h] = m.gss[l, h]

        def second(self):
            l = self.l
            self.a.wait()
            total = total_of(m.gbr.at[l], NH)
            part = dot(total.astype(BF16), nx[l][...], 1, 0).astype(BF16)
            for t in range(NS):
                m.gcs[l, t] = padded(part[:, C * t : C * t + C])
            self.b.start()
            m.gcr[l, s] = m.gcs[l, s]

        def second_small(self):
            l = self.l
            self.e.wait()
            total = total_of(m.gsr.at[l], NH)
            m.sm[l, 0:5, 256:512] = total[0:5]
            m.sm[l, 7:8, 0:256] = total[5:6]
            self.c.start()
            m.smr[l, s] = m.sm[l]

        def third(self):
            l = self.l
            self.b.wait()
            m.gds[l] = total_of(m.gcr.at[l], NS).astype(BF16)
            self.d.start()
            bct[l, h] = m.gds[l]

        def third_small(self):
            self.c.wait()
            smo[self.l] = total_of(m.smr.at[self.l], NS)

    small = [Small(0), Small(1)]
    outs = [
        pltpu.make_async_copy(a, b, m.loc.at[13 + i])
        for i, (a, b) in enumerate(
            zip((ho, gi, wout, bct, smo), (ho_out, gi_out, w_out, bct_out, smo_out))
        )
    ]

    loads[1].wait()
    loads[2].wait()
    forward(0, lambda: pl.semaphore_wait(bar, NH - 1 + NS - 1))
    loads[3].wait()
    ends = []

    def high_parts():
        vg = (m.v[0] * sp[0, 5:6, 0:256])[:, 0:C]
        for j in range(3):
            at = slice(512 * j, 512 * j + 512)
            m.op0[:, at] = fine(vg, m.wo[0, :, at], 1, 0)
            m.oph[:, at] = m.op0[:, at].astype(BF16)
        ends.append(rows_sum(m.oph, m.opr0, m.opq, (0,)))

    sq = scalars(0, m.v[0] * m.v[0], beside=high_parts)[0]
    r0 = lax.rsqrt(sq / INNER + EPS)
    m.r0[...] = jnp.broadcast_to(r0, (T, 128))
    rest = gate_norm(0, r0)[:, 0:C].astype(BF16)
    for j in range(3):
        at = slice(512 * j, 512 * j + 512)
        left = dot(rest, m.wo[0, :, at], 1, 0)
        m.lo[:, at] = left.astype(BF16)
        m.opl[:, at] = (r0 * (m.op0[:, at] - m.oph[:, at].astype(F32)) - left).astype(BF16)
    ends.append(rows_sum(m.opl, m.oplr, m.oplq))
    o0 = m.r0[rows16(h), 0:1] * ends[0]() + ends[1]()
    m.orow[...] = o0
    u1 = m.hid[rows16(h), :] + o0
    m.urow[...] = u1
    m.nx1[rows16(h), :] = norm_rows(u1, 1)[1]
    ag_end = gather_rows(m.nx1, D // 2, D, m.agq)

    for cp in loads[4:]:
        cp.wait()
    m.gm1[...] = m.og[...].astype(BF16)
    g_gate(1)
    ag_end()

    low = head_ring(lambda t: m.lo.at[rows16(t)], lambda me: m.lor.at[me], m.loq)
    low.start()
    m.lor[h] = m.lo[rows16(h), :]
    forward(1, lambda: None)
    v = m.v[1]
    sq, s2 = scalars(1, v * v, m.ggn[1] * (sp[1, 5:6, 0:256] * v))
    r1 = lax.rsqrt(sq / INNER + EPS)
    rings = []

    def hidden_rows():
        final = m.urow[...] + rings[0]()
        for t in range(NH):
            m.hos[t] = padded(final[:, S * t : S * t + S], 128)

    back1, e1_end, l1_mid, l1_end = backward(
        1, r1, r1 * s2, lambda: rings.append(mix_out(1)), lambda: None, lambda: None
    )
    l1_mid()
    hidden_rows()
    low.wait()
    m.orow[...] = m.orow[...] + total_of(m.lor, NH)
    g_rows = norm_back(1, m.urow[...], m.og[rows16(h), :], back1())
    m.grow[...] = g_rows
    rounded = g_rows.astype(BF16)
    m.gm0[rows16(h), 0:D] = rounded
    m.gm0[rows16(h), D:] = scalar_lanes(
        jnp.sum(rounded.astype(F32) * m.orow[...], axis=1, keepdims=True)
    )
    agm_end = gather_rows(m.gm0, D // 2, X, m.gmq)
    e1_end(256)
    l1_end(0)
    agm_end()

    g_gate(0)
    s2 = m.gm0[:, D:].astype(F32)
    hor = head_ring(lambda t: m.hos.at[t], lambda me: ho.at[rows16(me)], m.hoq)

    def early0():
        hor.start()
        ho[rows16(h), :] = m.hos[h]
        small[1].first()
        small[1].first_small()

    back0, e0_end, l0_mid, l0_end = backward(0, m.r0[:, 0:1], s2[:, 0:1] + s2[:, 1:2], early0, small[0].first, small[0].first_small)
    small[1].second()
    small[1].second_small()
    small[0].second()
    l0_mid()
    small[0].second_small()
    small[1].third()
    small[0].third()
    hor.wait()
    outs[0].start()
    g_rows = norm_back(0, m.hid[rows16(h), :], m.grow[...], back0())
    for t in range(NH):
        m.fas[t] = padded(g_rows[:, S * t : S * t + S], 128)
    far = head_ring(lambda t: m.fas.at[t], lambda me: gi.at[rows16(me)], m.faq)
    far.start()
    gi[rows16(h), :] = m.fas[h]
    e0_end(256)
    l0_end(0)
    outs[2].start()
    small[1].third_small()
    small[0].third_small()
    outs[4].start()
    small[1].d.wait()
    small[0].d.wait()
    outs[3].start()
    far.wait()
    outs[1].start()
    for cp in outs:
        cp.wait()
    for f in finals:
        f()


def arrange(*refs):
    ins, outs, kept, forms, sems = refs[0:5], refs[5:16], refs[16:21], refs[21:32], refs[32]
    ho, gi, w, bct, smo = kept
    o_ho, o_gi, o_ng, o_zx, o_bc, o_dt, o_cx, o_cb, o_hp, o_gg, o_wo = forms
    copies = [pltpu.make_async_copy(a, b, sems.at[i]) for i, (a, b) in enumerate(zip(ins, kept))]
    back = [pltpu.make_async_copy(a, b, sems.at[5 + i]) for i, (a, b) in enumerate(zip(forms, outs))]
    for i in (2, 3, 0, 1, 4):
        copies[i].start()
    copies[2].wait()
    for l in range(2):
        o_zx[l, :, 0, :] = w[l, :, 256 : 256 + C]
        o_zx[l, :, 1, :] = w[l, :, 0:C]
    back[3].start()
    for l in range(2):
        o_wo[l] = jnp.transpose(w[l, :, 512:768])[0:C, :]
    back[10].start()
    copies[3].wait()
    for l in range(2):
        rows = jnp.concatenate([bct[l, t].astype(F32) for t in range(NH)], axis=0)
        o_bc[l] = jnp.transpose(rows)[0:C, :]
    back[4].start()
    copies[0].wait()
    o_ho[...] = jnp.transpose(ho[...])[0:S, :]
    back[0].start()
    copies[1].wait()
    o_gi[...] = jnp.transpose(gi[...])[0:S, :]
    back[1].start()
    copies[4].wait()
    for l in range(2):
        o_ng[l : l + 1, :] = smo[l, 7:8, 0:S]
        dts = jnp.transpose(w[l, :, 128:256])
        for k in range(3):
            o_dt[k, l : l + 1, :] = dts[64 + k : 65 + k, :]
            o_hp[k, l : l + 1, :] = smo[l, 6:7, 128 * k : 128 * k + 3]
        for k in range(5):
            o_cx[k, l : l + 1, :] = smo[l, k : k + 1, 0:C]
            o_cb[k, l : l + 1, :] = smo[l, k : k + 1, 256:512]
        o_gg[l : l + 1, :] = smo[l, 5:6, 0:C]
    for i in (2, 5, 6, 7, 8, 9):
        back[i].start()
    for cp in back:
        cp.wait()


def on_device(
    hidden_in,
    norm_gain,
    gate_mixer_weight,
    w_bc,
    w_dt,
    conv_x,
    conv_bc,
    head_params,
    gate_gain,
    w_out,
    out_grad,
):
    whole = pl.BlockSpec(memory_space=pltpu.VMEM)
    there = pl.BlockSpec(memory_space=pl.ANY)

    def out(*shape, dtype=F32):
        return jax.ShapeDtypeStruct(shape, dtype)

    raw = pl.pallas_call(
        kernel,
        out_shape=[
            out(T, 128),
            out(T, 128),
            out(2, C, 768),
            out(2, NH, R, 256, dtype=BF16),
            out(2, 8, 512),
        ],
        in_specs=[there] * 7 + [whole] + [there] * 3,
        out_specs=[there] * 5,
        scratch_shapes=LEAVES,
        compiler_params=pltpu.CompilerParams(
            collective_id=0, has_side_effects=True, vmem_limit_bytes=60 * 2**20
        ),
        name="two_layers",
    )(
        hidden_in,
        out_grad,
        norm_gain,
        jnp.transpose(conv_x, (1, 0, 2)),
        jnp.transpose(conv_bc, (1, 0, 2)),
        jnp.transpose(head_params, (1, 0, 2)),
        gate_gain,
        jnp.transpose(w_dt, (2, 0, 1)),
        jnp.transpose(gate_mixer_weight, (0, 2, 3, 1)),
        w_bc,
        w_out,
    )
    shapes = [
        (S, T),
        (S, T),
        (2, S),
        (2, C, 2, C),
        (2, C, 256),
        (3, 2, C),
        (5, 2, C),
        (5, 2, 256),
        (3, 2, 3),
        (2, C),
        (2, C, C),
    ]
    ho, gi, ng, zx, bc, dt, cx, cb, hp, gg, wo = pl.pallas_call(
        arrange,
        out_shape=[out(*shape) for shape in shapes],
        in_specs=[there] * 5,
        out_specs=[there] * 11,
        scratch_shapes=[
            vm(T, 128),
            vm(T, 128),
            vm(2, C, 768),
            half(2, NH, R, 256),
            vm(2, 8, 512),
            *[vm(*shape) for shape in shapes],
            sem(16),
        ],
        compiler_params=pltpu.CompilerParams(vmem_limit_bytes=60 * 2**20),
        name="arrange",
    )(*raw)
    return (
        jnp.transpose(ho),
        jnp.transpose(gi),
        ng,
        zx,
        bc,
        jnp.transpose(dt, (1, 2, 0)),
        jnp.transpose(cx, (1, 0, 2)),
        jnp.transpose(cb, (1, 0, 2)),
        jnp.transpose(hp, (1, 0, 2)),
        gg,
        wo,
    )


def solution(mesh):
    return jax.shard_map(
        on_device,
        mesh=mesh,
        in_specs=(
            P("seq", None),
            P(),
            P(None, None, None, "head"),
            P(),
            P(None, None, "head"),
            P(None, None, "head"),
            P(),
            P(None, None, "head"),
            P(None, "head"),
            P(None, "head", None),
            P("seq", None),
        ),
        out_specs=(
            P("seq", "head"),
            P("seq", "head"),
            P(None, "head"),
            P(None, "seq", None, "head"),
            P(None, "seq", None),
            P(None, "seq", "head"),
            P(None, None, "head"),
            P(),
            P(None, None, "head"),
            P(None, "head"),
            P(None, "head", "seq"),
        ),
        check_vma=False,
    )
```

```python
from types import SimpleNamespace

import jax
import jax.numpy as jnp
from jax import lax
from jax.experimental import pallas as pl
from jax.experimental.pallas import tpu as pltpu
from jax.sharding import PartitionSpec as P

EPS = 1e-05
MESH = pl.DeviceIdType.MESH
F32 = jnp.float32
BF16 = jnp.bfloat16

T = 256
R = 16
G = 8
D = 1536
INNER = 3072
C = 192
N = 128
NH = 16
NS = 8
X = D + 128
S = D // NH


def dot(a, b, ca, cb):
    return lax.dot_general(a, b, (((ca,), (cb,)), ((), ())), preferred_element_type=F32)


def halves(a):
    if a.dtype == BF16:
        return (a,)
    hi = a.astype(BF16)
    return hi, (a - hi.astype(F32)).astype(BF16)


def fine(a, b, ca, cb):
    total = None
    for i, p in enumerate(halves(a)):
        for j, q in enumerate(halves(b)):
            if i + j < 2:
                term = dot(p, q, ca, cb)
                total = term if total is None else total + term
    return total


def sums(ones, value, ca, cb):
    hi, lo = halves(value)
    rest = (value - hi.astype(F32) - lo.astype(F32)).astype(BF16)
    return dot(ones, hi, ca, cb) + dot(ones, lo, ca, cb) + dot(ones, rest, ca, cb)


def iota(shape, dim):
    return lax.broadcasted_iota(jnp.int32, shape, dim)


def padded(a, lanes=256):
    return jnp.concatenate([a, jnp.zeros((a.shape[0], lanes - a.shape[1]), a.dtype)], axis=1)


def spread(col):
    rows = col.shape[0]
    lane = iota((rows, 128), 1)
    parts = [jnp.broadcast_to(col[:, k : k + 1], (rows, 128)) for k in range(3)]
    return jnp.concatenate(
        [jnp.where(lane < 64, parts[0], parts[1]), jnp.where(lane < 64, parts[2], 0.0)], axis=1
    )


def scalar_lanes(col):
    hi = col.astype(BF16).astype(F32)
    lane = iota((col.shape[0], 128), 1)
    return jnp.where(lane == 0, hi, jnp.where(lane == 1, col - hi, 0.0)).astype(BF16)


def decay_rows(log_row):
    e = jnp.exp(log_row)
    return jnp.concatenate(
        [jnp.broadcast_to(e[:, k : k + 1], (64, 128)) for k in range(3)], axis=0
    )


def vm(*shape, dtype=F32):
    return pltpu.VMEM(shape, dtype)


def half(*shape):
    return pltpu.VMEM(shape, BF16)


def sem(*shape):
    return pltpu.SemaphoreType.DMA(shape)


def both(*shape):
    return dict(S=sem(*shape), R=sem(*shape))


def chain_refs():
    return dict(
        As=vm(2, C + G, N),
        Ar=vm(2, C + G, N),
        AS=sem(2),
        AR=sem(2),
        Bs=vm(2, C + G, N),
        Br=vm(2, 4, C + G, N),
        BS=sem(2, 4),
        BR=sem(2, 4),
        Cs=vm(2, C, N),
        Cr=vm(2, C, N),
        CS=sem(2),
        CR=sem(2),
    )


def weight_refs(w):
    return dict(
        s=half(2, 2, 4, C, w),
        r=half(2, 4, C, w),
        c=half(2, 4, C, w),
        x=half(2, 4, C, w),
        S=sem(2),
        R=sem(2),
        U=sem(2, 4),
        V=sem(2, 4),
    )


SCRATCH = dict(
    hid=vm(T, D),
    og=vm(T, D),
    wz=half(2, 2, C, D),
    wb=half(2, D, 256),
    wo=half(2, C, D),
    sp=vm(2, 16, 512),
    wd=half(2, R, D),
    q0=vm(T, 128),
    nx0=half(T, D),
    nx1=half(T, D),
    pj=vm(2, G + T, 768),
    pre=vm(2, T, 512),
    pjd=vm(2, T, 128),
    dz=vm(2, T, 256),
    jhS=sem(2),
    jhR=sem(2),
    x=vm(2, T, 256),
    dtb=vm(2, T, 256),
    ecb=vm(2, T, 256),
    etb=vm(2, T, 256),
    yn=vm(2, T, 256),
    v=vm(2, T, 256),
    xdt=vm(2, T, 256),
    xtail=vm(2, T, 256),
    bm=half(2, T, N),
    cm=half(2, T, N),
    seg=vm(2, 3, T, T),
    vw=vm(2, 3, T, T),
    dt=vm(2, T, 128),
    cum=vm(2, T, 128),
    hl=vm(2, 256, N),
    hin=vm(2, 256, N),
    gl=vm(2, 256, N),
    gn=vm(2, 256, N),
    acc=vm(C, N),
    fc=chain_refs(),
    bc=chain_refs(),
    op0=vm(T, D),
    oph=half(T, D),
    opr0=half(NH, R, D),
    opl=half(T, D),
    oplr=half(NH, R, D),
    oplq=both(NH),
    op1=half(T, D),
    opr1=half(NH, R, D),
    opq=both(2, NH),
    lo=half(T, D),
    lor=half(NH, R, D),
    loq=both(NH),
    r0=vm(T, 128),
    urow=vm(R, D),
    orow=vm(R, D),
    agq=dict(LS=sem(NH), LR=sem(NH), RS=sem(NH), RR=sem(NH)),
    scs=vm(2, 8, 128),
    scr=vm(2, NH, 8, 128),
    scq=both(2, NH),
    hos=vm(NH, R, 128),
    hoq=both(NH),
    gm0=half(T, X),
    gm1=half(T, D),
    gmq=dict(LS=sem(NH), LR=sem(NH), RS=sem(NH), RR=sem(NH)),
    ggn=vm(2, T, 256),
    gnb=half(2, T, 256),
    gp=vm(2, T + G, 512),
    ghS=sem(2),
    ghR=sem(2),
    ge=half(2, T, 768),
    gq=half(2, T, D),
    gqr=half(2, NH, R, D),
    gqq=both(2, NH),
    grow=vm(R, D),
    ngp=vm(2, 8, D),
    fas=vm(NH, R, 128),
    faq=both(NH),
    sm=vm(2, 8, 512),
    gbs=vm(2, NH, R, 256),
    gbr=vm(2, NH, R, 256),
    gbq=both(2, NH),
    gss=vm(2, NH, G, 256),
    gsr=vm(2, NH, G, 256),
    gsq=both(2, NH),
    smr=vm(2, NS, 8, 512),
    smq=both(2, NS),
    gcs=half(2, NS, R, 256),
    gcr=half(2, NS, R, 256),
    gcq=both(2, NS),
    gds=half(2, R, 256),
    gdq=both(2, NH),
    we=weight_refs(512),
    wl=weight_refs(256),
    ngv=vm(2, D),
    cxv=vm(5, 2, C),
    cbv=vm(5, 2, 256),
    hpv=vm(3, 2, 3),
    ggv=vm(2, C),
    hov=vm(T, 128),
    giv=vm(T, 128),
    wv=vm(2, C, 768),
    bctv=half(2, NH, R, 256),
    smov=vm(2, 8, 512),
    loc=sem(18),
)
LEAVES, TREE = jax.tree.flatten(SCRATCH)


def kernel(
    hid_in,
    og_in,
    ng_in,
    cx_in,
    cb_in,
    hp_in,
    gg_in,
    wd_ref,
    wz_in,
    wb_in,
    wo_in,
    ho_out,
    gi_out,
    w_out,
    bct_out,
    smo_out,
    *scratch,
):
    m = SimpleNamespace(
        **{
            k: SimpleNamespace(**v) if isinstance(v, dict) else v
            for k, v in jax.tree.unflatten(TREE, scratch).items()
        }
    )
    s = lax.axis_index("seq")
    h = lax.axis_index("head")
    z = s // 2
    c = s % 2
    hx = h // 4
    hy = h % 4
    finals = []

    def rdma(src, dst, ss, rs, dev):
        return pltpu.make_async_remote_copy(
            src_ref=src, dst_ref=dst, send_sem=ss, recv_sem=rs, device_id=dev, device_id_type=MESH
        )

    def every(lo, hi, f):
        def step(d, carry):
            f(d)
            return carry

        lax.fori_loop(lo, hi, step, 0)

    class Ring:
        def __init__(self, mk, size, send):
            self.mk, self.size, self.send = mk, size, send

        def start(self):
            self.send(lambda d: self.mk(d).start())
            finals.append(lambda: every(1, self.size, lambda d: self.mk(d).wait_send()))

        def wait(self):
            every(1, self.size, lambda d: self.mk(d).wait_recv())

    def far_first(f):
        for d in (10, 6, 9, 14, 11, 5, 15, 7, 13, 8, 2, 4, 1, 12, 3):
            f(d)

    def head_ring(src, dst, q, lead=()):
        def mk(d):
            t = (hx + d // 4) % 4 * 4 + (hy + d % 4) % 4
            return rdma(src(t), dst(h), q.S.at[(*lead, d)], q.R.at[(*lead, d)], (s, t))

        return Ring(mk, NH, far_first)

    def seq_ring(src, dst, q, lead=()):
        def mk(d):
            t = lax.rem(s + d, NS)
            return rdma(src(t), dst(s), q.S.at[(*lead, d)], q.R.at[(*lead, d)], (t, h))

        return Ring(mk, NS, lambda f: every(1, NS, f))

    class One:
        def __init__(self, mk, sends, receives):
            self.mk, self.sends, self.receives = mk, sends, receives

        def start(self):
            @pl.when(self.sends)
            def _():
                self.mk().start()

            def last():
                @pl.when(self.sends)
                def _():
                    self.mk().wait_send()

            finals.append(last)

        def wait(self):
            @pl.when(self.receives)
            def _():
                self.mk().wait_recv()

    def rows16(t):
        return pl.ds(pl.multiple_of(t * R, R), R)

    ng_ref, cx_ref, cb_ref, hp_ref, gg_ref = m.ngv, m.cxv, m.cbv, m.hpv, m.ggv
    ho, gi, wout, bct, smo = m.hov, m.giv, m.wv, m.bctv, m.smov

    few = [
        pltpu.make_async_copy(a, b, m.loc.at[8 + i])
        for i, (a, b) in enumerate(
            zip((cx_in, cb_in, hp_in, gg_in, ng_in), (cx_ref, cb_ref, hp_ref, gg_ref, ng_ref))
        )
    ]
    for cp in few:
        cp.start()
    loads = [
        pltpu.make_async_copy(hid_in, m.hid, m.loc.at[0]),
        pltpu.make_async_copy(wz_in.at[0], m.wz.at[0], m.loc.at[1]),
        pltpu.make_async_copy(wb_in.at[0], m.wb.at[0], m.loc.at[2]),
        pltpu.make_async_copy(wo_in.at[0], m.wo.at[0], m.loc.at[3]),
        pltpu.make_async_copy(wz_in.at[1], m.wz.at[1], m.loc.at[4]),
        pltpu.make_async_copy(wb_in.at[1], m.wb.at[1], m.loc.at[5]),
        pltpu.make_async_copy(wo_in.at[1], m.wo.at[1], m.loc.at[6]),
        pltpu.make_async_copy(og_in, m.og, m.loc.at[7]),
    ]
    for cp in loads[:4]:
        cp.start()

    bar = pltpu.get_barrier_semaphore()

    def greet(dev):
        pl.semaphore_signal(bar, inc=1, device_id=dev, device_id_type=MESH)

    every(1, NS, lambda d: greet((lax.rem(s + d, NS), h)))
    every(1, NH, lambda d: greet((s, lax.rem(h + d, NH))))

    m.sp[...] = jnp.zeros((2, 16, 512), F32)
    for cp in few:
        cp.wait()
    for l in range(2):
        for k in range(5):
            m.sp[l, k : k + 1, 0:C] = cx_ref[k, l : l + 1, :]
            m.sp[l, k : k + 1, 256:512] = cb_ref[k, l : l + 1, :]
        m.sp[l, 5:6, 0:C] = gg_ref[l : l + 1, :]
        for k in range(3):
            m.sp[l, 6 + k : 7 + k, 0:3] = hp_ref[k, l : l + 1, :]
        rows = [wd_ref[k, l : l + 1, :].astype(F32) for k in range(3)]
        m.wd[l] = jnp.concatenate(rows + [jnp.zeros((R - 3, D), F32)], axis=0).astype(BF16)
    sp = m.sp

    def norm_rows(u, l):
        q = lax.rsqrt(jnp.mean(u * u, axis=1, keepdims=True) + EPS)
        return q, (u * q * ng_ref[l : l + 1, :]).astype(BF16)

    loads[0].wait()

    def norm_step(i):
        at = pl.ds(pl.multiple_of(i * 32, 32), 32)
        q, n = norm_rows(m.hid[at, :], 0)
        m.nx0[at, :] = n
        m.q0[at, :] = jnp.broadcast_to(q, (32, 128))

    every(0, T // 32, norm_step)

    nx = (m.nx0, m.nx1)
    gm = (m.gm0, m.gm1)
    lane = iota((T, 128), 1)
    dt_lane = lane < 3
    lane256 = iota((T, 256), 1)
    head_lane = [jnp.logical_and(lane256 >= 64 * k, lane256 < 64 * k + 64) for k in range(3)]
    causal = iota((T, T), 0) >= iota((T, T), 1)
    tri = jnp.where(causal, 1.0, 0.0).astype(BF16)
    ecol = jnp.where(iota((256, 128), 0) // 64 == iota((256, 128), 1), 1.0, 0.0)
    ecol = jnp.where(iota((256, 128), 1) < 3, ecol, 0.0)
    ecolb = ecol.astype(BF16)

    def only(k, a):
        return jnp.where(head_lane[k], a, jnp.zeros_like(a))

    def silu_slope(a):
        sa = jax.nn.sigmoid(a)
        return sa * (1.0 + a * (1.0 - sa))

    def chain(l, local, out, q, near, far, step):
        ld = m.cum[l, T - 1 : T, :]
        ra, rb, rc = q.Ar, q.Br, q.Cr
        sa, sb, sc = q.As, q.Bs, q.Cs
        A = One(
            lambda: rdma(sa.at[l], ra.at[l], q.AS.at[l], q.AR.at[l], (2 * z + near, h)),
            c == far,
            c == near,
        )

        def link(d):
            zz = z + step * d
            inside = jnp.logical_and(zz >= 0, zz < 4)
            prev = z - step * d
            gets = jnp.logical_and(prev >= 0, prev < 4)
            return One(
                lambda: rdma(
                    sb.at[l], rb.at[l, z], q.BS.at[l, d], q.BR.at[l, d], (2 * zz + near, h)
                ),
                jnp.logical_and(c == near, inside),
                jnp.logical_and(c == near, gets),
            )

        B = [link(d) for d in (2, 1, 3)]
        first = z == 0 if step > 0 else z == 3
        more = jnp.logical_not(first)
        Cc = One(
            lambda: rdma(sc.at[l], rc.at[l], q.CS.at[l], q.CR.at[l], (2 * z + far, h)),
            jnp.logical_and(c == near, more),
            jnp.logical_and(c == far, more),
        )

        def begin():
            @pl.when(c == far)
            def _():
                sa[l, 0:C, :] = local[l, 0:C, :]
                sa[l, C:, :] = jnp.broadcast_to(ld, (G, N))

            A.start()

        def middle():
            A.wait()

            @pl.when(c == near)
            def _():
                other = ra[l, 0:C, :]
                lo = ra[l, C : C + 1, :]
                sb[l, 0:C, :] = decay_rows(ld) * other + local[l, 0:C, :]
                sb[l, C:, :] = jnp.broadcast_to(lo + ld, (G, N))

            for b in B:
                b.start()

        def end():
            for b in B:
                b.wait()

            @pl.when(c == near)
            def _():
                m.acc[...] = jnp.zeros((C, N), F32)
                order = (0, 1, 2) if step > 0 else (3, 2, 1)
                for zz in order:

                    @pl.when(zz < z if step > 0 else zz > z)
                    def _():
                        m.acc[...] = decay_rows(rb[l, zz, C : C + 1, :]) * m.acc[...] + rb[
                            l, zz, 0:C, :
                        ]

                sc[l] = m.acc[...]

            Cc.start()
            out[l, C:, :] = jnp.zeros((256 - C, N), F32)

            @pl.when(c == near)
            def _():
                lo = ra[l, C : C + 1, :]
                out[l, 0:C, :] = decay_rows(lo) * m.acc[...] + ra[l, 0:C, :]

            Cc.wait()

            @pl.when(c == far)
            def _():
                @pl.when(more)
                def _():
                    out[l, 0:C, :] = rc[l]

                @pl.when(first)
                def _():
                    out[l, 0:C, :] = jnp.zeros((C, N), F32)

        return begin, middle, end

    def forward(l, ready):
        n = nx[l][...]
        m.pj[l, G:, 0:256] = padded(dot(n, m.wz[l, 1], 1, 1))
        m.pj[l, G:, 256:512] = dot(n, m.wb[l], 1, 0)
        ready()
        halo = One(
            lambda: rdma(
                m.pj.at[l, pl.ds(T, G), pl.ds(0, 512)],
                m.pj.at[l, pl.ds(0, G), pl.ds(0, 512)],
                m.jhS.at[l],
                m.jhR.at[l],
                (s + 1, h),
            ),
            s < NS - 1,
            s > 0,
        )
        halo.start()
        if l == 0:
            for cp in loads[4:]:
                cp.start()
        m.pjd[l] = padded(dot(n, m.wd[l], 1, 1), 128)
        m.pj[l, G:, 512:768] = padded(dot(n, m.wz[l, 0], 1, 1))
        dt = jnp.where(dt_lane, jax.nn.softplus(m.pjd[l] + sp[l, 6:7, 0:128]), 0.0)
        la = -dt * jnp.exp(sp[l, 7:8, 0:128])
        cum = sums(tri, la, 1, 0)
        m.dt[l] = dt
        m.cum[l] = cum
        dtb = spread(dt)
        etb = spread(jnp.exp(cum[T - 1 : T, :] - cum))
        m.dtb[l] = dtb
        m.etb[l] = etb
        m.ecb[l] = spread(jnp.exp(cum))
        cumt = jnp.transpose(cum)
        for k in range(3):
            m.seg[l, k] = jnp.where(causal, jnp.exp(cum[:, k : k + 1] - cumt[k : k + 1, :]), 0.0)

        @pl.when(s == 0)
        def _():
            m.pj[l, 0:G, 0:512] = jnp.zeros((G, 512), F32)

        halo.wait()
        for kc in (256, 0):
            a = sp[l, 4:5, kc : kc + 256]
            for k in range(4):
                at = G - 3 + k
                a = a + sp[l, k : k + 1, kc : kc + 256] * m.pj[l, at : at + T, kc : kc + 256]
            m.pre[l, :, kc : kc + 256] = a
            post = a * jax.nn.sigmoid(a)
            if kc:
                m.bm[l] = post[:, 0:N].astype(BF16)
                m.cm[l] = post[:, N:].astype(BF16)
        x = post
        m.x[l] = x
        m.xdt[l] = dtb * x
        m.xtail[l] = dtb * etb * x
        m.hl[l] = fine(m.xtail[l], m.bm[l], 0, 0)
        begin, middle, end = chain(l, m.hl, m.hin, m.fc, 1, 0, 1)
        begin()
        scores = dot(m.cm[l], m.bm[l], 1, 1)
        for k in range(3):
            m.vw[l, k] = scores * m.seg[l, k]
        middle()
        yi = jnp.zeros((T, 256), F32)
        for k in range(3):
            yi = yi + fine(m.vw[l, k], only(k, m.xdt[l]), 1, 0)
        m.yn[l] = yi
        end()
        yn = m.yn[l] + m.ecb[l] * fine(m.cm[l], m.hin[l], 1, 1)
        m.yn[l] = yn
        zz = m.pj[l, G:, 512:768]
        m.v[l] = (yn + spread(sp[l, 8:9, 0:128]) * m.x[l]) * (zz * jax.nn.sigmoid(zz))

    def gate_norm(l, r):
        exact = r * m.v[l] * sp[l, 5:6, 0:256]
        m.gnb[l] = exact.astype(BF16)
        return exact - m.gnb[l].astype(F32)

    def gather_rows(buf, cut, width, q):
        def place(dx, dy):
            return (hx + dx) % 4 * 4 + (hy + dy) % 4

        def left(d):
            dx, dy = d // 4, d % 4
            source = rows16(jnp.where(dy == 0, h, place(4 - dx, 0)))
            to = jnp.where(dy == 0, place(dx, 0), place(0, dy))
            part = buf.at[source, pl.ds(0, cut)]
            return rdma(part, part, q.LS.at[d], q.LR.at[d], (s, to))

        def right(d):
            dx, dy = d // 4, d % 4
            source = rows16(jnp.where(dx == 0, h, place(0, 4 - dy)))
            to = jnp.where(dx == 0, place(0, dy), place(dx, 0))
            part = buf.at[source, pl.ds(cut, width - cut)]
            return rdma(part, part, q.RS.at[d], q.RR.at[d], (s, to))

        def all_sent():
            every(1, NH, lambda d: left(d).wait_send())
            every(1, NH, lambda d: right(d).wait_send())

        finals.append(all_sent)
        order = (2, 1, 3)
        for k in order:
            left(4 * k).start()
            right(k).start()
        for k in order:
            left(k).start()
            right(4 * k).start()

        def end():
            for k in (1, 3, 2):
                left(4 * k).wait_recv()
                for j in order:
                    left(4 * k + j).start()
                right(k).wait_recv()
                for j in order:
                    right(4 * j + k).start()

            def rest(d):
                @pl.when(d % 4 > 0)
                def _():
                    left(d).wait_recv()

                @pl.when(d // 4 > 0)
                def _():
                    right(d).wait_recv()

            every(1, NH, rest)

        return end

    def rows_sum(src, dst, q, lead=()):
        ring = head_ring(lambda t: src.at[rows16(t)], lambda me: dst.at[me], q, lead)
        ring.start()
        dst[h] = src[rows16(h), :]

        def end():
            ring.wait()
            return total_of(dst, NH)

        return end

    def mix_out(l):
        for j in range(3):
            at = slice(512 * j, 512 * j + 512)
            m.op1[:, at] = dot(m.gnb[l, :, 0:C], m.wo[l, :, at], 1, 0).astype(BF16)
        return rows_sum(m.op1, m.opr1, m.opq, (l,))

    def total_of(ref, count):
        total = ref[0].astype(F32)
        for t in range(1, count):
            total = total + ref[t].astype(F32)
        return total

    def scalars(i, *values, beside=lambda: None):
        ones = jnp.full((R, 256), 1.0, BF16)
        row = iota((8, 128), 0)
        packed = jnp.zeros((8, 128), F32)
        for k, value in enumerate(values):
            over = sums(ones, value, 1, 1)[0:8]
            packed = jnp.where(row == 2 * k, over[:, 0:128], packed)
            packed = jnp.where(row == 2 * k + 1, over[:, 128:256], packed)
        m.scs[i] = packed
        ring = head_ring(lambda t: m.scs.at[i], lambda me: m.scr.at[i, me], m.scq, (i,))
        ring.start()
        m.scr[i, h] = m.scs[i]
        beside()
        ring.wait()
        total = total_of(m.scr.at[i], NH)
        cols = jnp.transpose(jnp.concatenate([total, jnp.zeros((120, 128), F32)], axis=0))
        return [
            jnp.concatenate([cols[:, 2 * k : 2 * k + 1], cols[:, 2 * k + 1 : 2 * k + 2]], axis=0)
            for k in range(len(values))
        ]

    def g_gate(l):
        m.ggn[l] = padded(dot(gm[l][:, 0:D], m.wo[l], 1, 1))

    def weight_parts(q, l, parts):
        w = q.r.shape[-1]
        for k in range(4):
            at = 0
            for left, right in parts:
                piece = dot(left[:, 384 * k : 384 * k + 384], right, 0, 0)
                wide = piece.shape[1]
                q.s[l, 0, k, :, at : at + wide] = piece[0:C].astype(BF16)
                q.s[l, 1, k, :, at : at + wide] = piece[C:].astype(BF16)
                at += wide
        yes = jnp.bool_(True)
        pair = One(
            lambda: rdma(
                q.s.at[l, 1 - c], q.r.at[l], q.S.at[l], q.R.at[l], (2 * z + 1 - c, h)
            ),
            yes,
            yes,
        )

        def mk(d):
            t = lax.rem(z + d, 4)
            return rdma(
                q.c.at[l, t], q.x.at[l, z], q.U.at[l, d], q.V.at[l, d], (2 * t + c, h)
            )

        ring = Ring(mk, 4, lambda f: every(1, 4, f))

        def middle():
            pair.wait()
            for k in range(4):
                q.c[l, k] = (q.s[l, c, k].astype(F32) + q.r[l, k].astype(F32)).astype(BF16)
            ring.start()
            q.x[l, z] = q.c[l, z]

        def end(col):
            ring.wait()
            wout[l, :, col : col + w] = total_of(q.x.at[l], 4)

        return pair.start, middle, end

    def slopes(l):
        zz = m.pj[l, G:, 512:768]
        sz = jax.nn.sigmoid(zz)
        m.pj[l, G:, 512:768] = zz * sz
        m.dz[l] = sz * (1.0 + zz * (1.0 - sz))
        for kc in (0, 256):
            m.pre[l, :, kc : kc + 256] = silu_slope(m.pre[l, :, kc : kc + 256])

    def backward(l, r, s2, early, late, last_of_all):
        gain = sp[l, 5:6, 0:256]
        skip = spread(sp[l, 8:9, 0:128])
        v = m.v[l]
        ggn = m.ggn[l]
        rv = r * v
        gv = r * (gain * ggn) - v * (r * r * s2 / INNER)
        x = m.x[l]
        y = m.yn[l] + skip * x
        gy = gv * m.pj[l, G:, 512:768]
        gyc = m.ecb[l] * gy
        m.gl[l] = fine(gyc, m.cm[l], 0, 0)
        begin, middle, end = chain(l, m.gl, m.gn, m.bc, 0, 1, -1)
        begin()
        m.sm[l, 5:6, 0:256] = jnp.sum(ggn * rv, axis=0, keepdims=True)
        if l:
            gate_norm(l, r)
        m.ge[l, :, 512:768] = (gv * y * m.dz[l]).astype(BF16)
        gxd = jnp.zeros((T, 256), F32)
        ds = jnp.zeros((T, T), F32)
        xdt = m.xdt[l]
        for k in range(3):
            g_k = only(k, gy)
            gxd = gxd + fine(m.vw[l, k], g_k, 0, 0)
            ds = ds + fine(g_k, xdt, 1, 1) * m.seg[l, k]
        middle()
        weight_go, weight_mid, weight_end = weight_parts(
            m.we, l, [(nx[l], m.ge[l, :, 512:768]), (gm[l], m.gnb[l])]
        )
        bm, cm = m.bm[l], m.cm[l]
        db = fine(ds, cm, 0, 0)
        dc = fine(ds, bm, 1, 0) + fine(gyc, m.hin[l], 1, 0)
        gskip = jnp.sum(gy * x, axis=0, keepdims=True)
        early()
        end()
        weight_go()
        gnx = m.gn[l]
        db = db + fine(m.xtail[l], gnx, 1, 0)
        rt = m.etb[l] * fine(bm, gnx, 1, 1)
        gxs = gxd + rt
        gx = m.dtb[l] * gxs + skip * gy
        for kc, gpost in ((0, gx), (256, jnp.concatenate([db, dc], axis=1))):
            gpre = gpost * m.pre[l, :, kc : kc + 256]
            m.gp[l, 0:T, kc : kc + 256] = gpre
        halo = One(
            lambda: rdma(
                m.gp.at[l, pl.ds(0, G)], m.gp.at[l, pl.ds(T, G)], m.ghS.at[l], m.ghR.at[l], (s - 1, h)
            ),
            s > 0,
            s < NS - 1,
        )
        halo.start()
        dt = m.dt[l]
        gdt = fine(x * gxs, ecolb, 1, 0)
        cum = m.cum[l]
        inner = jnp.sum(gnx * m.hin[l], axis=1, keepdims=True)
        inner = jnp.sum(inner * ecol, axis=0, keepdims=True)
        tail = jnp.sum(xdt * rt, axis=0, keepdims=True)
        both = fine(jnp.concatenate([tail, gskip, jnp.zeros((6, 256), F32)], axis=0), ecolb, 1, 0)
        last = both[0:1] + jnp.exp(cum[T - 1 : T, :]) * inner
        pairs = gy * m.yn[l] - xdt * gxs
        hi, lo = halves(pairs)
        rest = (pairs - hi.astype(F32) - lo.astype(F32)).astype(BF16)
        dcum = fine(pairs, ecolb, 1, 0) + dot(rest, ecolb, 1, 0)
        dcum = dcum + jnp.where(iota((T, 128), 0) == T - 1, last, 0.0)
        gla = sums(tri, dcum, 0, 0)
        rate = jnp.exp(sp[l, 7:8, 0:128])
        gd = gdt - gla * rate
        gdtr = jnp.where(dt_lane, gd * jax.nn.sigmoid(m.pjd[l] + sp[l, 6:7, 0:128]), 0.0)
        weight_mid()
        m.sm[l, 5:6, 256:512] = jnp.zeros((1, 256), F32)
        m.sm[l, 6:7, 0:128] = jnp.sum(gdtr, axis=0, keepdims=True)
        m.sm[l, 6:7, 128:256] = jnp.sum(-gla * dt * rate, axis=0, keepdims=True)
        m.sm[l, 6:7, 256:384] = both[1:2]
        m.sm[l, 6:7, 384:512] = jnp.zeros((1, 128), F32)
        m.sm[l, 7:8, :] = jnp.zeros((1, 512), F32)
        @pl.when(s == NS - 1)
        def _():
            m.gp[l, T:, :] = jnp.zeros((G, 512), F32)

        halo.wait()
        for kc in (0, 256):
            gj = jnp.zeros((T, 256), F32)
            for k in range(4):
                gj = gj + sp[l, k : k + 1, kc : kc + 256] * m.gp[l, 3 - k : 3 - k + T, kc : kc + 256]
            if kc == 0:
                gj = jnp.concatenate([gj[:, 0:C], gdtr[:, 0:64]], axis=1)
            else:
                gt = jnp.transpose(gj)
                for t in range(NH):
                    m.gbs[l, t] = gt[R * t : R * t + R, :]
            m.ge[l, :, kc : kc + 256] = gj.astype(BF16)
        late()
        low = gdtr[:, 0:R].astype(BF16)
        for j in range(3):
            at = slice(512 * j, 512 * j + 512)
            part = (
                dot(m.ge[l, :, 0:C], m.wz[l, 1, :, at], 1, 0)
                + dot(m.ge[l, :, 512 : 512 + C], m.wz[l, 0, :, at], 1, 0)
                + dot(m.ge[l, :, 256:512], m.wb[l, at, :], 1, 1)
                + dot(low, m.wd[l, :, at], 1, 0)
            )
            if l == 0:
                m.ngp[l, 0:1, at] = jnp.sum(part * (m.hid[:, at] * m.q0[:, 0:1]), axis=0, keepdims=True)
            m.gq[l, :, at] = part.astype(BF16)
        ring = head_ring(
            lambda t: m.gq.at[l, rows16(t)], lambda me: m.gqr.at[l, me], m.gqq, (l,)
        )
        ring.start()
        m.gqr[l, h] = m.gq[l, rows16(h), :]
        for kc in (0, 256):
            gpre = m.gp[l, 0:T, kc : kc + 256]
            for k in range(4):
                at = G - 3 + k
                m.sm[l, k : k + 1, kc : kc + 256] = jnp.sum(
                    gpre * m.pj[l, at : at + T, kc : kc + 256], axis=0, keepdims=True
                )
            m.sm[l, 4:5, kc : kc + 256] = jnp.sum(gpre, axis=0, keepdims=True)
        last_of_all()
        last_go, last_mid, last_end = weight_parts(m.wl, l, [(nx[l], m.ge[l, :, 0:256])])
        last_go()

        def finish():
            ring.wait()
            return total_of(m.gqr.at[l], NH)

        return finish, weight_end, last_mid, last_end

    def norm_back(l, u, g, gn):
        q = lax.rsqrt(jnp.mean(u * u, axis=1, keepdims=True) + EPS)
        w = gn * ng_ref[l : l + 1, :]
        if l:
            m.ngp[l, 0:1, :] = jnp.sum(gn * u * q, axis=0, keepdims=True)
        return g + q * w - u * (q * q * q * (jnp.sum(w * u, axis=1, keepdims=True) / D))

    class Small:
        def __init__(self, l):
            self.l = l
            self.a = head_ring(
                lambda t: m.gbs.at[l, t], lambda me: m.gbr.at[l, me], m.gbq, (l,)
            )
            self.e = head_ring(
                lambda t: m.gss.at[l, t], lambda me: m.gsr.at[l, me], m.gsq, (l,)
            )
            self.b = seq_ring(lambda t: m.gcs.at[l, t], lambda me: m.gcr.at[l, me], m.gcq, (l,))
            self.c = seq_ring(lambda t: m.sm.at[l], lambda me: m.smr.at[l, me], m.smq, (l,))
            self.d = head_ring(lambda t: m.gds.at[l], lambda me: bct.at[l, me], m.gdq, (l,))

        def first(self):
            l = self.l
            self.a.start()
            m.gbr[l, h] = m.gbs[l, h]

        def first_small(self):
            l = self.l
            for t in range(NH):
                m.gss[l, t, 0:5, :] = m.sm[l, 0:5, 256:512]
                m.gss[l, t, 5:6, 0:S] = m.ngp[l, 0:1, S * t : S * t + S]
                m.gss[l, t, 5:6, S:] = jnp.zeros((1, 256 - S), F32)
                m.gss[l, t, 6:, :] = jnp.zeros((2, 256), F32)
            self.e.start()
            m.gsr[l, h] = m.gss[l, h]

        def second(self):
            l = self.l
            self.a.wait()
            total = total_of(m.gbr.at[l], NH)
            part = dot(total.astype(BF16), nx[l][...], 1, 0).astype(BF16)
            for t in range(NS):
                m.gcs[l, t] = padded(part[:, C * t : C * t + C])
            self.b.start()
            m.gcr[l, s] = m.gcs[l, s]

        def second_small(self):
            l = self.l
            self.e.wait()
            total = total_of(m.gsr.at[l], NH)
            m.sm[l, 0:5, 256:512] = total[0:5]
            m.sm[l, 7:8, 0:256] = total[5:6]
            self.c.start()
            m.smr[l, s] = m.sm[l]

        def third(self):
            l = self.l
            self.b.wait()
            m.gds[l] = total_of(m.gcr.at[l], NS).astype(BF16)
            self.d.start()
            bct[l, h] = m.gds[l]

        def third_small(self):
            self.c.wait()
            smo[self.l] = total_of(m.smr.at[self.l], NS)

    small = [Small(0), Small(1)]
    outs = [
        pltpu.make_async_copy(a, b, m.loc.at[13 + i])
        for i, (a, b) in enumerate(
            zip((ho, gi, wout, bct, smo), (ho_out, gi_out, w_out, bct_out, smo_out))
        )
    ]

    loads[1].wait()
    loads[2].wait()
    forward(0, lambda: pl.semaphore_wait(bar, NH - 1 + NS - 1))
    loads[3].wait()
    ends = []

    def high_parts():
        vg = (m.v[0] * sp[0, 5:6, 0:256])[:, 0:C]
        for j in range(3):
            at = slice(512 * j, 512 * j + 512)
            m.op0[:, at] = fine(vg, m.wo[0, :, at], 1, 0)
            m.oph[:, at] = m.op0[:, at].astype(BF16)
        ends.append(rows_sum(m.oph, m.opr0, m.opq, (0,)))

    sq = scalars(0, m.v[0] * m.v[0], beside=high_parts)[0]
    r0 = lax.rsqrt(sq / INNER + EPS)
    m.r0[...] = jnp.broadcast_to(r0, (T, 128))
    rest = gate_norm(0, r0)[:, 0:C].astype(BF16)
    for j in range(3):
        at = slice(512 * j, 512 * j + 512)
        left = dot(rest, m.wo[0, :, at], 1, 0)
        m.lo[:, at] = left.astype(BF16)
        m.opl[:, at] = (r0 * (m.op0[:, at] - m.oph[:, at].astype(F32)) - left).astype(BF16)
    ends.append(rows_sum(m.opl, m.oplr, m.oplq))
    o0 = m.r0[rows16(h), 0:1] * ends[0]() + ends[1]()
    m.orow[...] = o0
    u1 = m.hid[rows16(h), :] + o0
    m.urow[...] = u1
    m.nx1[rows16(h), :] = norm_rows(u1, 1)[1]
    ag_end = gather_rows(m.nx1, D // 2, D, m.agq)

    for cp in loads[4:]:
        cp.wait()
    m.gm1[...] = m.og[...].astype(BF16)
    g_gate(1)
    slopes(0)
    ag_end()

    low = head_ring(lambda t: m.lo.at[rows16(t)], lambda me: m.lor.at[me], m.loq)
    low.start()
    m.lor[h] = m.lo[rows16(h), :]
    forward(1, lambda: None)
    v = m.v[1]
    sq, s2 = scalars(1, v * v, m.ggn[1] * (sp[1, 5:6, 0:256] * v), beside=lambda: slopes(1))
    r1 = lax.rsqrt(sq / INNER + EPS)
    rings = []

    def hidden_rows():
        final = m.urow[...] + rings[0]()
        for t in range(NH):
            m.hos[t] = padded(final[:, S * t : S * t + S], 128)

    back1, e1_end, l1_mid, l1_end = backward(
        1, r1, r1 * s2, lambda: rings.append(mix_out(1)), lambda: None, lambda: None
    )
    l1_mid()
    hidden_rows()
    low.wait()
    m.orow[...] = m.orow[...] + total_of(m.lor, NH)
    g_rows = norm_back(1, m.urow[...], m.og[rows16(h), :], back1())
    m.grow[...] = g_rows
    rounded = g_rows.astype(BF16)
    m.gm0[rows16(h), 0:D] = rounded
    m.gm0[rows16(h), D:] = scalar_lanes(
        jnp.sum(rounded.astype(F32) * m.orow[...], axis=1, keepdims=True)
    )
    agm_end = gather_rows(m.gm0, D // 2, X, m.gmq)
    e1_end(256)
    l1_end(0)
    agm_end()

    g_gate(0)
    s2 = m.gm0[:, D:].astype(F32)
    hor = head_ring(lambda t: m.hos.at[t], lambda me: ho.at[rows16(me)], m.hoq)

    def early0():
        hor.start()
        ho[rows16(h), :] = m.hos[h]
        small[1].first()
        small[1].first_small()

    back0, e0_end, l0_mid, l0_end = backward(0, m.r0[:, 0:1], s2[:, 0:1] + s2[:, 1:2], early0, small[0].first, small[0].first_small)
    small[1].second()
    small[1].second_small()
    small[0].second()
    l0_mid()
    small[0].second_small()
    small[1].third()
    small[0].third()
    hor.wait()
    outs[0].start()
    g_rows = norm_back(0, m.hid[rows16(h), :], m.grow[...], back0())
    for t in range(NH):
        m.fas[t] = padded(g_rows[:, S * t : S * t + S], 128)
    far = head_ring(lambda t: m.fas.at[t], lambda me: gi.at[rows16(me)], m.faq)
    far.start()
    gi[rows16(h), :] = m.fas[h]
    e0_end(256)
    l0_end(0)
    outs[2].start()
    small[1].third_small()
    small[0].third_small()
    outs[4].start()
    small[1].d.wait()
    small[0].d.wait()
    outs[3].start()
    far.wait()
    outs[1].start()
    for cp in outs:
        cp.wait()
    for f in finals:
        f()


def arrange(*refs):
    ins, outs, kept, forms, sems = refs[0:5], refs[5:16], refs[16:21], refs[21:32], refs[32]
    ho, gi, w, bct, smo = kept
    o_ho, o_gi, o_ng, o_zx, o_bc, o_dt, o_cx, o_cb, o_hp, o_gg, o_wo = forms
    copies = [pltpu.make_async_copy(a, b, sems.at[i]) for i, (a, b) in enumerate(zip(ins, kept))]
    back = [pltpu.make_async_copy(a, b, sems.at[5 + i]) for i, (a, b) in enumerate(zip(forms, outs))]
    for i in (2, 3, 0, 1, 4):
        copies[i].start()
    copies[2].wait()
    for l in range(2):
        o_zx[l, :, 0, :] = w[l, :, 256 : 256 + C]
        o_zx[l, :, 1, :] = w[l, :, 0:C]
    back[3].start()
    for l in range(2):
        o_wo[l] = jnp.transpose(w[l, :, 512:768])[0:C, :]
    back[10].start()
    copies[3].wait()
    for l in range(2):
        rows = jnp.concatenate([bct[l, t].astype(F32) for t in range(NH)], axis=0)
        o_bc[l] = jnp.transpose(rows)[0:C, :]
    back[4].start()
    copies[0].wait()
    o_ho[...] = jnp.transpose(ho[...])[0:S, :]
    back[0].start()
    copies[1].wait()
    o_gi[...] = jnp.transpose(gi[...])[0:S, :]
    back[1].start()
    copies[4].wait()
    for l in range(2):
        o_ng[l : l + 1, :] = smo[l, 7:8, 0:S]
        dts = jnp.transpose(w[l, :, 128:256])
        for k in range(3):
            o_dt[k, l : l + 1, :] = dts[64 + k : 65 + k, :]
            o_hp[k, l : l + 1, :] = smo[l, 6:7, 128 * k : 128 * k + 3]
        for k in range(5):
            o_cx[k, l : l + 1, :] = smo[l, k : k + 1, 0:C]
            o_cb[k, l : l + 1, :] = smo[l, k : k + 1, 256:512]
        o_gg[l : l + 1, :] = smo[l, 5:6, 0:C]
    for i in (2, 5, 6, 7, 8, 9):
        back[i].start()
    for cp in back:
        cp.wait()


def on_device(
    hidden_in,
    norm_gain,
    gate_mixer_weight,
    w_bc,
    w_dt,
    conv_x,
    conv_bc,
    head_params,
    gate_gain,
    w_out,
    out_grad,
):
    whole = pl.BlockSpec(memory_space=pltpu.VMEM)
    there = pl.BlockSpec(memory_space=pl.ANY)

    def out(*shape, dtype=F32):
        return jax.ShapeDtypeStruct(shape, dtype)

    raw = pl.pallas_call(
        kernel,
        out_shape=[
            out(T, 128),
            out(T, 128),
            out(2, C, 768),
            out(2, NH, R, 256, dtype=BF16),
            out(2, 8, 512),
        ],
        in_specs=[there] * 7 + [whole] + [there] * 3,
        out_specs=[there] * 5,
        scratch_shapes=LEAVES,
        compiler_params=pltpu.CompilerParams(
            collective_id=0, has_side_effects=True, vmem_limit_bytes=60 * 2**20
        ),
        name="two_layers",
    )(
        hidden_in,
        out_grad,
        norm_gain,
        jnp.transpose(conv_x, (1, 0, 2)),
        jnp.transpose(conv_bc, (1, 0, 2)),
        jnp.transpose(head_params, (1, 0, 2)),
        gate_gain,
        jnp.transpose(w_dt, (2, 0, 1)),
        jnp.transpose(gate_mixer_weight, (0, 2, 3, 1)),
        w_bc,
        w_out,
    )
    shapes = [
        (S, T),
        (S, T),
        (2, S),
        (2, C, 2, C),
        (2, C, 256),
        (3, 2, C),
        (5, 2, C),
        (5, 2, 256),
        (3, 2, 3),
        (2, C),
        (2, C, C),
    ]
    ho, gi, ng, zx, bc, dt, cx, cb, hp, gg, wo = pl.pallas_call(
        arrange,
        out_shape=[out(*shape) for shape in shapes],
        in_specs=[there] * 5,
        out_specs=[there] * 11,
        scratch_shapes=[
            vm(T, 128),
            vm(T, 128),
            vm(2, C, 768),
            half(2, NH, R, 256),
            vm(2, 8, 512),
            *[vm(*shape) for shape in shapes],
            sem(16),
        ],
        compiler_params=pltpu.CompilerParams(vmem_limit_bytes=60 * 2**20),
        name="arrange",
    )(*raw)
    return (
        jnp.transpose(ho),
        jnp.transpose(gi),
        ng,
        zx,
        bc,
        jnp.transpose(dt, (1, 2, 0)),
        jnp.transpose(cx, (1, 0, 2)),
        jnp.transpose(cb, (1, 0, 2)),
        jnp.transpose(hp, (1, 0, 2)),
        gg,
        wo,
    )


def solution(mesh):
    return jax.shard_map(
        on_device,
        mesh=mesh,
        in_specs=(
            P("seq", None),
            P(),
            P(None, None, None, "head"),
            P(),
            P(None, None, "head"),
            P(None, None, "head"),
            P(),
            P(None, None, "head"),
            P(None, "head"),
            P(None, "head", None),
            P("seq", None),
        ),
        out_specs=(
            P("seq", "head"),
            P("seq", "head"),
            P(None, "head"),
            P(None, "seq", None, "head"),
            P(None, "seq", None),
            P(None, "seq", "head"),
            P(None, None, "head"),
            P(),
            P(None, None, "head"),
            P(None, "head"),
            P(None, "head", "seq"),
        ),
        check_vma=False,
    )
```
